32 devices in a mesh: fsdp: 32 (over z, y, x, core).
Axes of the slice: x: 2, y: 2, z: 4, core: 2. Of those that a mesh axis runs over, the one named last changes fastest.
Arguments:
- tokens: bfloat16 [35840, 768], P('fsdp'), may hold values from -6 to 6
- cotangent: bfloat16 [35840, 768], P('fsdp'), may hold values from -6 to 6
- lengths: int32 [224], P('fsdp'), may hold values from 80 to 160, as said below
- span_start: int32 [224, 4], P('fsdp'), may hold values from 0 to 159, as said below
- span_end: int32 [224, 4], P('fsdp'), may hold values from 1 to 160, as said below
- query_weight: bfloat16 [768, 768], P('fsdp'), may hold values from -0.21875 to 0.21875
- query_bias: bfloat16 [768], P('fsdp'), may hold values from -1.75 to 1.75
- key_weight: bfloat16 [768, 768], P('fsdp'), may hold values from -0.21875 to 0.21875
- value_weight: bfloat16 [768, 768], P('fsdp'), may hold values from -0.21875 to 0.21875
- value_bias: bfloat16 [768], P('fsdp'), may hold values from -1.75 to 1.75
- out_weight: bfloat16 [768, 768], P('fsdp'), may hold values from -0.875 to 0.875
- out_bias: bfloat16 [768], P('fsdp'), may hold values from -1.75 to 1.75
- attn_gain: bfloat16 [768], P('fsdp'), may hold values from 0.5 to 1.5
- attn_shift: bfloat16 [768], P('fsdp'), may hold values from -1.75 to 1.75
- up_weight: bfloat16 [768, 3072], P('fsdp'), may hold values from -0.21875 to 0.21875
- up_bias: bfloat16 [3072], P('fsdp'), may hold values from -1.75 to 1.75
- down_weight: bfloat16 [3072, 768], P('fsdp'), may hold values from -0.109375 to 0.109375
- down_bias: bfloat16 [768], P('fsdp'), may hold values from -1.75 to 1.75
- ffn_gain: bfloat16 [768], P('fsdp'), may hold values from 0.5 to 1.5
- ffn_shift: bfloat16 [768], P('fsdp'), may hold values from -1.75 to 1.75
Outputs:
- layer_out: bfloat16 [35840, 768], P('fsdp')
- input_grad: bfloat16 [35840, 768], P('fsdp')
- query_weight_grad: float32 [768, 768], P('fsdp')
- query_bias_grad: float32 [768], P('fsdp')
- key_weight_grad: float32 [768, 768], P('fsdp')
- value_weight_grad: float32 [768, 768], P('fsdp')
- value_bias_grad: float32 [768], P('fsdp')
- out_weight_grad: float32 [768, 768], P('fsdp')
- out_bias_grad: float32 [768], P('fsdp')
- attn_gain_grad: float32 [768], P('fsdp')
- attn_shift_grad: float32 [768], P('fsdp')
- up_weight_grad: float32 [768, 3072], P('fsdp')
- up_bias_grad: float32 [3072], P('fsdp')
- down_weight_grad: float32 [3072, 768], P('fsdp')
- down_bias_grad: float32 [768], P('fsdp')
- ffn_gain_grad: float32 [768], P('fsdp')
- ffn_shift_grad: float32 [768], P('fsdp')
The draws below stay inside these ranges and needn't reach their ends.
Inputs may be any that keep to these rules, and one draw needn't show every extreme that they name: `lengths`: residues of each chain; positions at or past it are padding; some chain has exactly 160 and some exactly 80. `span_start`: each span lies inside its chain's residues; spans of a chain may intersect. `span_end`: greater than the span's start and at most the chain's length.
All inputs are finite; a program needn't handle non-finite values.
Results may differ from the reference program's by a relative error of at most 0.013.
Values may be sent and summed in bfloat16 or wider, within the bound.
No kernel may reach another device: no remote copies, remote signals or barrier semaphores. Data moves between devices by JAX's collectives and lax.ppermute only.
A program may use at most 256 MiB of HBM per device.

```python
import jax
import jax.numpy as jnp
from jax import lax

D = 768
HEADS = 12
HEAD = 64
FF = 3072
LENGTH = 160
SPANS = 4
CHAINS_DEV = 7
CHAINS = 224
TOKENS = 35840
N_FSDP = 32


def chain_lengths(key):
    key = jax.random.fold_in(key, 101)
    first_key, place_key, other_key = jax.random.split(key, 3)
    drawn = jax.random.randint(first_key, (CHAINS,), LENGTH // 2, LENGTH + 1)
    longest = jax.random.randint(place_key, (), 0, CHAINS)
    shortest = (longest + 1 + jax.random.randint(other_key, (), 0, CHAINS - 1)) % CHAINS
    return drawn.at[longest].set(LENGTH).at[shortest].set(LENGTH // 2)


def span_pairs(key):
    chain_len = chain_lengths(key)
    key = jax.random.fold_in(key, 202)
    cap_key, width_key, start_key = jax.random.split(key, 3)
    widest = jax.random.randint(cap_key, (CHAINS, SPANS), 1, LENGTH // 8 + 1)
    widths = jax.random.randint(width_key, (CHAINS, SPANS), 1, widest + 1)
    starts = jax.random.randint(start_key, (CHAINS, SPANS), 0, chain_len[:, None])
    ends = jnp.minimum(starts + widths, chain_len[:, None])
    return (starts.astype(jnp.int32), ends.astype(jnp.int32))


def draw_lengths(key, part):
    return chain_lengths(key).astype(jnp.int32)


def draw_span_start(key, part):
    return span_pairs(key)[0]


def draw_span_end(key, part):
    return span_pairs(key)[1]


def spiked(array, key, source, target, shards_of, factor):
    def block_of(position):
        return (jnp.arange(array.shape[position]) // (array.shape[position] // shards_of)).reshape((-1,) + (1,) * (array.ndim - 1 - position))

    first = jax.random.permutation(key, shards_of)[block_of(target)]
    other_side = (block_of(target) + shards_of // 2) % shards_of
    return jnp.where((block_of(source) == first) | (block_of(source) == other_side), factor * array, array)


def levels(own_key, shape, cuts, smallest, high):
    factor_of = 1.0
    for axis_at, parts in cuts:
        steps = jax.random.uniform(jax.random.fold_in(jax.random.fold_in(own_key, 6), axis_at), (parts,), jnp.float32, smallest / len(cuts), high / len(cuts))
        factor_of = factor_of * jnp.repeat(jnp.exp(steps), shape[axis_at] // parts).reshape((-1,) + (1,) * (len(shape) - 1 - axis_at))
    return factor_of


def noise(own_key, shape, width, reach, pieces=(), held_as=jnp.bfloat16):
    loudness = levels(own_key, shape, pieces, -0.22, 0.18) if pieces else 1.0
    values = jax.random.normal(own_key, shape, jnp.float32) * width * loudness
    return jnp.minimum(jnp.maximum(values, -reach), reach).astype(held_as)


def gaussian_with(own_key, shape, width, reach, cuts, heavy, dtype=jnp.bfloat16):
    values = width * jax.random.normal(own_key, shape, jnp.float32)
    if cuts:
        values = values * levels(own_key, shape, cuts, -0.22, 0.18)
    return jnp.clip(spiked(values, jax.random.fold_in(own_key, 3), *heavy), -reach, reach).astype(dtype)


def setup_inputs(seed: int = 0) -> dict:
    seeds = jax.random.split(jax.random.key(seed), 21)
    tokens = gaussian_with(seeds[0], (TOKENS, D), 1.0, 6.0, ((0, 32),), (0, 1, 32, 2.75))
    cotangent = gaussian_with(seeds[1], (TOKENS, D), 1.0, 6.0, ((0, 32),), (0, 1, 32, 2.75))
    lengths = draw_lengths(jax.random.fold_in(seeds[20], 71), 0)
    span_start = draw_span_start(jax.random.fold_in(seeds[20], 71), 0)
    span_end = draw_span_end(jax.random.fold_in(seeds[20], 71), 0)
    query_weight = noise(seeds[5], (D, D), D ** -0.5, 0.21875, ((0, 32),))
    query_bias = noise(seeds[6], (D,), 0.3, 1.75, ((0, 32),))
    key_weight = noise(seeds[7], (D, D), D ** -0.5, 0.21875, ((0, 32),))
    value_weight = noise(seeds[8], (D, D), D ** -0.5, 0.21875, ((0, 32),))
    value_bias = noise(seeds[9], (D,), 0.3, 1.75, ((0, 32),))
    out_weight = noise(seeds[10], (D, D), (D // 16) ** -0.5, 0.875, ((0, 32),))
    out_bias = noise(seeds[11], (D,), 0.3, 1.75, ((0, 32),))
    attn_gain = jnp.clip(1.0 + 0.1 * jax.random.normal(seeds[12], (D,), jnp.float32), 0.5, 1.5).astype(jnp.bfloat16)
    attn_shift = noise(seeds[13], (D,), 0.3, 1.75, ((0, 32),))
    up_weight = noise(seeds[14], (D, FF), D ** -0.5, 0.21875, ((0, 32),))
    up_bias = noise(seeds[15], (FF,), 0.3, 1.75, ((0, 32),))
    down_weight = noise(seeds[16], (FF, D), FF ** -0.5, 0.109375, ((0, 32),))
    down_bias = noise(seeds[17], (D,), 0.3, 1.75, ((0, 32),))
    ffn_gain = jnp.clip(1.0 + 0.1 * jax.random.normal(seeds[18], (D,), jnp.float32), 0.5, 1.5).astype(jnp.bfloat16)
    ffn_shift = noise(seeds[19], (D,), 0.3, 1.75, ((0, 32),))
    return {"tokens": tokens, "cotangent": cotangent, "lengths": lengths, "span_start": span_start, "span_end": span_end, "query_weight": query_weight, "query_bias": query_bias, "key_weight": key_weight, "value_weight": value_weight, "value_bias": value_bias, "out_weight": out_weight, "out_bias": out_bias, "attn_gain": attn_gain, "attn_shift": attn_shift, "up_weight": up_weight, "up_bias": up_bias, "down_weight": down_weight, "down_bias": down_bias, "ffn_gain": ffn_gain, "ffn_shift": ffn_shift}


@jax.custom_vjp
def low(v):
    return lax.optimization_barrier(v.astype(jnp.bfloat16)).astype(jnp.float32)

@jax.custom_vjp
def low_back(v):
    return v

def low_keep(v):
    return (low(v), None)

def low_pass(kept, grad):
    return (grad,)

def back_keep(v):
    return (v, None)

def back_low(kept, grad):
    return (low(grad),)
low.defvjp(low_keep, low_pass)
low_back.defvjp(back_keep, back_low)
epsilon = 1e-05
masked_score = -1000000000.0

def matmul(left, right):
    return jnp.dot(left, right, precision=lax.Precision.HIGHEST)

def rounded_both(values):
    return low_back(low(values))

def layer_norm(values, gain, shift):
    center = values - lax.optimization_barrier(jnp.mean(values, axis=-1, keepdims=True))
    spread = lax.optimization_barrier(jnp.mean(center * center, axis=-1, keepdims=True))
    return center * lax.rsqrt(spread + epsilon) * gain + shift

def forward(inputs, params, chain_len):
    query_weight, query_bias, key_weight, value_weight, value_bias, out_weight, out_bias, attn_gain, attn_shift, up_weight, up_bias, down_weight, down_bias, ffn_gain, ffn_shift = params
    group = chain_len.shape[0]
    shape = (group, LENGTH, HEADS, HEAD)
    query = rounded_both(matmul(inputs, query_weight) + query_bias).reshape(shape)
    keyrows = rounded_both(matmul(inputs, key_weight)).reshape(shape)
    valrows = rounded_both(matmul(inputs, value_weight) + value_bias).reshape(shape)
    scores = jnp.einsum('cqhe,ckhe->chqk', query, keyrows, precision=lax.Precision.HIGHEST) * 0.125
    valid = (jnp.arange(LENGTH)[None, :] < chain_len[:, None])[:, None, None, :]
    scores = low_back(jnp.where(valid, scores, masked_score))
    probs = low(jax.nn.softmax(scores, axis=-1))
    mixed = jnp.einsum('chqk,ckhe->cqhe', probs, valrows, precision=lax.Precision.HIGHEST)
    mixed = rounded_both(mixed.reshape(group * LENGTH, D))
    attn = low_back(matmul(mixed, out_weight) + out_bias)
    first = layer_norm(inputs + attn, attn_gain, attn_shift)
    pre = low_back(matmul(low(first), up_weight) + up_bias)
    hidden = low(jax.nn.gelu(pre, approximate=False))
    ffn = low_back(matmul(hidden, down_weight) + down_bias)
    return layer_norm(first + ffn, ffn_gain, ffn_shift)

def reference(tokens, cotangent, lengths, span_start, span_end, query_weight, query_bias, key_weight, value_weight, value_bias, out_weight, out_bias, attn_gain, attn_shift, up_weight, up_bias, down_weight, down_bias, ffn_gain, ffn_shift):
    params = tuple((p.astype(jnp.float32) for p in (query_weight, query_bias, key_weight, value_weight, value_bias, out_weight, out_bias, attn_gain, attn_shift, up_weight, up_bias, down_weight, down_bias, ffn_gain, ffn_shift)))
    positions = jnp.arange(LENGTH)
    inside = jnp.any((positions[None, None, :] >= span_start[:, :, None]) & (positions[None, None, :] < span_end[:, :, None]), axis=1)
    inside = inside.astype(jnp.float32).reshape(TOKENS, 1)
    rows = CHAINS_DEV * LENGTH
    inputs = tokens.astype(jnp.float32).reshape(N_FSDP, rows, D)
    grads_out = (cotangent.astype(jnp.float32) * inside).reshape(N_FSDP, rows, D)
    chain_lens = lengths.reshape(N_FSDP, CHAINS_DEV)

    def step(totals, item):
        block_in, block_grad, block_len = item
        output, backward = jax.vjp(lambda values, weights: forward(values, weights, block_len), block_in, params)
        input_back, param_back = backward(block_grad)
        totals = tuple((a + b for a, b in zip(totals, param_back)))
        return (totals, (output.astype(jnp.bfloat16), input_back.astype(jnp.bfloat16)))
    start = tuple((jnp.zeros(p.shape, jnp.float32) for p in params))
    grads, (outputs, input_backs) = lax.scan(step, start, (inputs, grads_out, chain_lens))
    return (outputs.reshape(TOKENS, D), input_backs.reshape(TOKENS, D), grads[0], grads[1], grads[2], grads[3], grads[4], grads[5], grads[6], grads[7], grads[8], grads[9], grads[10], grads[11], grads[12], grads[13], grads[14])
```

```python
import functools
import jax
import jax.numpy as jnp
from jax import lax
from jax.sharding import PartitionSpec as P
from jax.experimental import pallas as pl
from jax.experimental.pallas import tpu as pltpu

D = 768
HEADS = 12
HEAD = 64
epsilon = 1e-05
masked_score = -1000000000.0
F32 = jnp.float32
BF16 = jnp.bfloat16


def dot(left, right):
    return lax.dot_general(left, right, (((1,), (0,)), ((), ())), preferred_element_type=F32)


def dot_rt(left, right):
    return lax.dot_general(left, right, (((1,), (1,)), ((), ())), preferred_element_type=F32)


def dot_lt(left, right):
    return lax.dot_general(left, right, (((0,), (0,)), ((), ())), preferred_element_type=F32)


def call(body, grid, in_specs, out_specs, out_shape, scratch=(), flops=0, moved=0, vmem=60):
    return pl.pallas_call(
        body,
        grid_spec=pltpu.PrefetchScalarGridSpec(
            num_scalar_prefetch=0, grid=grid, in_specs=in_specs, out_specs=out_specs, scratch_shapes=scratch
        ),
        out_shape=out_shape,
        compiler_params=pltpu.CompilerParams(vmem_limit_bytes=vmem * 1024 * 1024),
        cost_estimate=pl.CostEstimate(flops=flops, bytes_accessed=moved, transcendentals=0),
    )


def shaped(shape, dtype):
    return jax.ShapeDtypeStruct(shape, dtype)


def half_mask(dtype, scale=1.0):
    lane = lax.broadcasted_iota(jnp.int32, (1, 128), 1)
    low = jnp.where(lane < HEAD, scale, 0.0).astype(dtype)
    high = jnp.where(lane < HEAD, 0.0, scale).astype(dtype)
    return low, high


def attn_fwd_body(len_ref, x_ref, wq_ref, wk_ref, wv_ref, bq_ref, bv_ref, q_ref, k_ref, v_ref, mix_ref, lse_ref):
    c = pl.program_id(0)
    x = x_ref[...]
    length = x.shape[0]
    q_ref[...] = (dot(x, wq_ref[...]) + bq_ref[...]).astype(BF16)
    k_ref[...] = dot(x, wk_ref[...]).astype(BF16)
    v_ref[...] = (dot(x, wv_ref[...]) + bv_ref[...]).astype(BF16)
    valid = lax.broadcasted_iota(jnp.int32, (1, length), 1) < len_ref[c]
    masks = half_mask(BF16, 0.125)
    lane = lax.broadcasted_iota(jnp.int32, (1, 128), 1)
    lses = jnp.zeros((length, 128), F32)
    for p in range(HEADS // 2):
        cols = slice(128 * p, 128 * p + 128)
        qp, kp, vp = q_ref[:, cols], k_ref[:, cols], v_ref[:, cols]
        outs = []
        for t in range(2):
            s = dot_rt(qp * masks[t], kp)
            s = jnp.where(valid, s, masked_score)
            m = jnp.max(s, axis=1, keepdims=True)
            e = jnp.exp(s - m)
            total = jnp.sum(e, axis=1, keepdims=True)
            pr = (e * (1.0 / total)).astype(BF16)
            outs.append(dot(pr, vp))
            lses = jnp.where(lane == 2 * p + t, m + jnp.log(total), lses)
        mix_ref[:, cols] = jnp.where(lane < HEAD, outs[0], outs[1]).astype(BF16)
    lse_ref[...] = lses


def attn_fwd(x, wq, wk, wv, bq, bv, lengths):
    rows = x.shape[0]
    n = lengths.shape[0]
    length = rows // n
    tile = pl.BlockSpec((length, D), lambda c: (c, 0))
    full = pl.BlockSpec((D, D), lambda c: (0, 0))
    one = pl.BlockSpec((1, D), lambda c: (0, 0))
    act = shaped((rows, D), BF16)
    return call(
        attn_fwd_body, (n,),
        [pl.BlockSpec(memory_space=pltpu.SMEM), tile, full, full, full, one, one],
        [tile, tile, tile, tile, pl.BlockSpec((length, 128), lambda c: (c, 0))],
        [act, act, act, act, shaped((rows, 128), F32)],
        flops=2 * rows * D * D * 3 + 4 * rows * length * D * 4, moved=rows * D * 10 + 6 * D * D,
    )(lengths, x, wq, wk, wv, bq, bv)


def attn_bwd_body(len_ref, q_ref, k_ref, v_ref, gm_ref, lse_ref, gq_ref, gk_ref, gv_ref, gbq_ref, gbv_ref):
    c = pl.program_id(0)
    length = q_ref.shape[0]
    valid = lax.broadcasted_iota(jnp.int32, (1, length), 1) < len_ref[c]
    masks = half_mask(BF16)
    scaled = half_mask(BF16, 0.125)

    @pl.when(c == 0)
    def _():
        gbq_ref[...] = jnp.zeros_like(gbq_ref)
        gbv_ref[...] = jnp.zeros_like(gbv_ref)

    for p in range(HEADS // 2):
        cols = slice(128 * p, 128 * p + 128)
        qp, kp, vp, gm = q_ref[:, cols], k_ref[:, cols], v_ref[:, cols], gm_ref[:, cols]
        gq, gk, gv = 0.0, 0.0, 0.0
        for t in range(2):
            h = 2 * p + t
            qt = qp * scaled[t]
            kt = kp * scaled[t]
            gt = gm * masks[t]
            s = dot_rt(qt, kp)
            s = jnp.where(valid, s, masked_score)
            pf = jnp.exp(s - lse_ref[:, h : h + 1])
            gp = dot_rt(gt, vp)
            gs = pf * (gp - jnp.sum(pf * gp, axis=1, keepdims=True))
            gs = gs.astype(BF16)
            gv = gv + dot_lt(pf.astype(BF16), gt)
            gq = gq + dot(gs, kt)
            gk = gk + dot_lt(gs, qt)
        gq, gk, gv = gq.astype(BF16), gk.astype(BF16), gv.astype(BF16)
        gq_ref[:, cols] = gq
        gk_ref[:, cols] = gk
        gv_ref[:, cols] = gv
        gbq_ref[:, cols] += jnp.sum(gq.astype(F32), axis=0, keepdims=True)
        gbv_ref[:, cols] += jnp.sum(gv.astype(F32), axis=0, keepdims=True)


def attn_bwd(q, k, v, gm, lse, lengths):
    rows = q.shape[0]
    n = lengths.shape[0]
    length = rows // n
    tile = pl.BlockSpec((length, D), lambda c: (c, 0))
    one = pl.BlockSpec((1, D), lambda c: (0, 0))
    act = shaped((rows, D), BF16)
    return call(
        attn_bwd_body, (n,),
        [pl.BlockSpec(memory_space=pltpu.SMEM), tile, tile, tile, tile, pl.BlockSpec((length, 128), lambda c: (c, 0))],
        [tile, tile, tile, one, one],
        [act, act, act, shaped((1, D), F32), shaped((1, D), F32)],
        flops=2 * rows * length * D * 5 * 4, moved=rows * D * 14,
    )(lengths, q, k, v, gm, lse)


def mean(v):
    return jnp.sum(v, axis=-1, keepdims=True) * (1.0 / D)


def normalize(values):
    center = values - mean(values)
    scale = lax.rsqrt(mean(center * center) + epsilon)
    return center * scale, scale


def norm_back(incoming, normed, scale, gain):
    weighted = incoming * gain
    return scale * (weighted - mean(weighted) - normed * mean(weighted * normed))


def colsum(v):
    return jnp.sum(v, axis=0, keepdims=True)


def gelu_parts(pre):
    cdf = 0.5 + 0.5 * lax.erf(pre * 0.7071067811865476)
    pdf = 0.3989422804014327 * jnp.exp(-0.5 * pre * pre)
    return pre * cdf, cdf + pre * pdf


def ffn_body(chunk, mix_ref, x_ref, gy_ref, wo_ref, wu_ref, wd_ref, small_ref, ub_ref,
             out_ref, hid_ref, gffn_ref, low_ref, gpre_ref, gattn_ref, g1_ref, gmix_ref, gsmall_ref, gub_ref, dg_ref):
    i = pl.program_id(0)
    bo, again, ashift, bd, fgain, fshift = (small_ref[j : j + 1, :] for j in range(6))
    ff = wu_ref.shape[1]

    @pl.when(i == 0)
    def _():
        gsmall_ref[...] = jnp.zeros_like(gsmall_ref)
        gub_ref[...] = jnp.zeros_like(gub_ref)

    attn = dot(mix_ref[...], wo_ref[...]) + bo
    xhat1, rs1 = normalize(x_ref[...].astype(F32) + attn)
    first = xhat1 * again + ashift
    low = first.astype(BF16)
    low_ref[...] = low
    ffn = 0.0
    for j in range(ff // chunk):
        cols = slice(j * chunk, (j + 1) * chunk)
        pre = dot(low, wu_ref[:, cols]) + ub_ref[:, cols]
        hid, dg = gelu_parts(pre)
        hid = hid.astype(BF16)
        hid_ref[:, cols] = hid
        dg_ref[:, cols] = dg.astype(dg_ref.dtype)
        ffn = ffn + dot(hid, wd_ref[cols, :])
    xhat2, rs2 = normalize(first + ffn + bd)
    out_ref[...] = (xhat2 * fgain + fshift).astype(BF16)
    gy = gy_ref[...].astype(F32)
    g2 = norm_back(gy, xhat2, rs2, fgain)
    gffn = g2.astype(BF16)
    gffn_ref[...] = gffn
    gsmall_ref[3:4, :] += colsum(gffn.astype(F32))
    gsmall_ref[4:5, :] += colsum(gy * xhat2)
    gsmall_ref[5:6, :] += colsum(gy)
    gfirst = g2
    for j in range(ff // chunk):
        cols = slice(j * chunk, (j + 1) * chunk)
        gh = dot_rt(gffn, wd_ref[cols, :])
        gpre = (gh * dg_ref[:, cols].astype(F32)).astype(BF16)
        gpre_ref[:, cols] = gpre
        gub_ref[:, cols] += colsum(gpre.astype(F32))
        gfirst = gfirst + dot_rt(gpre, wu_ref[:, cols])
    g1 = norm_back(gfirst, xhat1, rs1, again)
    gattn = g1.astype(BF16)
    g1_ref[...] = g1
    gattn_ref[...] = gattn
    gsmall_ref[0:1, :] += colsum(gattn.astype(F32))
    gsmall_ref[1:2, :] += colsum(gfirst * xhat1)
    gsmall_ref[2:3, :] += colsum(gfirst)
    gmix_ref[...] = dot_rt(gattn, wo_ref[...]).astype(BF16)


def ffn_both(mixed, x, gy, wo, wu, wd, small, ub, tile_rows=280, chunk=768, dg_dtype=F32):
    rows = x.shape[0]
    ff = wu.shape[1]
    n = rows // tile_rows
    tile = pl.BlockSpec((tile_rows, D), lambda c: (c, 0))
    wide = pl.BlockSpec((tile_rows, ff), lambda c: (c, 0))
    fixed = lambda s: pl.BlockSpec(s, lambda c: (0, 0), pipeline_mode=pl.Buffered(1))
    act = shaped((rows, D), BF16)
    big = shaped((rows, ff), BF16)
    return call(
        functools.partial(ffn_body, chunk), (n,),
        [tile, tile, tile, fixed((D, D)), fixed((D, ff)), fixed((ff, D)), fixed((8, D)), fixed((1, ff))],
        [tile, wide, tile, tile, wide, tile, tile, tile, pl.BlockSpec((8, D), lambda c: (0, 0)), pl.BlockSpec((1, ff), lambda c: (0, 0))],
        [act, big, act, act, big, act, shaped((rows, D), F32), act, shaped((8, D), F32), shaped((1, ff), F32)],
        scratch=[pltpu.VMEM((tile_rows, ff), dg_dtype)],
        flops=2 * rows * D * (2 * D + 4 * ff), moved=rows * (D * 20 + ff * 4) + D * (D + 2 * ff) * 2,
    )(mixed, x, gy, wo, wu, wd, small, ub)


def wgrad_body(l_ref, r_ref, o_ref):
    o_ref[...] = dot_lt(l_ref[...], r_ref[...]).astype(o_ref.dtype)


def wgrad(left, right, tile_m=384, dtype=BF16):
    rows, m = left.shape
    n = right.shape[1]
    tn = min(n, 768)
    return call(
        wgrad_body, (n // tn, m // tile_m),
        [pl.BlockSpec((rows, tile_m), lambda j, i: (0, i)), pl.BlockSpec((rows, tn), lambda j, i: (0, j))],
        pl.BlockSpec((tile_m, tn), lambda j, i: (i, j)),
        shaped((m, n), dtype),
        flops=2 * rows * m * n, moved=2 * (rows * (m + n) + m * n),
    )(left, right)


def wgrad3_body(l_ref, a_ref, b_ref, c_ref, oa_ref, ob_ref, oc_ref):
    left = l_ref[...]
    for r_ref, o_ref in ((a_ref, oa_ref), (b_ref, ob_ref), (c_ref, oc_ref)):
        o_ref[...] = dot_lt(left, r_ref[...]).astype(o_ref.dtype)


def wgrad3(left, a, b, c, tile_m=384, dtype=BF16):
    rows = left.shape[0]
    right = pl.BlockSpec((rows, D), lambda i: (0, 0))
    out = pl.BlockSpec((tile_m, D), lambda i: (i, 0))
    return call(
        wgrad3_body, (D // tile_m,),
        [pl.BlockSpec((rows, tile_m), lambda i: (0, i)), right, right, right],
        [out, out, out],
        [shaped((D, D), dtype)] * 3,
        flops=6 * rows * D * D, moved=2 * (4 * rows * D + 3 * D * D),
    )(left, a, b, c)


def input_grad_body(g1_ref, gq_ref, gk_ref, gv_ref, wq_ref, wk_ref, wv_ref, o_ref):
    total = g1_ref[...] + dot_rt(gq_ref[...], wq_ref[...])
    total = total + dot_rt(gk_ref[...], wk_ref[...]) + dot_rt(gv_ref[...], wv_ref[...])
    o_ref[...] = total.astype(BF16)


def input_grad(g1, gq, gk, gv, wq, wk, wv, tile_rows=280):
    rows = g1.shape[0]
    tile = pl.BlockSpec((tile_rows, D), lambda c: (c, 0))
    full = pl.BlockSpec((D, D), lambda c: (0, 0))
    return call(
        input_grad_body, (rows // tile_rows,),
        [tile, tile, tile, tile, full, full, full], tile, shaped((rows, D), BF16),
        flops=6 * rows * D * D, moved=rows * D * 12 + 6 * D * D,
    )(g1, gq, gk, gv, wq, wk, wv)


def shards(
    tokens, cotangent, lengths, span_start, span_end,
    query_weight, query_bias, key_weight, value_weight, value_bias, out_weight, out_bias,
    attn_gain, attn_shift, up_weight, up_bias, down_weight, down_bias, ffn_gain, ffn_shift,
):
    chains = lengths.shape[0]
    rows = tokens.shape[0]
    length = rows // chains
    own = query_weight.shape[0]
    parts = D // own
    ff = up_weight.shape[1]
    vectors = (query_bias, value_bias, out_bias, attn_gain, attn_shift, down_bias, ffn_gain, ffn_shift, up_bias)
    packed = jnp.concatenate(vectors)
    packed = jnp.pad(packed, (0, D - packed.shape[0])).reshape(1, D)
    wide = own * ff // D
    sent = jnp.concatenate(
        [query_weight, key_weight, value_weight, out_weight, up_weight.reshape(own, ff // D, D).swapaxes(0, 1).reshape(wide, D), down_weight, packed],
        axis=0,
    )
    held = lax.all_gather(sent, "fsdp", axis=0, tiled=False)
    wq, wk, wv, wo = (held[:, own * i : own * (i + 1)].reshape(D, D) for i in range(4))
    wu = jnp.concatenate(
        [held[:, own * (4 + i) : own * (5 + i)].reshape(D, D) for i in range(ff // D)], axis=1
    )
    wd = held[:, 4 * own + wide : 4 * own + 2 * wide].reshape(ff, D)
    small = held[:, -1].astype(F32)
    qb, vb, ob, again, ashift, db, fgain, fshift = (
        small[:, own * i : own * (i + 1)].reshape(1, D) for i in range(8)
    )
    ub = small[:, 8 * own : 8 * own + wide].reshape(1, ff)
    zero = jnp.zeros((1, D), F32)
    table = jnp.concatenate([ob, again, ashift, db, fgain, fshift, zero, zero], axis=0)

    positions = jnp.arange(length)
    inside = jnp.any(
        (positions[None, None, :] >= span_start[:, :, None]) & (positions[None, None, :] < span_end[:, :, None]),
        axis=1,
    )
    gy = jnp.where(inside.reshape(rows, 1), cotangent, jnp.zeros_like(cotangent))

    q, k, v, mixed, lse = attn_fwd(tokens, wq, wk, wv, qb, vb, lengths)
    layer_out, hidden, gffn, low, gpre, gattn, g1, gmixed, gtable, gub = ffn_both(
        mixed, tokens, gy, wo, wu, wd, table, ub
    )
    down_grad = wgrad(hidden, gffn)
    up_grad = wgrad(low, gpre)
    gathered_ffn = jnp.concatenate(
        [up_grad.reshape(parts, wide, D), down_grad.reshape(parts, wide, D)], axis=1
    )
    ffn_own = lax.psum_scatter(gathered_ffn, "fsdp", scatter_dimension=0, tiled=False)
    out_grad = wgrad(mixed, gattn)
    gq, gk, gv, gqb, gvb = attn_bwd(q, k, v, gmixed, lse, lengths)
    query_grad, key_grad, value_grad = wgrad3(tokens, gq, gk, gv)
    parts_of = [gqb, gvb, gtable[0:1], gtable[1:2], gtable[2:3], gtable[3:4], gtable[4:5], gtable[5:6]]
    vec = jnp.concatenate([p.reshape(parts, own) for p in parts_of] + [gub.reshape(parts, wide)], axis=1)
    vec = jnp.pad(vec.astype(BF16), ((0, 0), (0, D - vec.shape[1]))).reshape(parts, 1, D)
    attn_parts = jnp.concatenate(
        [g.reshape(parts, own, D) for g in (query_grad, key_grad, value_grad, out_grad)] + [vec], axis=1
    )
    attn_own = lax.psum_scatter(attn_parts, "fsdp", scatter_dimension=0, tiled=False)
    in_grad = input_grad(g1, gq, gk, gv, wq, wk, wv)

    attn_own = attn_own.astype(F32)
    ffn_own = ffn_own.astype(F32)
    gq_w, gk_w, gv_w, go_w = (attn_own[own * i : own * (i + 1)] for i in range(4))
    vec = attn_own[-1]
    gqb, gvb, gob, gag, gas, gdb, gfg, gfs = (vec[own * i : own * (i + 1)] for i in range(8))
    gub = vec[8 * own : 8 * own + wide]
    gup = ffn_own[:wide].reshape(own, ff)
    gdown = ffn_own[wide:]
    return (
        layer_out, in_grad, gq_w, gqb, gk_w, gv_w, gvb, go_w, gob, gag, gas, gup, gub, gdown, gdb, gfg, gfs,
    )


def solution(mesh):
    two, one = P("fsdp", None), P("fsdp")
    return jax.shard_map(
        shards,
        mesh=mesh,
        in_specs=(two, two, one, two, two, two, one, two, two, one, two, one, one, one, two, one, two, one, one, one),
        out_specs=(two, two, two, one, two, two, one, two, one, one, one, two, one, two, one, one, one),
        check_vma=False,
    )
```

```python
import functools
import jax
import jax.numpy as jnp
from jax import lax
from jax.sharding import PartitionSpec as P
from jax.experimental import pallas as pl
from jax.experimental.pallas import tpu as pltpu

D = 768
HEADS = 12
HEAD = 64
epsilon = 1e-05
masked_score = -1000000000.0
F32 = jnp.float32
BF16 = jnp.bfloat16
WAIT = 1 << 40


def dot(left, right):
    return lax.dot_general(left, right, (((1,), (0,)), ((), ())), preferred_element_type=F32)


def dot_rt(left, right):
    return lax.dot_general(left, right, (((1,), (1,)), ((), ())), preferred_element_type=F32)


def dot_lt(left, right):
    return lax.dot_general(left, right, (((0,), (0,)), ((), ())), preferred_element_type=F32)


def call(body, grid, in_specs, out_specs, out_shape, scratch=(), flops=0, moved=0, vmem=60, aliases={}, weight=0):
    return pl.pallas_call(
        body,
        grid_spec=pltpu.PrefetchScalarGridSpec(
            num_scalar_prefetch=0, grid=grid, in_specs=in_specs, out_specs=out_specs, scratch_shapes=scratch
        ),
        out_shape=out_shape,
        input_output_aliases=aliases,
        compiler_params=pltpu.CompilerParams(vmem_limit_bytes=vmem * 1024 * 1024),
        cost_estimate=pl.CostEstimate(flops=weight, bytes_accessed=weight // 64, transcendentals=0),
    )


def shaped(shape, dtype):
    return jax.ShapeDtypeStruct(shape, dtype)


def half_mask(dtype, scale=1.0):
    lane = lax.broadcasted_iota(jnp.int32, (1, 128), 1)
    low = jnp.where(lane < HEAD, scale, 0.0).astype(dtype)
    high = jnp.where(lane < HEAD, 0.0, scale).astype(dtype)
    return low, high


def attn_fwd_body(len_ref, x_ref, wq_ref, wk_ref, wv_ref, bq_ref, bv_ref, q_ref, k_ref, v_ref, mix_ref, lse_ref):
    c = pl.program_id(0)
    x = x_ref[...]
    length = x.shape[0]
    q_ref[...] = (dot(x, wq_ref[...]) + bq_ref[...]).astype(BF16)
    k_ref[...] = dot(x, wk_ref[...]).astype(BF16)
    v_ref[...] = (dot(x, wv_ref[...]) + bv_ref[...]).astype(BF16)
    valid = lax.broadcasted_iota(jnp.int32, (1, length), 1) < len_ref[c]
    masks = half_mask(BF16, 0.125)
    lane = lax.broadcasted_iota(jnp.int32, (1, 128), 1)
    lses = jnp.zeros((length, 128), F32)
    for p in range(HEADS // 2):
        cols = slice(128 * p, 128 * p + 128)
        qp, kp, vp = q_ref[:, cols], k_ref[:, cols], v_ref[:, cols]
        outs = []
        for t in range(2):
            s = dot_rt(qp * masks[t], kp)
            s = jnp.where(valid, s, masked_score)
            m = jnp.max(s, axis=1, keepdims=True)
            e = jnp.exp(s - m)
            total = jnp.sum(e, axis=1, keepdims=True)
            pr = (e * (1.0 / total)).astype(BF16)
            outs.append(dot(pr, vp))
            lses = jnp.where(lane == 2 * p + t, m + jnp.log(total), lses)
        mix_ref[:, cols] = jnp.where(lane < HEAD, outs[0], outs[1]).astype(BF16)
    lse_ref[...] = lses


def attn_fwd(x, wq, wk, wv, bq, bv, lengths):
    rows = x.shape[0]
    n = lengths.shape[0]
    length = rows // n
    tile = pl.BlockSpec((length, D), lambda c: (c, 0))
    full = pl.BlockSpec((D, D), lambda c: (0, 0))
    one = pl.BlockSpec((1, D), lambda c: (0, 0))
    act = shaped((rows, D), BF16)
    return call(
        attn_fwd_body, (n,),
        [pl.BlockSpec(memory_space=pltpu.SMEM), tile, full, full, full, one, one],
        [tile, tile, tile, tile, pl.BlockSpec((length, 128), lambda c: (c, 0))],
        [act, act, act, act, shaped((rows, 128), F32)],
        flops=2 * rows * D * D * 3 + 4 * rows * length * D * 4, moved=rows * D * 10 + 6 * D * D,
    )(lengths, x, wq, wk, wv, bq, bv)


def attn_bwd_body(start, len_ref, q_ref, k_ref, v_ref, gm_ref, lse_ref, *rest):
    gq_ref, gk_ref, gv_ref, gbq_ref, gbv_ref = rest[-5:]
    c = pl.program_id(0)
    length = q_ref.shape[0]
    valid = lax.broadcasted_iota(jnp.int32, (1, length), 1) < len_ref[c + start]
    masks = half_mask(BF16)
    scaled = half_mask(BF16, 0.125)

    @pl.when(c == 0)
    def _():
        gbq_ref[...] = rest[3][...] if start else jnp.zeros_like(gbq_ref)
        gbv_ref[...] = rest[4][...] if start else jnp.zeros_like(gbv_ref)

    for p in range(HEADS // 2):
        cols = slice(128 * p, 128 * p + 128)
        qp, kp, vp, gm = q_ref[:, cols], k_ref[:, cols], v_ref[:, cols], gm_ref[:, cols]
        gq, gk, gv = 0.0, 0.0, 0.0
        for t in range(2):
            h = 2 * p + t
            qt = qp * scaled[t]
            kt = kp * scaled[t]
            gt = gm * masks[t]
            s = dot_rt(qt, kp)
            s = jnp.where(valid, s, masked_score)
            pf = jnp.exp(s - lse_ref[:, h : h + 1])
            gp = dot_rt(gt, vp)
            gs = pf * (gp - jnp.sum(pf * gp, axis=1, keepdims=True))
            gs = gs.astype(BF16)
            gv = gv + dot_lt(pf.astype(BF16), gt)
            gq = gq + dot(gs, kt)
            gk = gk + dot_lt(gs, qt)
        gq, gk, gv = gq.astype(BF16), gk.astype(BF16), gv.astype(BF16)
        gq_ref[:, cols] = gq
        gk_ref[:, cols] = gk
        gv_ref[:, cols] = gv
        gbq_ref[:, cols] += jnp.sum(gq.astype(F32), axis=0, keepdims=True)
        gbv_ref[:, cols] += jnp.sum(gv.astype(F32), axis=0, keepdims=True)


def attn_bwd(q, k, v, gm, lse, lengths, start=0, stop=None, before=(), weight=0):
    rows = q.shape[0]
    n = lengths.shape[0]
    stop = n if stop is None else stop
    length = rows // n
    tile = pl.BlockSpec((length, D), lambda c: (c + start, 0))
    one = pl.BlockSpec((1, D), lambda c: (0, 0))
    act = shaped((rows, D), BF16)
    whole = pl.BlockSpec(memory_space=pl.ANY)
    return call(
        functools.partial(attn_bwd_body, start), (stop - start,),
        [pl.BlockSpec(memory_space=pltpu.SMEM), tile, tile, tile, tile, pl.BlockSpec((length, 128), lambda c: (c + start, 0))]
        + ([whole, whole, whole, one, one] if before else []),
        [tile, tile, tile, one, one],
        [act, act, act, shaped((1, D), F32), shaped((1, D), F32)],
        flops=2 * (stop - start) * length * length * D * 5 * 4, moved=(stop - start) * length * D * 14,
        aliases={6: 0, 7: 1, 8: 2} if before else {}, weight=weight,
    )(lengths, q, k, v, gm, lse, *before)


def mean(v):
    return jnp.sum(v, axis=-1, keepdims=True) * (1.0 / D)


def normalize(values):
    center = values - mean(values)
    scale = lax.rsqrt(mean(center * center) + epsilon)
    return center * scale, scale


def norm_back(incoming, normed, scale, gain):
    weighted = incoming * gain
    return scale * (weighted - mean(weighted) - normed * mean(weighted * normed))


def colsum(v):
    return jnp.sum(v, axis=0, keepdims=True)


def gelu_parts(pre):
    cdf = 0.5 + 0.5 * lax.erf(pre * 0.7071067811865476)
    pdf = 0.3989422804014327 * jnp.exp(-0.5 * pre * pre)
    return pre * cdf, cdf + pre * pdf


def wgrad_body(l_ref, r_ref, o_ref):
    o_ref[...] = dot_lt(l_ref[...], r_ref[...]).astype(o_ref.dtype)


def wgrad(left, right, tile_m=768, dtype=BF16):
    rows, m = left.shape
    n = right.shape[1]
    tn = min(n, 768)
    return call(
        wgrad_body, (n // tn, m // tile_m),
        [pl.BlockSpec((rows, tile_m), lambda j, i: (0, i)), pl.BlockSpec((rows, tn), lambda j, i: (0, j))],
        pl.BlockSpec((tile_m, tn), lambda j, i: (i, j)),
        shaped((m, n), dtype),
        flops=2 * rows * m * n, moved=2 * (rows * (m + n) + m * n),
    )(left, right)

def place():
    idx = lax.axis_index("fsdp")
    return idx % 2, (idx // 2) % 4, idx // 8

def swap(n, bits):
    return [(i, i ^ bits) for i in range(n)]

def shift(n, k):
    return [(i, (i + 8 * k) % n) for i in range(n)]

def hop(value, pairs):
    return lax.ppermute(value, "fsdp", pairs)


def gather_blocks(block, n):
    far = n // 8
    zs = [hop(block, shift(n, k)) for k in range(1, far)]
    x0, y0, d0 = (hop(block, swap(n, b)) for b in (2, 4, 6))
    line = jnp.stack(zs)
    first = jnp.stack([block, x0, y0, d0])
    first_other = hop(first, swap(n, 1))
    line_other = hop(line, swap(n, 1))
    xs = hop(line, swap(n, 2))
    ys = hop(line, swap(n, 4))
    ds = jnp.stack([hop(d0, shift(n, k)) for k in range(1, far)])
    rest = jnp.concatenate([xs, ys, ds])
    rest_other = hop(rest, swap(n, 1))
    return (first, line, rest), (first_other, line_other, rest_other)


def sources(far):
    out = [(0, i, i, 0) for i in range(4)]
    out += [(1, k - 1, 0, k) for k in range(1, far)]
    out += [(2, (d - 1) * (far - 1) + k - 1, d, k) for d in (1, 2, 3) for k in range(1, far)]
    return out


def assemble_body(far, own, at_ref, f_ref, l_ref, r_ref, fo_ref, lo_ref, ro_ref, wq_ref, wk_ref, wv_ref, table_ref, ub_ref):
    core, fast, slow = at_ref[0], at_ref[1], at_ref[2]
    first = core == 0
    mine, other = (f_ref, l_ref, r_ref), (fo_ref, lo_ref, ro_ref)
    table = jnp.zeros((8, D), F32)
    ub = jnp.zeros((1, ub_ref.shape[1]), F32)
    for array, i, dxy, dz in sources(far):
        chip = ((slow - dz) % far) * 4 + (fast ^ dxy)
        a, b = mine[array][i], other[array][i]
        low, high = jnp.where(first, a, b), jnp.where(first, b, a)
        for m, ref in enumerate((wq_ref, wk_ref, wv_ref)):
            rows = slice(own * m, own * m + own)
            ref[chip] = jnp.concatenate([low[rows], high[rows]], axis=0)
        for side, part in ((0, low), (1, high)):
            tail = part[3 * own :].astype(F32)
            spot = chip * 2 + side
            lane = lax.broadcasted_iota(jnp.int32, (1, D), 1)
            table = table + pltpu.roll(jnp.where(lane < own, tail, 0.0), spot * own, 1)
            wide = tail[0:1, 128:256]
            wide = jnp.concatenate([wide, jnp.zeros((1, ub_ref.shape[1] - 128), F32)], axis=1)
            ub = ub + pltpu.roll(wide, spot * 4 * own, 1)
    table_ref[...] = table
    ub_ref[...] = ub


def assemble(at, mine, other, own, n):
    far = n // 8
    full = lambda a: pl.BlockSpec(a.shape, lambda i: (0,) * a.ndim)
    arrays = list(mine) + list(other)
    w = shaped((n // 2, 2 * own, D), BF16)
    outs = [w, w, w, shaped((8, D), F32), shaped((1, 4 * D), F32)]
    wq, wk, wv, table, ub = call(
        functools.partial(assemble_body, far, own), (1,),
        [pl.BlockSpec(memory_space=pltpu.SMEM)] + [full(a) for a in arrays],
        [full(a) for a in outs], outs, moved=7 * D * D * 2,
    )(at, *arrays)
    return wq.reshape(D, D), wk.reshape(D, D), wv.reshape(D, D), table, ub


def pack_small(vectors, wide):
    total = jnp.pad(wide[None, :], ((0, 7), (128, D - 128 - wide.shape[0])))
    for i, v in enumerate(vectors):
        total = total + jnp.pad(v[None, :], ((i, 7 - i), (0, D - v.shape[0])))
    return total


def ffn_raw_body(chunk, own, mix_ref, x_ref, gy_ref, raw_ref, small_ref, ub_ref, *rest):
    outs, (dg_ref, wo_ref, wu_ref) = rest[:-3], rest[-3:]
    wide = 4 * own

    @pl.when(pl.program_id(0) == 0)
    def _():
        def step(i, _):
            low, high = raw_ref[2 * i, wide:], raw_ref[2 * i + 1, wide:]
            at = pl.ds(pl.multiple_of(2 * own * i, 16), 2 * own)
            for j in range(5):
                rows = slice(own * j, own * j + own)
                both = jnp.concatenate([low[rows], high[rows]], axis=0)
                if j < 4:
                    wu_ref[at, D * j : D * j + D] = both
                else:
                    wo_ref[at, :] = both
            return 0

        lax.fori_loop(0, D // (2 * own), step, 0)

    ffn_steps(chunk, mix_ref, x_ref, gy_ref, wo_ref, wu_ref, RawDown(raw_ref, wide), small_ref, ub_ref, *outs, dg_ref)


class RawDown:
    def __init__(self, ref, wide):
        self.ref, self.wide = ref, wide

    def rows(self, start, size):
        return self.ref[start // self.wide : (start + size) // self.wide, : self.wide].reshape(size, D)


class FullDown:
    def __init__(self, ref):
        self.ref = ref

    def rows(self, start, size):
        return self.ref[start : start + size, :]


def ffn_steps(chunk, mix_ref, x_ref, gy_ref, wo_ref, wu_ref, down, small_ref, ub_ref,
              out_ref, hid_ref, gffn_ref, low_ref, gpre_ref, gattn_ref, g1_ref, gmix_ref, gsmall_ref, gub_ref, dg_ref):
    i = pl.program_id(0)
    bo, again, ashift, bd, fgain, fshift = (small_ref[j : j + 1, :] for j in range(2, 8))
    ff = wu_ref.shape[1]

    @pl.when(i == 0)
    def _():
        gsmall_ref[...] = jnp.zeros_like(gsmall_ref)
        gub_ref[...] = jnp.zeros_like(gub_ref)

    attn = dot(mix_ref[...], wo_ref[...]) + bo
    xhat1, rs1 = normalize(x_ref[...].astype(F32) + attn)
    first = xhat1 * again + ashift
    low = first.astype(BF16)
    low_ref[...] = low
    ffn = 0.0
    for j in range(ff // chunk):
        cols = slice(j * chunk, (j + 1) * chunk)
        pre = dot(low, wu_ref[:, cols]) + ub_ref[:, cols]
        hid, dg = gelu_parts(pre)
        hid = hid.astype(BF16)
        hid_ref[:, cols] = hid
        dg_ref[:, cols] = dg.astype(dg_ref.dtype)
        ffn = ffn + dot(hid, down.rows(j * chunk, chunk))
    xhat2, rs2 = normalize(first + ffn + bd)
    out_ref[...] = (xhat2 * fgain + fshift).astype(BF16)
    gy = gy_ref[...].astype(F32)
    g2 = norm_back(gy, xhat2, rs2, fgain)
    gffn = g2.astype(BF16)
    gffn_ref[...] = gffn
    gsmall_ref[5:6, :] += colsum(gffn.astype(F32))
    gsmall_ref[6:7, :] += colsum(gy * xhat2)
    gsmall_ref[7:8, :] += colsum(gy)
    gfirst = g2
    for j in range(ff // chunk):
        cols = slice(j * chunk, (j + 1) * chunk)
        gh = dot_rt(gffn, down.rows(j * chunk, chunk))
        gpre = (gh * dg_ref[:, cols].astype(F32)).astype(BF16)
        gpre_ref[:, cols] = gpre
        gub_ref[:, cols] += colsum(gpre.astype(F32))
        gfirst = gfirst + dot_rt(gpre, wu_ref[:, cols])
    g1 = norm_back(gfirst, xhat1, rs1, again)
    gattn = g1.astype(BF16)
    g1_ref[...] = g1
    gattn_ref[...] = gattn
    gsmall_ref[2:3, :] += colsum(gattn.astype(F32))
    gsmall_ref[3:4, :] += colsum(gfirst * xhat1)
    gsmall_ref[4:5, :] += colsum(gfirst)
    gmix_ref[...] = dot_rt(gattn, wo_ref[...]).astype(BF16)


def ffn_full_body(chunk, mix_ref, x_ref, gy_ref, wo_ref, wu_ref, wd_ref, small_ref, ub_ref, *rest):
    ffn_steps(chunk, mix_ref, x_ref, gy_ref, wo_ref, wu_ref, FullDown(wd_ref), small_ref, ub_ref, *rest)


def ffn_both(mixed, x, gy, weights, small, ub, own=0, tile_rows=280, chunk=768):
    rows = x.shape[0]
    ff = ub.shape[1]
    tile = pl.BlockSpec((tile_rows, D), lambda c: (c, 0))
    wide = pl.BlockSpec((tile_rows, ff), lambda c: (c, 0))
    fixed = lambda a: pl.BlockSpec(a.shape, lambda c: (0,) * a.ndim, pipeline_mode=pl.Buffered(1))
    act = shaped((rows, D), BF16)
    big = shaped((rows, ff), BF16)
    scratch = [pltpu.VMEM((tile_rows, ff), F32)]
    if len(weights) == 1:
        body = functools.partial(ffn_raw_body, chunk, own)
        scratch += [pltpu.VMEM((D, D), BF16), pltpu.VMEM((D, ff), BF16)]
    else:
        body = functools.partial(ffn_full_body, chunk)
    return call(
        body, (rows // tile_rows,),
        [tile, tile, tile] + [fixed(w) for w in weights] + [fixed(small), fixed(ub)],
        [tile, wide, tile, tile, wide, tile, tile, tile, pl.BlockSpec((8, D), lambda c: (0, 0)), pl.BlockSpec((1, ff), lambda c: (0, 0))],
        [act, big, act, act, big, act, shaped((rows, D), F32), act, shaped((8, D), F32), shaped((1, ff), F32)],
        scratch=scratch,
        flops=2 * rows * D * (2 * D + 4 * ff), moved=rows * (D * 20 + ff * 4) + D * (D + 2 * ff) * 2,
    )(mixed, x, gy, *weights, small, ub)


def row_block(at_ref, far, own, dxy, dz):
    chip = ((at_ref[2] + dz) % far) * 4 + (at_ref[1] ^ dxy)
    return tuple(2 * chip + side for side in (at_ref[0], 1 - at_ref[0]))


def acc_rows(ref, m, d, own):
    at = pl.ds(pl.multiple_of(own * d, 8), own)
    return ref[at, :] if m is None else ref[m, at, :]


def wgrad_down_body(far, own, at_ref, hid_ref, gffn_ref, *rest):
    outs, acc_ref = rest[:-1], rest[-1]
    acc_ref[...] = dot_lt(hid_ref[...], gffn_ref[...])
    dz = (pl.program_id(0) - at_ref[2]) % far
    for dxy in range(4):
        chip = at_ref[1] ^ dxy
        for out, side in zip(outs, (at_ref[0], 1 - at_ref[0])):
            out[dxy, dz] = acc_rows(acc_ref, None, 2 * chip + side, own).astype(BF16)


def keep_send(*shape):
    out = shaped((4,) + shape, BF16)
    spec = pl.BlockSpec(out.shape, lambda j: (0,) * len(out.shape))
    return [spec, spec], [out, out]


def wgrad_down(at, hidden, gffn, n):
    rows, ff = hidden.shape
    far = n // 8
    own = ff // n
    specs, outs = keep_send(far, own, D)
    return call(
        functools.partial(wgrad_down_body, far, own), (far,),
        [pl.BlockSpec(memory_space=pltpu.SMEM), pl.BlockSpec((rows, ff // far), lambda j: (0, j)), pl.BlockSpec((rows, D), lambda j: (0, 0))],
        specs, outs, scratch=[pltpu.VMEM((ff // far, D), F32)],
        flops=2 * rows * D * ff, moved=2 * (rows * (D + ff) + D * ff),
    )(at, hidden, gffn)


def wgrad_up_body(far, own, at_ref, low_ref, gpre_ref, mix_ref, gattn_ref, *rest):
    outs, acc_ref = rest[:-1], rest[-1]
    j = pl.program_id(0)

    @pl.when(j < 4)
    def _():
        acc_ref[j] = dot_lt(low_ref[...], gpre_ref[...])

    @pl.when(j == 4)
    def _():
        acc_ref[4] = dot_lt(mix_ref[...], gattn_ref[...])
        for dxy in range(4):
            for dz in range(far):
                for k, d in enumerate(row_block(at_ref, far, own, dxy, dz)):
                    value = jnp.concatenate([acc_rows(acc_ref, m, d, own) for m in range(5)], axis=0)
                    outs[k][dxy, dz] = value.astype(BF16)


def wgrad_up(at, low, gpre, mixed, gattn, own, n):
    rows = low.shape[0]
    far = n // 8
    act = pl.BlockSpec((rows, D), lambda j: (0, 0))
    specs, outs = keep_send(far, 5 * own, D)
    return call(
        functools.partial(wgrad_up_body, far, own), (5,),
        [pl.BlockSpec(memory_space=pltpu.SMEM), act, pl.BlockSpec((rows, D), lambda j: (0, jnp.minimum(j, 3))), act, act],
        specs, outs, scratch=[pltpu.VMEM((5, D, D), F32)],
        flops=10 * rows * D * D, moved=2 * (7 * rows * D + 5 * D * D),
    )(at, low, gpre, mixed, gattn)


def wgrad_in_body(far, own, at_ref, x_ref, gq_ref, gk_ref, gv_ref, small_ref, ub_ref, *rest):
    outs, acc_ref = rest[:-1], rest[-1]
    left = x_ref[...]
    for m, ref in enumerate((gq_ref, gk_ref, gv_ref)):
        acc_ref[m] = dot_lt(left, ref[...])
    lane = lax.broadcasted_iota(jnp.int32, (8, D), 1)
    row = lax.broadcasted_iota(jnp.int32, (8, D), 0)
    ff = ub_ref.shape[1]
    wide = ff // (8 * far)
    for dxy in range(4):
        for dz in range(far):
            for k, d in enumerate(row_block(at_ref, far, own, dxy, dz)):
                tail = pltpu.roll(small_ref[...], (D - own * d) % D, 1)
                ub = pltpu.roll(ub_ref[...], (ff + 128 - wide * d) % ff, 1)[:, :D]
                tail = jnp.where(lane < own, tail, 0.0)
                tail = jnp.where((row == 0) & (lane >= 128) & (lane < 128 + wide), ub, tail)
                parts = [acc_rows(acc_ref, m, d, own) for m in range(3)] + [tail]
                outs[k][dxy, dz] = jnp.concatenate(parts, axis=0).astype(BF16)


def wgrad_in(at, x, gq, gk, gv, small, ub, own, n):
    rows = x.shape[0]
    far = n // 8
    full = lambda a: pl.BlockSpec(a.shape, lambda i: (0,) * a.ndim)
    specs, outs = keep_send(far, 3 * own + 8, D)
    return call(
        functools.partial(wgrad_in_body, far, own), (1,),
        [pl.BlockSpec(memory_space=pltpu.SMEM)] + [full(a) for a in (x, gq, gk, gv, small, ub)],
        specs, outs, scratch=[pltpu.VMEM((3, D, D), F32)],
        flops=6 * rows * D * D, moved=2 * (4 * rows * D + 3 * D * D),
    )(at, x, gq, gk, gv, small, ub)


def pair_sum(keep, other, i):
    return keep[i].astype(F32) + other[i].astype(F32)


def near_parts(keep, other):
    return tuple(pair_sum(keep, other, i).astype(BF16) for i in (1, 2, 3))


def near_hops(parts, n):
    return tuple(hop(p, swap(n, 2 * i)) for i, p in enumerate(parts, 1))


def line_body(keep_ref, other_ref, x_ref, y_ref, d_ref, base_ref, *sent):
    total = keep_ref[...].astype(F32) + other_ref[...].astype(F32)
    for ref in (x_ref, y_ref, d_ref):
        total = total + ref[...].astype(F32)
    base_ref[...] = total[0, 0]
    for k, ref in enumerate(sent, 1):
        ref[...] = total[0, k].astype(BF16)


def line_sum(keep, other, near):
    far, rows = keep.shape[1:3]
    block = pl.BlockSpec((1, far, rows, D), lambda i: (0, 0, 0, 0))
    part = pl.BlockSpec((rows, D), lambda i: (0, 0))
    base, *sent = call(
        line_body, (1,), [block] * 5, [part] * far,
        [shaped((rows, D), F32)] + [shaped((rows, D), BF16)] * (far - 1), weight=WAIT,
    )(keep, other, *(p[None] for p in near))
    return base, sent


def far_hops(sent, n, which):
    return {k: hop(sent[k - 1], shift(n, k)) for k in which}


def last_sum(base, far):
    return base + sum(p.astype(F32) for p in far.values())


def wgrad3_body(l_ref, a_ref, b_ref, c_ref, oa_ref, ob_ref, oc_ref):
    left = l_ref[...]
    for r_ref, o_ref in ((a_ref, oa_ref), (b_ref, ob_ref), (c_ref, oc_ref)):
        o_ref[...] = dot_lt(left, r_ref[...]).astype(o_ref.dtype)


def wgrad3(left, a, b, c, tile_m=384, dtype=BF16):
    rows = left.shape[0]
    right = pl.BlockSpec((rows, D), lambda i: (0, 0))
    out = pl.BlockSpec((tile_m, D), lambda i: (i, 0))
    return call(
        wgrad3_body, (D // tile_m,),
        [pl.BlockSpec((rows, tile_m), lambda i: (0, i)), right, right, right],
        [out, out, out],
        [shaped((D, D), dtype)] * 3,
        flops=6 * rows * D * D, moved=2 * (4 * rows * D + 3 * D * D),
    )(left, a, b, c)


def input_grad_body(g1_ref, gq_ref, gk_ref, gv_ref, wq_ref, wk_ref, wv_ref, *rest):
    total = g1_ref[...] + dot_rt(gq_ref[...], wq_ref[...])
    total = total + dot_rt(gk_ref[...], wk_ref[...]) + dot_rt(gv_ref[...], wv_ref[...])
    rest[-1][...] = total.astype(BF16)


def input_grad(g1, gq, gk, gv, wq, wk, wv, start=0, stop=4, before=(), tiles=4):
    rows = g1.shape[0]
    tile = pl.BlockSpec((rows // tiles, D), lambda c: (c + start, 0))
    full = pl.BlockSpec((D, D), lambda c: (0, 0))
    return call(
        input_grad_body, (stop - start,),
        [tile, tile, tile, tile, full, full, full] + [pl.BlockSpec(memory_space=pl.ANY)] * len(before),
        tile, shaped((rows, D), BF16), aliases={7: 0} if before else {},
        flops=6 * rows * D * D, moved=rows * D * 12 + 6 * D * D,
    )(g1, gq, gk, gv, wq, wk, wv, *before)


def residue_mask(cotangent, span_start, span_end):
    chains = span_start.shape[0]
    rows = cotangent.shape[0]
    positions = jnp.arange(rows // chains)
    inside = jnp.any(
        (positions[None, None, :] >= span_start[:, :, None]) & (positions[None, None, :] < span_end[:, :, None]),
        axis=1,
    )
    return jnp.where(inside.reshape(rows, 1), cotangent, jnp.zeros_like(cotangent))


def tie(*values):
    return lax.optimization_barrier(values)


def chunked(weight):
    own = weight.shape[0]
    return weight.reshape(own, -1, D).swapaxes(0, 1).reshape(-1, D)


def fast_shards(
    n, tokens, cotangent, lengths, span_start, span_end,
    query_weight, query_bias, key_weight, value_weight, value_bias, out_weight, out_bias,
    attn_gain, attn_shift, up_weight, up_bias, down_weight, down_bias, ffn_gain, ffn_shift,
):
    own = query_weight.shape[0]
    wide = up_bias.shape[0]
    vectors = (query_bias, value_bias, out_bias, attn_gain, attn_shift, down_bias, ffn_gain, ffn_shift)
    at = jnp.stack(place()).astype(jnp.int32)
    block = jnp.concatenate([query_weight, key_weight, value_weight, pack_small(vectors, up_bias)], axis=0)
    sent = jnp.concatenate([down_weight, chunked(up_weight), out_weight], axis=0)
    sent = jnp.pad(sent, ((0, -sent.shape[0] % 16), (0, 0)))
    raw = lax.all_gather(sent, "fsdp", axis=0, tiled=False)
    mine, other = gather_blocks(block, n)
    wq, wk, wv, table, ub = assemble(at, mine, other, own, n)
    gy = residue_mask(cotangent, span_start, span_end)

    q, k, v, mixed, lse = attn_fwd(tokens, wq, wk, wv, table[0:1], table[1:2], lengths)
    layer_out, hidden, gffn, low, gpre, gattn, g1, gmixed, gtable, gub = ffn_both(
        mixed, tokens, gy, (raw,), table, ub, own
    )
    chains = lengths.shape[0]
    cuts = (0, 1, 4, chains)
    keep_d, send_d = wgrad_down(at, hidden, gffn, n)
    gmixed, keep_d, send_d = tie(gmixed, keep_d, send_d)
    other_d = hop(send_d, swap(n, 1))
    begun = attn_bwd(q, k, v, gmixed, lse, lengths, cuts[0], cuts[1], weight=WAIT)
    begun, other_d = tie(begun, other_d)
    low, begun, parts_d = tie(low, begun, near_parts(keep_d, other_d))
    near_d = near_hops(parts_d, n)
    keep_u, send_u = wgrad_up(at, low, gpre, mixed, gattn, own, n)
    begun, keep_u, send_u = tie(begun, keep_u, send_u)
    other_u = hop(send_u, swap(n, 1))
    begun = attn_bwd(q, k, v, gmixed, lse, lengths, cuts[1], cuts[2], begun)
    begun, near_d = tie(begun, near_d)
    base_d, sent_d = line_sum(keep_d, other_d, near_d)
    base_d, sent_d, other_u = tie(base_d, sent_d, other_u)
    far_d = far_hops(sent_d, n, (1, 3))
    begun, parts_u = tie(begun, near_parts(keep_u, other_u))
    near_u = near_hops(parts_u, n)
    gq, gk, gv, gqb, gvb = attn_bwd(q, k, v, gmixed, lse, lengths, cuts[2], cuts[3], begun)
    gq, far_d, sent_d = tie(gq, far_d, sent_d)
    far_d.update(far_hops(sent_d, n, (2,)))
    gtable = jnp.concatenate([gqb, gvb, gtable[2:]], axis=0)
    keep_i, send_i = wgrad_in(at, tokens, gq, gk, gv, gtable, gub, own, n)
    g1, keep_i, send_i = tie(g1, keep_i, send_i)
    other_i = hop(send_i, swap(n, 1))
    in_grad = input_grad(g1, gq, gk, gv, wq, wk, wv, 0, 2)
    in_grad, near_u, far_d = tie(in_grad, near_u, far_d)
    base_u, sent_u = line_sum(keep_u, other_u, near_u)
    base_u, sent_u, other_i = tie(base_u, sent_u, other_i)
    far_u = far_hops(sent_u, n, (1, 2))
    in_grad, parts_i = tie(in_grad, near_parts(keep_i, other_i))
    near_i = near_hops(parts_i, n)
    in_grad = input_grad(g1, gq, gk, gv, wq, wk, wv, 2, 4, (in_grad,))
    in_grad, near_i, far_u = tie(in_grad, near_i, far_u)
    base_i, sent_i = line_sum(keep_i, other_i, near_i)
    far_i = far_hops(sent_i, n, (1, 2, 3))
    far_u.update(far_hops(sent_u, n, (3,)))
    down_own, up_own, in_own = last_sum(base_d, far_d), last_sum(base_u, far_u), last_sum(base_i, far_i)

    gq_w, gk_w, gv_w = (in_own[own * i : own * (i + 1)] for i in range(3))
    gqb, gvb, gob, gag, gas, gdb, gfg, gfs = (in_own[3 * own + i, :own] for i in range(8))
    gub = in_own[3 * own, 128 : 128 + wide]
    gup = jnp.concatenate([up_own[own * i : own * (i + 1)] for i in range(wide // own)], axis=1)
    go_w = up_own[wide : wide + own]
    return (
        layer_out, in_grad, gq_w, gqb, gk_w, gv_w, gvb, go_w, gob, gag, gas, gup, gub, down_own, gdb, gfg, gfs,
    )


def plain_shards(
    tokens, cotangent, lengths, span_start, span_end,
    query_weight, query_bias, key_weight, value_weight, value_bias, out_weight, out_bias,
    attn_gain, attn_shift, up_weight, up_bias, down_weight, down_bias, ffn_gain, ffn_shift,
):
    own = query_weight.shape[0]
    parts = D // own
    ff = up_weight.shape[1]
    wide = own * ff // D
    vectors = (query_bias, value_bias, out_bias, attn_gain, attn_shift, down_bias, ffn_gain, ffn_shift, up_bias)
    packed = jnp.concatenate(vectors)
    packed = jnp.pad(packed, (0, D - packed.shape[0])).reshape(1, D)
    sent = jnp.concatenate(
        [query_weight, key_weight, value_weight, out_weight, chunked(up_weight), down_weight, packed], axis=0
    )
    held = lax.all_gather(sent, "fsdp", axis=0, tiled=False)
    wq, wk, wv, wo = (held[:, own * i : own * (i + 1)].reshape(D, D) for i in range(4))
    wu = jnp.concatenate(
        [held[:, own * (4 + i) : own * (5 + i)].reshape(D, D) for i in range(ff // D)], axis=1
    )
    wd = held[:, 4 * own + wide : 4 * own + 2 * wide].reshape(ff, D)
    small = held[:, -1].astype(F32)
    table = jnp.concatenate([small[:, own * i : own * (i + 1)].reshape(1, D) for i in range(8)], axis=0)
    ub = small[:, 8 * own : 8 * own + wide].reshape(1, ff)
    gy = residue_mask(cotangent, span_start, span_end)

    q, k, v, mixed, lse = attn_fwd(tokens, wq, wk, wv, table[0:1], table[1:2], lengths)
    layer_out, hidden, gffn, low, gpre, gattn, g1, gmixed, gtable, gub = ffn_both(
        mixed, tokens, gy, (wo, wu, wd), table, ub
    )
    down_grad = wgrad(hidden, gffn)
    up_grad = wgrad(low, gpre)
    ffn_parts = jnp.concatenate([up_grad.reshape(parts, wide, D), down_grad.reshape(parts, wide, D)], axis=1)
    ffn_own = lax.psum_scatter(ffn_parts, "fsdp", scatter_dimension=0, tiled=False).astype(F32)
    out_grad = wgrad(mixed, gattn)
    gq, gk, gv, gqb, gvb = attn_bwd(q, k, v, gmixed, lse, lengths)
    query_grad, key_grad, value_grad = wgrad3(tokens, gq, gk, gv)
    vec = [gqb, gvb] + [gtable[i : i + 1] for i in range(2, 8)]
    vec = jnp.concatenate([p.reshape(parts, own) for p in vec] + [gub.reshape(parts, wide)], axis=1)
    vec = jnp.pad(vec.astype(BF16), ((0, 0), (0, D - vec.shape[1]))).reshape(parts, 1, D)
    attn_parts = jnp.concatenate(
        [g.reshape(parts, own, D) for g in (query_grad, key_grad, value_grad, out_grad)] + [vec], axis=1
    )
    attn_own = lax.psum_scatter(attn_parts, "fsdp", scatter_dimension=0, tiled=False).astype(F32)
    in_grad = input_grad(g1, gq, gk, gv, wq, wk, wv)

    gq_w, gk_w, gv_w, go_w = (attn_own[own * i : own * (i + 1)] for i in range(4))
    vec = attn_own[-1]
    gqb, gvb, gob, gag, gas, gdb, gfg, gfs = (vec[own * i : own * (i + 1)] for i in range(8))
    gub = vec[8 * own : 8 * own + wide]
    gup = ffn_own[:wide].reshape(own, ff)
    gdown = ffn_own[wide:]
    return (
        layer_out, in_grad, gq_w, gqb, gk_w, gv_w, gvb, go_w, gob, gag, gas, gup, gub, gdown, gdb, gfg, gfs,
    )


def solution(mesh):
    two, one = P("fsdp", None), P("fsdp")
    n = mesh.shape["fsdp"]
    whole_tiles = n % 8 == 0 and n // 8 == 4 and (D // n) % 8 == 0
    return jax.shard_map(
        functools.partial(fast_shards, n) if whole_tiles else plain_shards,
        mesh=mesh,
        in_specs=(two, two, one, two, two, two, one, two, two, one, two, one, one, one, two, one, two, one, one, one),
        out_specs=(two, two, two, one, two, two, one, two, one, one, one, two, one, two, one, one, one),
        check_vma=False,
    )
```

```python
import functools
import jax
import jax.numpy as jnp
from jax import lax
from jax.sharding import PartitionSpec as P
from jax.experimental import pallas as pl
from jax.experimental.pallas import tpu as pltpu

D = 768
HEADS = 12
HEAD = 64
epsilon = 1e-05
masked_score = -1000000000.0
F32 = jnp.float32
BF16 = jnp.bfloat16
WAIT = 1 << 40


def dot(left, right):
    return lax.dot_general(left, right, (((1,), (0,)), ((), ())), preferred_element_type=F32)


def dot_rt(left, right):
    return lax.dot_general(left, right, (((1,), (1,)), ((), ())), preferred_element_type=F32)


def dot_lt(left, right):
    return lax.dot_general(left, right, (((0,), (0,)), ((), ())), preferred_element_type=F32)


def call(body, grid, in_specs, out_specs, out_shape, scratch=(), flops=0, moved=0, vmem=60, aliases={}, weight=0):
    return pl.pallas_call(
        body,
        grid_spec=pltpu.PrefetchScalarGridSpec(
            num_scalar_prefetch=0, grid=grid, in_specs=in_specs, out_specs=out_specs, scratch_shapes=scratch
        ),
        out_shape=out_shape,
        input_output_aliases=aliases,
        compiler_params=pltpu.CompilerParams(vmem_limit_bytes=vmem * 1024 * 1024),
        cost_estimate=pl.CostEstimate(flops=weight, bytes_accessed=weight // 64, transcendentals=0),
    )


def shaped(shape, dtype):
    return jax.ShapeDtypeStruct(shape, dtype)


def half_mask(dtype, scale=1.0):
    lane = lax.broadcasted_iota(jnp.int32, (1, 128), 1)
    low = jnp.where(lane < HEAD, scale, 0.0).astype(dtype)
    high = jnp.where(lane < HEAD, 0.0, scale).astype(dtype)
    return low, high


def attn_fwd_body(start, len_ref, x_ref, wq_ref, wk_ref, wv_ref, table_ref, *rest):
    q_ref, k_ref, v_ref, mix_ref, lse_ref = rest[-5:]
    x = x_ref[...]
    length = x.shape[0]
    q_ref[...] = (dot(x, wq_ref[...]) + table_ref[0:1, :]).astype(BF16)
    k_ref[...] = dot(x, wk_ref[...]).astype(BF16)
    v_ref[...] = (dot(x, wv_ref[...]) + table_ref[1:2, :]).astype(BF16)
    valid = lax.broadcasted_iota(jnp.int32, (1, length), 1) < len_ref[pl.program_id(0) + start]
    masks = half_mask(BF16, 0.125)
    lane = lax.broadcasted_iota(jnp.int32, (1, 128), 1)
    lses = jnp.zeros((length, 128), F32)
    for p in range(HEADS // 2):
        cols = slice(128 * p, 128 * p + 128)
        qp, kp, vp = q_ref[:, cols], k_ref[:, cols], v_ref[:, cols]
        outs = []
        for t in range(2):
            s = dot_rt(qp * masks[t], kp)
            s = jnp.where(valid, s, masked_score)
            m = jnp.max(s, axis=1, keepdims=True)
            e = jnp.exp(s - m)
            total = jnp.sum(e, axis=1, keepdims=True)
            pr = (e * (1.0 / total)).astype(BF16)
            outs.append(dot(pr, vp))
            lses = jnp.where(lane == 2 * p + t, m + jnp.log(total), lses)
        mix_ref[:, cols] = jnp.where(lane < HEAD, outs[0], outs[1]).astype(BF16)
    lse_ref[...] = lses


def attn_fwd(x, wq, wk, wv, table, lengths, start=0, stop=None, before=()):
    rows = x.shape[0]
    n = lengths.shape[0]
    stop = n if stop is None else stop
    length = rows // n
    tile = pl.BlockSpec((length, D), lambda c: (c + start, 0))
    full = pl.BlockSpec((D, D), lambda c: (0, 0))
    eight = pl.BlockSpec((8, D), lambda c: (0, 0))
    act = shaped((rows, D), BF16)
    return call(
        functools.partial(attn_fwd_body, start), (stop - start,),
        [pl.BlockSpec(memory_space=pltpu.SMEM), tile, full, full, full, eight] + [pl.BlockSpec(memory_space=pl.ANY)] * len(before),
        [tile, tile, tile, tile, pl.BlockSpec((length, 128), lambda c: (c + start, 0))],
        [act, act, act, act, shaped((rows, 128), F32)],
        flops=2 * rows * D * D * 3 + 4 * rows * length * D * 4, moved=rows * D * 10 + 6 * D * D,
        aliases={6 + i: i for i in range(5)} if before else {},
    )(lengths, x, wq, wk, wv, table, *before)


def attn_bwd_body(start, len_ref, q_ref, k_ref, v_ref, gm_ref, lse_ref, *rest):
    gq_ref, gk_ref, gv_ref, gbq_ref, gbv_ref = rest[-5:]
    c = pl.program_id(0)
    length = q_ref.shape[0]
    valid = lax.broadcasted_iota(jnp.int32, (1, length), 1) < len_ref[c + start]
    masks = half_mask(BF16)
    scaled = half_mask(BF16, 0.125)

    @pl.when(c == 0)
    def _():
        gbq_ref[...] = rest[3][...] if start else jnp.zeros_like(gbq_ref)
        gbv_ref[...] = rest[4][...] if start else jnp.zeros_like(gbv_ref)

    for p in range(HEADS // 2):
        cols = slice(128 * p, 128 * p + 128)
        qp, kp, vp, gm = q_ref[:, cols], k_ref[:, cols], v_ref[:, cols], gm_ref[:, cols]
        gq, gk, gv = 0.0, 0.0, 0.0
        for t in range(2):
            h = 2 * p + t
            qt = qp * scaled[t]
            kt = kp * scaled[t]
            gt = gm * masks[t]
            s = dot_rt(qt, kp)
            s = jnp.where(valid, s, masked_score)
            pf = jnp.exp(s - lse_ref[:, h : h + 1])
            gp = dot_rt(gt, vp)
            gs = pf * (gp - jnp.sum(pf * gp, axis=1, keepdims=True))
            gs = gs.astype(BF16)
            gv = gv + dot_lt(pf.astype(BF16), gt)
            gq = gq + dot(gs, kt)
            gk = gk + dot_lt(gs, qt)
        gq, gk, gv = gq.astype(BF16), gk.astype(BF16), gv.astype(BF16)
        gq_ref[:, cols] = gq
        gk_ref[:, cols] = gk
        gv_ref[:, cols] = gv
        gbq_ref[:, cols] += jnp.sum(gq.astype(F32), axis=0, keepdims=True)
        gbv_ref[:, cols] += jnp.sum(gv.astype(F32), axis=0, keepdims=True)


def attn_bwd(q, k, v, gm, lse, lengths, start=0, stop=None, before=(), weight=0):
    rows = q.shape[0]
    n = lengths.shape[0]
    stop = n if stop is None else stop
    length = rows // n
    tile = pl.BlockSpec((length, D), lambda c: (c + start, 0))
    one = pl.BlockSpec((1, D), lambda c: (0, 0))
    act = shaped((rows, D), BF16)
    whole = pl.BlockSpec(memory_space=pl.ANY)
    return call(
        functools.partial(attn_bwd_body, start), (stop - start,),
        [pl.BlockSpec(memory_space=pltpu.SMEM), tile, tile, tile, tile, pl.BlockSpec((length, 128), lambda c: (c + start, 0))]
        + ([whole, whole, whole, one, one] if before else []),
        [tile, tile, tile, one, one],
        [act, act, act, shaped((1, D), F32), shaped((1, D), F32)],
        flops=2 * (stop - start) * length * length * D * 5 * 4, moved=(stop - start) * length * D * 14,
        aliases={6: 0, 7: 1, 8: 2} if before else {}, weight=weight,
    )(lengths, q, k, v, gm, lse, *before)


def mean(v):
    return jnp.sum(v, axis=-1, keepdims=True) * (1.0 / D)


def normalize(values):
    center = values - mean(values)
    scale = lax.rsqrt(mean(center * center) + epsilon)
    return center * scale, scale


def norm_back(incoming, normed, scale, gain):
    weighted = incoming * gain
    return scale * (weighted - mean(weighted) - normed * mean(weighted * normed))


def colsum(v):
    return jnp.sum(v, axis=0, keepdims=True)


def gelu_parts(pre):
    cdf = 0.5 + 0.5 * lax.erf(pre * 0.7071067811865476)
    pdf = 0.3989422804014327 * jnp.exp(-0.5 * pre * pre)
    return pre * cdf, cdf + pre * pdf


def wgrad_body(l_ref, r_ref, o_ref):
    o_ref[...] = dot_lt(l_ref[...], r_ref[...]).astype(o_ref.dtype)


def wgrad(left, right, tile_m=768, dtype=BF16):
    rows, m = left.shape
    n = right.shape[1]
    tn = min(n, 768)
    return call(
        wgrad_body, (n // tn, m // tile_m),
        [pl.BlockSpec((rows, tile_m), lambda j, i: (0, i)), pl.BlockSpec((rows, tn), lambda j, i: (0, j))],
        pl.BlockSpec((tile_m, tn), lambda j, i: (i, j)),
        shaped((m, n), dtype),
        flops=2 * rows * m * n, moved=2 * (rows * (m + n) + m * n),
    )(left, right)

def tie(*values):
    return lax.optimization_barrier(values)


def place():
    idx = lax.axis_index("fsdp")
    return idx % 2, (idx // 2) % 4, idx // 8

def swap(n, bits):
    return [(i, i ^ bits) for i in range(n)]

def shift(n, k):
    return [(i, (i + 8 * k) % n) for i in range(n)]

def hop(value, pairs):
    return lax.ppermute(value, "fsdp", pairs)


def join_body(*refs):
    at = 0
    for ref in refs[:-1]:
        refs[-1][at : at + ref.shape[0]] = ref[...]
        at += ref.shape[0]


def join(*parts):
    parts = [p if p.ndim == 3 else p[None] for p in parts]
    full = lambda a: pl.BlockSpec(a.shape, lambda i: (0, 0, 0))
    out = shaped((sum(p.shape[0] for p in parts),) + parts[0].shape[1:], BF16)
    return call(join_body, (1,), [full(p) for p in parts], full(out), out)(*parts)


def gather_all(first, second, n, spare, steps):
    work, given = spare
    across = lambda part: hop(part, swap(n, 1))
    f1, f2, f3 = (hop(first, shift(n, k)) for k in (1, 2, 3))
    x0, y0 = (hop(second, swap(n, b)) for b in (2, 4))
    line = jnp.stack([first, f1, f2, f3])
    line, second, x0, y0 = tie(line, second, x0, y0)
    near = [hop(line, swap(n, b)) for b in (2, 4, 6)]
    z1, z3 = (hop(second, shift(n, k)) for k in (1, 3))
    near, second, z1, z3, given = tie(near, second, z1, z3, given)
    mine = jnp.concatenate([line, *near])
    other = across(mine)
    pair = jnp.stack([z1, z3])
    d0, z2 = hop(second, swap(n, 6)), hop(second, shift(n, 2))
    x13, y13 = (hop(pair, swap(n, b)) for b in (2, 4))
    other, begun = tie(other, jnp.stack([second, x0, y0, z1, z3]))
    begun_other = across(begun)
    held = steps[1](steps[0](mine, other))
    held, d0, z2, x13, y13, begun_other, done = tie(held, d0, z2, x13, y13, begun_other, work(given))
    middle = jnp.concatenate([d0[None], z2[None], x13, y13])
    middle_other = across(middle)
    last = [hop(z2, swap(n, b)) for b in (2, 4, 6)] + [hop(d0, shift(n, k)) for k in (1, 3)]
    held, middle_other = tie(held, middle_other)
    held, last = tie(steps[2](held), last)
    last = [p[None] for p in last]
    return done, held, [begun, middle, *last], [begun_other, middle_other, *(across(p) for p in last)]


def first_sources():
    return [(d, k) for d in range(4) for k in range(4)]


def second_sources():
    begun = [(0, 0), (1, 0), (2, 0), (0, 1), (0, 3)]
    middle = [(3, 0), (0, 2), (1, 1), (1, 3), (2, 1), (2, 3)]
    last = [[(1, 2)], [(2, 2)], [(3, 2)], [(3, 1)], [(3, 3)]]
    return [(p, i, *at) for p, part in enumerate([begun, middle] + last) for i, at in enumerate(part)]


def assemble_body(own, at_ref, mine_ref, other_ref, wq_ref, wk_ref, wv_ref, table_ref, ub_ref):
    core, fast, slow = at_ref[0], at_ref[1], at_ref[2]
    table = jnp.zeros((8, D), F32)
    ub = jnp.zeros((1, ub_ref.shape[1]), F32)
    for i, (dxy, dz) in enumerate(first_sources()):
        chip = ((slow - dz) % 4) * 4 + (fast ^ dxy)
        a, b = mine_ref[i], other_ref[i]
        low, high = jnp.where(core == 0, a, b), jnp.where(core == 0, b, a)
        for m, ref in enumerate((wq_ref, wk_ref, wv_ref)):
            rows = slice(own * m, own * m + own)
            ref[chip] = jnp.concatenate([low[rows], high[rows]], axis=0)
        for side, got in ((0, low), (1, high)):
            tail = got[3 * own :].astype(F32)
            spot = chip * 2 + side
            lane = lax.broadcasted_iota(jnp.int32, (1, D), 1)
            table = table + pltpu.roll(jnp.where(lane < own, tail, 0.0), spot * own, 1)
            wide = tail[0:1, 128:256]
            wide = jnp.concatenate([wide, jnp.zeros((1, ub_ref.shape[1] - 128), F32)], axis=1)
            ub = ub + pltpu.roll(wide, spot * 4 * own, 1)
    table_ref[...] = table
    ub_ref[...] = ub


def assemble(at, mine, other, own, n):
    full = lambda a: pl.BlockSpec(a.shape, lambda i: (0,) * a.ndim)
    arrays = [mine, other]
    w = shaped((n // 2, 2 * own, D), BF16)
    outs = [w, w, w, shaped((8, D), F32), shaped((1, 4 * D), F32)]
    wq, wk, wv, table, ub = call(
        functools.partial(assemble_body, own), (1,),
        [pl.BlockSpec(memory_space=pltpu.SMEM)] + [full(a) for a in arrays],
        [full(a) for a in outs], outs, moved=7 * D * D * 2,
    )(at, *arrays)
    return wq.reshape(D, D), wk.reshape(D, D), wv.reshape(D, D), table, ub


def pack_small(vectors, wide):
    total = jnp.pad(wide[None, :], ((0, 7), (128, D - 128 - wide.shape[0])))
    for i, v in enumerate(vectors):
        total = total + jnp.pad(v[None, :], ((i, 7 - i), (0, D - v.shape[0])))
    return total


def ffn_parts_body(chunk, own, at_ref, mix_ref, x_ref, gy_ref, *rest):
    mine, other, (small_ref, ub_ref) = rest[:7], rest[7:14], rest[14:16]
    outs, (dg_ref, wo_ref, wu_ref, wd_ref) = rest[16:-4], rest[-4:]
    wide = 4 * own

    @pl.when(pl.program_id(0) == 0)
    def _():
        core, fast, slow = at_ref[0], at_ref[1], at_ref[2]
        for part, i, dxy, dz in second_sources():
            chip = ((slow - dz) % 4) * 4 + (fast ^ dxy)
            a, b = mine[part][i], other[part][i]
            low, high = jnp.where(core == 0, a, b), jnp.where(core == 0, b, a)
            at = pl.ds(pl.multiple_of(2 * wide * chip, 16), wide)
            wd_ref[at, :] = low[:wide]
            at = pl.ds(pl.multiple_of(2 * wide * chip + wide, 16), wide)
            wd_ref[at, :] = high[:wide]
            at = pl.ds(pl.multiple_of(2 * own * chip, 16), 2 * own)
            for j in range(5):
                rows = slice(wide + own * j, wide + own * j + own)
                both = jnp.concatenate([low[rows], high[rows]], axis=0)
                if j < 4:
                    wu_ref[at, D * j : D * j + D] = both
                else:
                    wo_ref[at, :] = both

    ffn_steps(chunk, mix_ref, x_ref, gy_ref, wo_ref, wu_ref, wd_ref, small_ref, ub_ref, *outs, dg_ref)


def ffn_steps(chunk, mix_ref, x_ref, gy_ref, wo_ref, wu_ref, wd_ref, small_ref, ub_ref,
              out_ref, hid_ref, gffn_ref, low_ref, gpre_ref, gattn_ref, g1_ref, gmix_ref, gsmall_ref, gub_ref, dg_ref):
    i = pl.program_id(0)
    bo, again, ashift, bd, fgain, fshift = (small_ref[j : j + 1, :] for j in range(2, 8))
    ff = wu_ref.shape[1]

    @pl.when(i == 0)
    def _():
        gsmall_ref[...] = jnp.zeros_like(gsmall_ref)
        gub_ref[...] = jnp.zeros_like(gub_ref)

    attn = dot(mix_ref[...], wo_ref[...]) + bo
    xhat1, rs1 = normalize(x_ref[...].astype(F32) + attn)
    first = xhat1 * again + ashift
    low = first.astype(BF16)
    low_ref[...] = low
    ffn = 0.0
    for j in range(ff // chunk):
        cols = slice(j * chunk, (j + 1) * chunk)
        pre = dot(low, wu_ref[:, cols]) + ub_ref[:, cols]
        hid, dg = gelu_parts(pre)
        hid = hid.astype(BF16)
        hid_ref[:, cols] = hid
        dg_ref[:, cols] = dg.astype(dg_ref.dtype)
        ffn = ffn + dot(hid, wd_ref[cols, :])
    xhat2, rs2 = normalize(first + ffn + bd)
    out_ref[...] = (xhat2 * fgain + fshift).astype(BF16)
    gy = gy_ref[...].astype(F32)
    g2 = norm_back(gy, xhat2, rs2, fgain)
    gffn = g2.astype(BF16)
    gffn_ref[...] = gffn
    gsmall_ref[5:6, :] += colsum(gffn.astype(F32))
    gsmall_ref[6:7, :] += colsum(gy * xhat2)
    gsmall_ref[7:8, :] += colsum(gy)
    gfirst = g2
    for j in range(ff // chunk):
        cols = slice(j * chunk, (j + 1) * chunk)
        gh = dot_rt(gffn, wd_ref[cols, :])
        gpre = (gh * dg_ref[:, cols].astype(F32)).astype(BF16)
        gpre_ref[:, cols] = gpre
        gub_ref[:, cols] += colsum(gpre.astype(F32))
        gfirst = gfirst + dot_rt(gpre, wu_ref[:, cols])
    g1 = norm_back(gfirst, xhat1, rs1, again)
    gattn = g1.astype(BF16)
    g1_ref[...] = g1
    gattn_ref[...] = gattn
    gsmall_ref[2:3, :] += colsum(gattn.astype(F32))
    gsmall_ref[3:4, :] += colsum(gfirst * xhat1)
    gsmall_ref[4:5, :] += colsum(gfirst)
    gmix_ref[...] = dot_rt(gattn, wo_ref[...]).astype(BF16)


def ffn_full_body(chunk, *refs):
    ffn_steps(chunk, *refs)


def ffn_both(mixed, x, gy, weights, small, ub, at=None, own=0, tile_rows=280, chunk=768):
    rows = x.shape[0]
    ff = ub.shape[1]
    tile = pl.BlockSpec((tile_rows, D), lambda c: (c, 0))
    wide = pl.BlockSpec((tile_rows, ff), lambda c: (c, 0))
    fixed = lambda a: pl.BlockSpec(a.shape, lambda c: (0,) * a.ndim, pipeline_mode=pl.Buffered(1))
    act = shaped((rows, D), BF16)
    big = shaped((rows, ff), BF16)
    scratch = [pltpu.VMEM((tile_rows, ff), F32)]
    body, place_of, specs = functools.partial(ffn_full_body, chunk), [], []
    if at is not None:
        body, place_of, specs = functools.partial(ffn_parts_body, chunk, own), [at], [pl.BlockSpec(memory_space=pltpu.SMEM)]
        scratch += [pltpu.VMEM((D, D), BF16), pltpu.VMEM((D, ff), BF16), pltpu.VMEM((ff, D), BF16)]
    return call(
        body, (rows // tile_rows,),
        specs + [tile, tile, tile] + [fixed(w) for w in weights] + [fixed(small), fixed(ub)],
        [tile, wide, tile, tile, wide, tile, tile, tile, pl.BlockSpec((8, D), lambda c: (0, 0)), pl.BlockSpec((1, ff), lambda c: (0, 0))],
        [act, big, act, act, big, act, shaped((rows, D), F32), act, shaped((8, D), F32), shaped((1, ff), F32)],
        scratch=scratch,
        flops=2 * rows * D * (2 * D + 4 * ff), moved=rows * (D * 20 + ff * 4) + D * (D + 2 * ff) * 2,
    )(*place_of, mixed, x, gy, *weights, small, ub)


def row_block(at_ref, far, own, dxy, dz):
    chip = ((at_ref[2] + dz) % far) * 4 + (at_ref[1] ^ dxy)
    return tuple(2 * chip + side for side in (at_ref[0], 1 - at_ref[0]))


def acc_rows(ref, m, d, own):
    at = pl.ds(pl.multiple_of(own * d, 8), own)
    return ref[at, :] if m is None else ref[m, at, :]


def wgrad_down_body(far, own, at_ref, hid_ref, gffn_ref, *rest):
    outs, acc_ref = rest[:-1], rest[-1]
    acc_ref[...] = dot_lt(hid_ref[...], gffn_ref[...])
    dz = (pl.program_id(0) - at_ref[2]) % far
    for dxy in range(4):
        chip = at_ref[1] ^ dxy
        for out, side in zip(outs, (at_ref[0], 1 - at_ref[0])):
            out[dxy, dz] = acc_rows(acc_ref, None, 2 * chip + side, own).astype(BF16)


def keep_send(*shape):
    out = shaped((4,) + shape, BF16)
    spec = pl.BlockSpec(out.shape, lambda j: (0,) * len(out.shape))
    return [spec, spec], [out, out]


def wgrad_down(at, hidden, gffn, n):
    rows, ff = hidden.shape
    far = n // 8
    own = ff // n
    specs, outs = keep_send(far, own, D)
    return call(
        functools.partial(wgrad_down_body, far, own), (far,),
        [pl.BlockSpec(memory_space=pltpu.SMEM), pl.BlockSpec((rows, ff // far), lambda j: (0, j)), pl.BlockSpec((rows, D), lambda j: (0, 0))],
        specs, outs, scratch=[pltpu.VMEM((ff // far, D), F32)],
        flops=2 * rows * D * ff, moved=2 * (rows * (D + ff) + D * ff),
    )(at, hidden, gffn)


def wgrad_up_body(far, own, at_ref, low_ref, gpre_ref, mix_ref, gattn_ref, *rest):
    outs, acc_ref = rest[:-1], rest[-1]
    j = pl.program_id(0)

    @pl.when(j < 4)
    def _():
        acc_ref[j] = dot_lt(low_ref[...], gpre_ref[...])

    @pl.when(j == 4)
    def _():
        acc_ref[4] = dot_lt(mix_ref[...], gattn_ref[...])
        for dxy in range(4):
            for dz in range(far):
                for k, d in enumerate(row_block(at_ref, far, own, dxy, dz)):
                    value = jnp.concatenate([acc_rows(acc_ref, m, d, own) for m in range(5)], axis=0)
                    outs[k][dxy, dz] = value.astype(BF16)


def wgrad_up(at, low, gpre, mixed, gattn, own, n):
    rows = low.shape[0]
    far = n // 8
    act = pl.BlockSpec((rows, D), lambda j: (0, 0))
    specs, outs = keep_send(far, 5 * own, D)
    return call(
        functools.partial(wgrad_up_body, far, own), (5,),
        [pl.BlockSpec(memory_space=pltpu.SMEM), act, pl.BlockSpec((rows, D), lambda j: (0, jnp.minimum(j, 3))), act, act],
        specs, outs, scratch=[pltpu.VMEM((5, D, D), F32)],
        flops=10 * rows * D * D, moved=2 * (7 * rows * D + 5 * D * D),
    )(at, low, gpre, mixed, gattn)


def wgrad_in_body(far, own, at_ref, x_ref, gq_ref, gk_ref, gv_ref, small_ref, ub_ref, *rest):
    outs, acc_ref = rest[:-1], rest[-1]
    left = x_ref[...]
    for m, ref in enumerate((gq_ref, gk_ref, gv_ref)):
        acc_ref[m] = dot_lt(left, ref[...])
    lane = lax.broadcasted_iota(jnp.int32, (8, D), 1)
    row = lax.broadcasted_iota(jnp.int32, (8, D), 0)
    ff = ub_ref.shape[1]
    wide = ff // (8 * far)
    for dxy in range(4):
        for dz in range(far):
            for k, d in enumerate(row_block(at_ref, far, own, dxy, dz)):
                tail = pltpu.roll(small_ref[...], (D - own * d) % D, 1)
                ub = pltpu.roll(ub_ref[...], (ff + 128 - wide * d) % ff, 1)[:, :D]
                tail = jnp.where(lane < own, tail, 0.0)
                tail = jnp.where((row == 0) & (lane >= 128) & (lane < 128 + wide), ub, tail)
                parts = [acc_rows(acc_ref, m, d, own) for m in range(3)] + [tail]
                outs[k][dxy, dz] = jnp.concatenate(parts, axis=0).astype(BF16)


def wgrad_in(at, x, gq, gk, gv, small, ub, own, n):
    rows = x.shape[0]
    far = n // 8
    full = lambda a: pl.BlockSpec(a.shape, lambda i: (0,) * a.ndim)
    specs, outs = keep_send(far, 3 * own + 8, D)
    return call(
        functools.partial(wgrad_in_body, far, own), (1,),
        [pl.BlockSpec(memory_space=pltpu.SMEM)] + [full(a) for a in (x, gq, gk, gv, small, ub)],
        specs, outs, scratch=[pltpu.VMEM((3, D, D), F32)],
        flops=6 * rows * D * D, moved=2 * (4 * rows * D + 3 * D * D),
    )(at, x, gq, gk, gv, small, ub)


def pair_sum(keep, other, i):
    return keep[i].astype(F32) + other[i].astype(F32)


def near_parts(keep, other):
    return tuple(pair_sum(keep, other, i).astype(BF16) for i in (1, 2, 3))


def near_hops(parts, n):
    return tuple(hop(p, swap(n, 2 * i)) for i, p in enumerate(parts, 1))


def line_body(keep_ref, other_ref, x_ref, y_ref, d_ref, base_ref, *sent):
    total = keep_ref[...].astype(F32) + other_ref[...].astype(F32)
    for ref in (x_ref, y_ref, d_ref):
        total = total + ref[...].astype(F32)
    base_ref[...] = total[0, 0]
    for k, ref in enumerate(sent, 1):
        ref[...] = total[0, k].astype(BF16)


def line_sum(keep, other, near):
    far, rows = keep.shape[1:3]
    block = pl.BlockSpec((1, far, rows, D), lambda i: (0, 0, 0, 0))
    part = pl.BlockSpec((rows, D), lambda i: (0, 0))
    base, *sent = call(
        line_body, (1,), [block] * 5, [part] * far,
        [shaped((rows, D), F32)] + [shaped((rows, D), BF16)] * (far - 1), weight=WAIT,
    )(keep, other, *(p[None] for p in near))
    return base, sent


def far_hops(sent, n, which):
    return {k: hop(sent[k - 1], shift(n, k)) for k in which}


def last_sum(base, far):
    return base + sum(p.astype(F32) for p in far.values())


def wgrad3_body(l_ref, a_ref, b_ref, c_ref, oa_ref, ob_ref, oc_ref):
    left = l_ref[...]
    for r_ref, o_ref in ((a_ref, oa_ref), (b_ref, ob_ref), (c_ref, oc_ref)):
        o_ref[...] = dot_lt(left, r_ref[...]).astype(o_ref.dtype)


def wgrad3(left, a, b, c, tile_m=384, dtype=BF16):
    rows = left.shape[0]
    right = pl.BlockSpec((rows, D), lambda i: (0, 0))
    out = pl.BlockSpec((tile_m, D), lambda i: (i, 0))
    return call(
        wgrad3_body, (D // tile_m,),
        [pl.BlockSpec((rows, tile_m), lambda i: (0, i)), right, right, right],
        [out, out, out],
        [shaped((D, D), dtype)] * 3,
        flops=6 * rows * D * D, moved=2 * (4 * rows * D + 3 * D * D),
    )(left, a, b, c)


def input_grad_body(g1_ref, gq_ref, gk_ref, gv_ref, wq_ref, wk_ref, wv_ref, *rest):
    total = g1_ref[...] + dot_rt(gq_ref[...], wq_ref[...])
    total = total + dot_rt(gk_ref[...], wk_ref[...]) + dot_rt(gv_ref[...], wv_ref[...])
    rest[-1][...] = total.astype(BF16)


def input_grad(g1, gq, gk, gv, wq, wk, wv, start=0, stop=4, before=(), tiles=4):
    rows = g1.shape[0]
    tile = pl.BlockSpec((rows // tiles, D), lambda c: (c + start, 0))
    full = pl.BlockSpec((D, D), lambda c: (0, 0))
    return call(
        input_grad_body, (stop - start,),
        [tile, tile, tile, tile, full, full, full] + [pl.BlockSpec(memory_space=pl.ANY)] * len(before),
        tile, shaped((rows, D), BF16), aliases={7: 0} if before else {},
        flops=6 * rows * D * D, moved=rows * D * 12 + 6 * D * D,
    )(g1, gq, gk, gv, wq, wk, wv, *before)


def residue_mask(cotangent, span_start, span_end):
    chains = span_start.shape[0]
    rows = cotangent.shape[0]
    positions = jnp.arange(rows // chains)
    inside = jnp.any(
        (positions[None, None, :] >= span_start[:, :, None]) & (positions[None, None, :] < span_end[:, :, None]),
        axis=1,
    )
    return jnp.where(inside.reshape(rows, 1), cotangent, jnp.zeros_like(cotangent))


def chunked(weight):
    own = weight.shape[0]
    return weight.reshape(own, -1, D).swapaxes(0, 1).reshape(-1, D)


def fast_shards(
    n, tokens, cotangent, lengths, span_start, span_end,
    query_weight, query_bias, key_weight, value_weight, value_bias, out_weight, out_bias,
    attn_gain, attn_shift, up_weight, up_bias, down_weight, down_bias, ffn_gain, ffn_shift,
):
    own = query_weight.shape[0]
    wide = up_bias.shape[0]
    vectors = (query_bias, value_bias, out_bias, attn_gain, attn_shift, down_bias, ffn_gain, ffn_shift)
    at = jnp.stack(place()).astype(jnp.int32)
    block = jnp.concatenate([query_weight, key_weight, value_weight, pack_small(vectors, up_bias)], axis=0)
    second = jnp.concatenate([down_weight, chunked(up_weight), out_weight], axis=0)
    chains = lengths.shape[0]
    ahead = chains * 3 // 7

    def attend(w, start, stop, before=()):
        return w, attn_fwd(tokens, *w[:4], lengths, start, stop, before)

    gy, ((wq, wk, wv, table, ub), (q, k, v, mixed, lse)), mine, other = gather_all(
        block, second, n,
        (lambda given: residue_mask(*given), (cotangent, span_start, span_end)),
        (
            lambda mine, other: assemble(at, mine, other, own, n),
            lambda w: attend(w, 0, ahead),
            lambda held: attend(held[0], ahead, chains, held[1]),
        ),
    )
    layer_out, hidden, gffn, low, gpre, gattn, g1, gmixed, gtable, gub = ffn_both(
        mixed, tokens, gy, mine + other, table, ub, at, own
    )
    cuts = (0, 1, 4, chains)
    keep_d, send_d = wgrad_down(at, hidden, gffn, n)
    gmixed, keep_d, send_d = tie(gmixed, keep_d, send_d)
    other_d = hop(send_d, swap(n, 1))
    begun = attn_bwd(q, k, v, gmixed, lse, lengths, cuts[0], cuts[1], weight=WAIT)
    begun, other_d = tie(begun, other_d)
    low, begun, parts_d = tie(low, begun, near_parts(keep_d, other_d))
    near_d = near_hops(parts_d, n)
    keep_u, send_u = wgrad_up(at, low, gpre, mixed, gattn, own, n)
    begun, keep_u, send_u = tie(begun, keep_u, send_u)
    other_u = hop(send_u, swap(n, 1))
    begun = attn_bwd(q, k, v, gmixed, lse, lengths, cuts[1], cuts[2], begun)
    begun, near_d = tie(begun, near_d)
    base_d, sent_d = line_sum(keep_d, other_d, near_d)
    base_d, sent_d, other_u = tie(base_d, sent_d, other_u)
    far_d = far_hops(sent_d, n, (1, 3))
    begun, parts_u = tie(begun, near_parts(keep_u, other_u))
    near_u = near_hops(parts_u, n)
    gq, gk, gv, gqb, gvb = attn_bwd(q, k, v, gmixed, lse, lengths, cuts[2], cuts[3], begun)
    gq, far_d, sent_d = tie(gq, far_d, sent_d)
    far_d.update(far_hops(sent_d, n, (2,)))
    gtable = jnp.concatenate([gqb, gvb, gtable[2:]], axis=0)
    keep_i, send_i = wgrad_in(at, tokens, gq, gk, gv, gtable, gub, own, n)
    g1, keep_i, send_i = tie(g1, keep_i, send_i)
    other_i = hop(send_i, swap(n, 1))
    in_grad = input_grad(g1, gq, gk, gv, wq, wk, wv, 0, 2)
    in_grad, near_u, far_d = tie(in_grad, near_u, far_d)
    base_u, sent_u = line_sum(keep_u, other_u, near_u)
    base_u, sent_u, other_i = tie(base_u, sent_u, other_i)
    far_u = far_hops(sent_u, n, (1, 2))
    in_grad, parts_i = tie(in_grad, near_parts(keep_i, other_i))
    near_i = near_hops(parts_i, n)
    in_grad = input_grad(g1, gq, gk, gv, wq, wk, wv, 2, 4, (in_grad,))
    in_grad, near_i, far_u = tie(in_grad, near_i, far_u)
    base_i, sent_i = line_sum(keep_i, other_i, near_i)
    far_i = far_hops(sent_i, n, (1, 2, 3))
    far_u.update(far_hops(sent_u, n, (3,)))
    down_own, up_own, in_own = last_sum(base_d, far_d), last_sum(base_u, far_u), last_sum(base_i, far_i)

    gq_w, gk_w, gv_w = (in_own[own * i : own * (i + 1)] for i in range(3))
    gqb, gvb, gob, gag, gas, gdb, gfg, gfs = (in_own[3 * own + i, :own] for i in range(8))
    gub = in_own[3 * own, 128 : 128 + wide]
    gup = jnp.concatenate([up_own[own * i : own * (i + 1)] for i in range(wide // own)], axis=1)
    go_w = up_own[wide : wide + own]
    return (
        layer_out, in_grad, gq_w, gqb, gk_w, gv_w, gvb, go_w, gob, gag, gas, gup, gub, down_own, gdb, gfg, gfs,
    )


def plain_shards(
    tokens, cotangent, lengths, span_start, span_end,
    query_weight, query_bias, key_weight, value_weight, value_bias, out_weight, out_bias,
    attn_gain, attn_shift, up_weight, up_bias, down_weight, down_bias, ffn_gain, ffn_shift,
):
    own = query_weight.shape[0]
    parts = D // own
    ff = up_weight.shape[1]
    wide = own * ff // D
    vectors = (query_bias, value_bias, out_bias, attn_gain, attn_shift, down_bias, ffn_gain, ffn_shift, up_bias)
    packed = jnp.concatenate(vectors)
    packed = jnp.pad(packed, (0, D - packed.shape[0])).reshape(1, D)
    sent = jnp.concatenate(
        [query_weight, key_weight, value_weight, out_weight, chunked(up_weight), down_weight, packed], axis=0
    )
    held = lax.all_gather(sent, "fsdp", axis=0, tiled=False)
    wq, wk, wv, wo = (held[:, own * i : own * (i + 1)].reshape(D, D) for i in range(4))
    wu = jnp.concatenate(
        [held[:, own * (4 + i) : own * (5 + i)].reshape(D, D) for i in range(ff // D)], axis=1
    )
    wd = held[:, 4 * own + wide : 4 * own + 2 * wide].reshape(ff, D)
    small = held[:, -1].astype(F32)
    table = jnp.concatenate([small[:, own * i : own * (i + 1)].reshape(1, D) for i in range(8)], axis=0)
    ub = small[:, 8 * own : 8 * own + wide].reshape(1, ff)
    gy = residue_mask(cotangent, span_start, span_end)

    q, k, v, mixed, lse = attn_fwd(tokens, wq, wk, wv, table, lengths)
    layer_out, hidden, gffn, low, gpre, gattn, g1, gmixed, gtable, gub = ffn_both(
        mixed, tokens, gy, (wo, wu, wd), table, ub
    )
    down_grad = wgrad(hidden, gffn)
    up_grad = wgrad(low, gpre)
    ffn_parts = jnp.concatenate([up_grad.reshape(parts, wide, D), down_grad.reshape(parts, wide, D)], axis=1)
    ffn_own = lax.psum_scatter(ffn_parts, "fsdp", scatter_dimension=0, tiled=False).astype(F32)
    out_grad = wgrad(mixed, gattn)
    gq, gk, gv, gqb, gvb = attn_bwd(q, k, v, gmixed, lse, lengths)
    query_grad, key_grad, value_grad = wgrad3(tokens, gq, gk, gv)
    vec = [gqb, gvb] + [gtable[i : i + 1] for i in range(2, 8)]
    vec = jnp.concatenate([p.reshape(parts, own) for p in vec] + [gub.reshape(parts, wide)], axis=1)
    vec = jnp.pad(vec.astype(BF16), ((0, 0), (0, D - vec.shape[1]))).reshape(parts, 1, D)
    attn_parts = jnp.concatenate(
        [g.reshape(parts, own, D) for g in (query_grad, key_grad, value_grad, out_grad)] + [vec], axis=1
    )
    attn_own = lax.psum_scatter(attn_parts, "fsdp", scatter_dimension=0, tiled=False).astype(F32)
    in_grad = input_grad(g1, gq, gk, gv, wq, wk, wv)

    gq_w, gk_w, gv_w, go_w = (attn_own[own * i : own * (i + 1)] for i in range(4))
    vec = attn_own[-1]
    gqb, gvb, gob, gag, gas, gdb, gfg, gfs = (vec[own * i : own * (i + 1)] for i in range(8))
    gub = vec[8 * own : 8 * own + wide]
    gup = ffn_own[:wide].reshape(own, ff)
    gdown = ffn_own[wide:]
    return (
        layer_out, in_grad, gq_w, gqb, gk_w, gv_w, gvb, go_w, gob, gag, gas, gup, gub, gdown, gdb, gfg, gfs,
    )


def solution(mesh):
    two, one = P("fsdp", None), P("fsdp")
    n = mesh.shape["fsdp"]
    whole_tiles = n % 8 == 0 and n // 8 == 4 and (D // n) % 8 == 0
    return jax.shard_map(
        functools.partial(fast_shards, n) if whole_tiles else plain_shards,
        mesh=mesh,
        in_specs=(two, two, one, two, two, two, one, two, two, one, two, one, one, one, two, one, two, one, one, one),
        out_specs=(two, two, two, one, two, two, one, two, one, one, one, two, one, two, one, one, one),
        check_vma=False,
    )
```

```python
import functools
import jax
import jax.numpy as jnp
from jax import lax
from jax.sharding import PartitionSpec as P
from jax.experimental import pallas as pl
from jax.experimental.pallas import tpu as pltpu

D = 768
HEADS = 12
HEAD = 64
epsilon = 1e-05
masked_score = -1000000000.0
F32 = jnp.float32
BF16 = jnp.bfloat16
WAIT = 1 << 40


def dot(left, right):
    return lax.dot_general(left, right, (((1,), (0,)), ((), ())), preferred_element_type=F32)


def dot_rt(left, right):
    return lax.dot_general(left, right, (((1,), (1,)), ((), ())), preferred_element_type=F32)


def dot_lt(left, right):
    return lax.dot_general(left, right, (((0,), (0,)), ((), ())), preferred_element_type=F32)


def call(body, grid, in_specs, out_specs, out_shape, scratch=(), flops=0, moved=0, vmem=60, aliases={}, weight=0, prefetch=0):
    return pl.pallas_call(
        body,
        grid_spec=pltpu.PrefetchScalarGridSpec(
            num_scalar_prefetch=prefetch, grid=grid, in_specs=in_specs, out_specs=out_specs, scratch_shapes=scratch
        ),
        out_shape=out_shape,
        input_output_aliases=aliases,
        compiler_params=pltpu.CompilerParams(vmem_limit_bytes=vmem * 1024 * 1024),
        cost_estimate=pl.CostEstimate(flops=weight, bytes_accessed=weight // 64, transcendentals=0),
    )


def shaped(shape, dtype):
    return jax.ShapeDtypeStruct(shape, dtype)


GROUP = 4


def by_head(values, scale=1.0):
    lane = lax.broadcasted_iota(jnp.int32, (1, GROUP * HEAD), 1) // HEAD
    return jnp.concatenate([values * jnp.where(lane == t, scale, 0.0).astype(BF16) for t in range(GROUP)], axis=0)


def own_columns(stacked):
    rows = stacked.shape[0] // GROUP
    lane = lax.broadcasted_iota(jnp.int32, (1, GROUP * HEAD), 1) // HEAD
    out = stacked[:rows]
    for t in range(1, GROUP):
        out = jnp.where(lane == t, stacked[rows * t : rows * (t + 1)], out)
    return out


def attn_fwd_body(start, len_ref, x_ref, wq_ref, wk_ref, wv_ref, table_ref, *rest):
    q_ref, k_ref, v_ref, mix_ref, lse_ref = rest[-5:]
    x = x_ref[...]
    length = x.shape[0]
    q_ref[...] = (dot(x, wq_ref[...]) + table_ref[0:1, :]).astype(BF16)
    k_ref[...] = dot(x, wk_ref[...]).astype(BF16)
    v_ref[...] = (dot(x, wv_ref[...]) + table_ref[1:2, :]).astype(BF16)
    valid = lax.broadcasted_iota(jnp.int32, (length, length), 0) < len_ref[pl.program_id(0) + start]
    for g in range(HEADS // GROUP):
        cols = slice(GROUP * HEAD * g, GROUP * HEAD * (g + 1))
        scores = dot_rt(by_head(k_ref[:, cols], 0.125), q_ref[:, cols])
        probs = []
        for t in range(GROUP):
            s = jnp.where(valid, scores[length * t : length * (t + 1)], masked_score)
            m = jnp.max(s, axis=0, keepdims=True)
            e = jnp.exp(s - m)
            total = jnp.sum(e, axis=0, keepdims=True)
            probs.append((e * (1.0 / total)).astype(BF16))
            lse_ref[0, GROUP * g + t : GROUP * g + t + 1, :] = m + jnp.log(total)
        mix_ref[:, cols] = dot_lt(jnp.concatenate(probs, axis=0), by_head(v_ref[:, cols])).astype(BF16)


def attn_fwd(x, wq, wk, wv, table, lengths, start=0, stop=None, before=()):
    rows = x.shape[0]
    n = lengths.shape[0]
    stop = n if stop is None else stop
    length = rows // n
    tile = pl.BlockSpec((length, D), lambda c: (c + start, 0))
    full = pl.BlockSpec((D, D), lambda c: (0, 0))
    eight = pl.BlockSpec((8, D), lambda c: (0, 0))
    act = shaped((rows, D), BF16)
    return call(
        functools.partial(attn_fwd_body, start), (stop - start,),
        [pl.BlockSpec(memory_space=pltpu.SMEM), tile, full, full, full, eight] + [pl.BlockSpec(memory_space=pl.ANY)] * len(before),
        [tile, tile, tile, tile, pl.BlockSpec((1, HEADS, length), lambda c: (c + start, 0, 0))],
        [act, act, act, act, shaped((n, HEADS, length), F32)],
        flops=2 * rows * D * D * 3 + 4 * rows * length * D * 4, moved=rows * D * 10 + 6 * D * D,
        aliases={6 + i: i for i in range(5)} if before else {},
     vmem=24,)(lengths, x, wq, wk, wv, table, *before)


def attn_bwd_body(start, len_ref, q_ref, k_ref, v_ref, gm_ref, lse_ref, *rest):
    grads_ref, gbq_ref, gbv_ref = rest[-3:]
    c = pl.program_id(0)
    length = q_ref.shape[0]
    valid = lax.broadcasted_iota(jnp.int32, (length, length), 0) < len_ref[c + start]

    @pl.when(c == 0)
    def _():
        gbq_ref[...] = rest[1][...] if start else jnp.zeros_like(gbq_ref)
        gbv_ref[...] = rest[2][...] if start else jnp.zeros_like(gbv_ref)

    for g in range(HEADS // GROUP):
        cols = slice(GROUP * HEAD * g, GROUP * HEAD * (g + 1))
        q, gm = q_ref[:, cols], gm_ref[:, cols]
        keys = by_head(k_ref[:, cols], 0.125)
        scores = dot_rt(keys, q)
        gprobs = dot_rt(by_head(v_ref[:, cols]), gm)
        probs, gscores = [], []
        for t in range(GROUP):
            rows = slice(length * t, length * (t + 1))
            h = GROUP * g + t
            pf = jnp.exp(jnp.where(valid, scores[rows], masked_score) - lse_ref[0, h : h + 1, :])
            gp = gprobs[rows]
            gs = pf * (gp - jnp.sum(pf * gp, axis=0, keepdims=True))
            probs.append(pf.astype(BF16))
            gscores.append(gs.astype(BF16))
        gscores = jnp.concatenate(gscores, axis=0)
        gv = own_columns(dot(jnp.concatenate(probs, axis=0), gm)).astype(BF16)
        gk = (own_columns(dot(gscores, q)) * 0.125).astype(BF16)
        gq = dot_lt(gscores, keys).astype(BF16)
        for m, value in enumerate((gq, gk, gv)):
            grads_ref[:, m * D + cols.start : m * D + cols.stop] = value
        gbq_ref[:, cols] += jnp.sum(gq.astype(F32), axis=0, keepdims=True)
        gbv_ref[:, cols] += jnp.sum(gv.astype(F32), axis=0, keepdims=True)


def attn_bwd(q, k, v, gm, lse, lengths, start=0, stop=None, before=(), weight=0):
    rows = q.shape[0]
    n = lengths.shape[0]
    stop = n if stop is None else stop
    length = rows // n
    tile = pl.BlockSpec((length, D), lambda c: (c + start, 0))
    one = pl.BlockSpec((1, D), lambda c: (0, 0))
    whole = pl.BlockSpec(memory_space=pl.ANY)
    return call(
        functools.partial(attn_bwd_body, start), (stop - start,),
        [pl.BlockSpec(memory_space=pltpu.SMEM), tile, tile, tile, tile, pl.BlockSpec((1, HEADS, length), lambda c: (c + start, 0, 0))]
        + ([whole, one, one] if before else []),
        [pl.BlockSpec((length, 3 * D), lambda c: (c + start, 0)), one, one],
        [shaped((rows, 3 * D), BF16), shaped((1, D), F32), shaped((1, D), F32)],
        flops=2 * (stop - start) * length * length * D * 5 * 4, moved=(stop - start) * length * D * 14,
        aliases={6: 0} if before else {}, weight=weight,
     vmem=20,)(lengths, q, k, v, gm, lse, *before)


def mean(v):
    return jnp.sum(v, axis=-1, keepdims=True) * (1.0 / D)


def normalize(values):
    center = values - mean(values)
    scale = lax.rsqrt(mean(center * center) + epsilon)
    return center * scale, scale


def norm_back(incoming, normed, scale, gain):
    weighted = incoming * gain
    return scale * (weighted - mean(weighted) - normed * mean(weighted * normed))


def colsum(v):
    return jnp.sum(v, axis=0, keepdims=True)


def gelu_parts(pre):
    cdf = 0.5 + 0.5 * lax.erf(pre * 0.7071067811865476)
    pdf = 0.3989422804014327 * jnp.exp(-0.5 * pre * pre)
    return pre * cdf, cdf + pre * pdf


def wgrad_body(l_ref, r_ref, o_ref):
    o_ref[...] = dot_lt(l_ref[...], r_ref[...]).astype(o_ref.dtype)


def wgrad(left, right, tile_m=768, dtype=BF16):
    rows, m = left.shape
    n = right.shape[1]
    tn = min(n, 768)
    return call(
        wgrad_body, (n // tn, m // tile_m),
        [pl.BlockSpec((rows, tile_m), lambda j, i: (0, i)), pl.BlockSpec((rows, tn), lambda j, i: (0, j))],
        pl.BlockSpec((tile_m, tn), lambda j, i: (i, j)),
        shaped((m, n), dtype),
        flops=2 * rows * m * n, moved=2 * (rows * (m + n) + m * n),
    )(left, right)

def tie(*values):
    return lax.optimization_barrier(values)


def place():
    idx = lax.axis_index("fsdp")
    return idx % 2, (idx // 2) % 4, idx // 8

def swap(n, bits):
    return [(i, i ^ bits) for i in range(n)]

def shift(n, k):
    return [(i, (i + 8 * k) % n) for i in range(n)]

def hop(value, pairs):
    return lax.ppermute(value, "fsdp", pairs)


def join_body(*refs):
    at = 0
    for ref in refs[:-1]:
        refs[-1][at : at + ref.shape[0]] = ref[...]
        at += ref.shape[0]


def join(*parts):
    parts = [p if p.ndim == 3 else p[None] for p in parts]
    full = lambda a: pl.BlockSpec(a.shape, lambda i: (0, 0, 0))
    out = shaped((sum(p.shape[0] for p in parts),) + parts[0].shape[1:], BF16)
    return call(join_body, (1,), [full(p) for p in parts], full(out), out, vmem=16)(*parts)


def gather_all(first, second, n, spare, steps):
    work, given = spare
    across = lambda part: hop(part, swap(n, 1))
    f1, f2, f3 = (hop(first, shift(n, k)) for k in (1, 2, 3))
    x0, y0, d0 = (hop(second, swap(n, b)) for b in (2, 4, 6))
    line = jnp.stack([first, f1, f2, f3])
    line, second = tie(line, second)
    near = [hop(line, swap(n, b)) for b in (2, 4, 6)]
    z1, z3 = (hop(second, shift(n, k)) for k in (1, 3))
    near, second, z1, z3, given, x0, y0, d0 = tie(near, second, z1, z3, given, x0, y0, d0)
    mine = jnp.concatenate([line, *near])
    other = across(mine)
    pair = jnp.stack([z1, z3])
    z2 = hop(second, shift(n, 2))
    x13, y13 = (hop(pair, swap(n, b)) for b in (2, 4))
    other, begun = tie(other, join(second, x0, y0, z1, z3))
    begun_other = across(begun)
    held = steps[1](steps[0](mine, other))
    held, d0, z2, x13, y13, begun_other, done = tie(held, d0, z2, x13, y13, begun_other, work(given))
    middle = jnp.concatenate([d0[None], z2[None], x13, y13])
    middle_other = across(middle)
    last = [hop(z2, swap(n, b)) for b in (2, 4, 6)] + [hop(d0, shift(n, k)) for k in (1, 3)]
    held, middle_other = tie(held, middle_other)
    held, last = tie(steps[2](held), last)
    last = [p[None] for p in last]
    return done, held, [begun, middle, *last], [begun_other, middle_other, *(across(p) for p in last)]


def first_sources():
    return [(d, k) for d in range(4) for k in range(4)]


def second_sources():
    begun = [(0, 0), (1, 0), (2, 0), (0, 1), (0, 3)]
    middle = [(3, 0), (0, 2), (1, 1), (1, 3), (2, 1), (2, 3)]
    last = [[(1, 2)], [(2, 2)], [(3, 2)], [(3, 1)], [(3, 3)]]
    return [(p, i, *at) for p, part in enumerate([begun, middle] + last) for i, at in enumerate(part)]


def assemble_body(own, at_ref, mine_ref, other_ref, wq_ref, wk_ref, wv_ref, table_ref, ub_ref):
    core, fast, slow = at_ref[0], at_ref[1], at_ref[2]
    table = jnp.zeros((8, D), F32)
    ub = jnp.zeros((8, D), F32)
    for i, (dxy, dz) in enumerate(first_sources()):
        chip = ((slow - dz) % 4) * 4 + (fast ^ dxy)
        a, b = mine_ref[i], other_ref[i]
        low, high = jnp.where(core == 0, a, b), jnp.where(core == 0, b, a)
        for m, ref in enumerate((wq_ref, wk_ref, wv_ref)):
            rows = slice(own * m, own * m + own)
            ref[chip] = jnp.concatenate([low[rows], high[rows]], axis=0)
        for side, got in ((0, low), (1, high)):
            tail = got[3 * own :].astype(F32)
            spot = chip * 2 + side
            lane = lax.broadcasted_iota(jnp.int32, (8, D), 1)
            row = lax.broadcasted_iota(jnp.int32, (8, D), 0)
            table = table + pltpu.roll(jnp.where(lane < own, tail, 0.0), spot * own, 1)
            wide = jnp.where((lane >= 128) & (lane < 128 + 4 * own) & (row == spot // 8), tail[0:1], 0.0)
            ub = ub + pltpu.roll(wide, (D - 128 + spot % 8 * 4 * own) % D, 1)
    table_ref[...] = table
    ub_ref[...] = ub[:4]


def assemble(at, mine, other, own, n):
    full = lambda a: pl.BlockSpec(a.shape, lambda i: (0,) * a.ndim)
    arrays = [mine, other]
    w = shaped((n // 2, 2 * own, D), BF16)
    outs = [w, w, w, shaped((8, D), F32), shaped((4, D), F32)]
    wq, wk, wv, table, ub = call(
        functools.partial(assemble_body, own), (1,),
        [pl.BlockSpec(memory_space=pltpu.SMEM)] + [full(a) for a in arrays],
        [full(a) for a in outs], outs, moved=7 * D * D * 2,
     vmem=28,)(at, *arrays)
    return wq.reshape(D, D), wk.reshape(D, D), wv.reshape(D, D), table, ub


def pack_small(vectors, wide):
    total = jnp.pad(wide[None, :], ((0, 7), (128, D - 128 - wide.shape[0])))
    for i, v in enumerate(vectors):
        total = total + jnp.pad(v[None, :], ((i, 7 - i), (0, D - v.shape[0])))
    return total


def ffn_parts_body(chunk, own, at_ref, mix_ref, x_ref, gy_ref, *rest):
    mine, other, (small_ref, ub_ref) = rest[:7], rest[7:14], rest[14:16]
    outs, (dg_ref, wo_ref, wu_ref, wd_ref) = rest[16:-4], rest[-4:]
    wide = 4 * own

    @pl.when(pl.program_id(0) == 0)
    def _():
        core, fast, slow = at_ref[0], at_ref[1], at_ref[2]
        for part, i, dxy, dz in second_sources():
            chip = ((slow - dz) % 4) * 4 + (fast ^ dxy)
            a, b = mine[part][i], other[part][i]
            low, high = jnp.where(core == 0, a, b), jnp.where(core == 0, b, a)
            at = pl.ds(pl.multiple_of(2 * wide * chip, 16), wide)
            wd_ref[at, :] = low[:wide]
            at = pl.ds(pl.multiple_of(2 * wide * chip + wide, 16), wide)
            wd_ref[at, :] = high[:wide]
            at = pl.ds(pl.multiple_of(2 * own * chip, 16), 2 * own)
            for j in range(5):
                rows = slice(wide + own * j, wide + own * j + own)
                both = jnp.concatenate([low[rows], high[rows]], axis=0)
                if j < 4:
                    wu_ref[at, D * j : D * j + D] = both
                else:
                    wo_ref[at, :] = both

    ffn_steps(chunk, mix_ref, x_ref, gy_ref, wo_ref, wu_ref, wd_ref, small_ref, ub_ref, *outs, dg_ref)


def ffn_steps(chunk, mix_ref, x_ref, gy_ref, wo_ref, wu_ref, wd_ref, small_ref, ub_ref,
              out_ref, hid_ref, gffn_ref, low_ref, gpre_ref, gattn_ref, g1_ref, gmix_ref, gsmall_ref, gub_ref, dg_ref):
    i = pl.program_id(0)
    bo, again, ashift, bd, fgain, fshift = (small_ref[j : j + 1, :] for j in range(2, 8))
    ff = wu_ref.shape[1]

    @pl.when(i == 0)
    def _():
        gsmall_ref[...] = jnp.zeros_like(gsmall_ref)
        gub_ref[...] = jnp.zeros_like(gub_ref)

    attn = dot(mix_ref[...], wo_ref[...]) + bo
    xhat1, rs1 = normalize(x_ref[...].astype(F32) + attn)
    first = xhat1 * again + ashift
    low = first.astype(BF16)
    low_ref[...] = low
    ffn = 0.0
    for j in range(ff // chunk):
        cols = slice(j * chunk, (j + 1) * chunk)
        pre = dot(low, wu_ref[:, cols]) + ub_ref[j : j + 1, :]
        hid, dg = gelu_parts(pre)
        hid = hid.astype(BF16)
        hid_ref[:, cols] = hid
        dg_ref[:, cols] = dg.astype(dg_ref.dtype)
        ffn = ffn + dot(hid, wd_ref[cols, :])
    xhat2, rs2 = normalize(first + ffn + bd)
    out_ref[...] = (xhat2 * fgain + fshift).astype(BF16)
    gy = gy_ref[...].astype(F32)
    g2 = norm_back(gy, xhat2, rs2, fgain)
    gffn = g2.astype(BF16)
    gffn_ref[...] = gffn
    gsmall_ref[5:6, :] += colsum(gffn.astype(F32))
    gsmall_ref[6:7, :] += colsum(gy * xhat2)
    gsmall_ref[7:8, :] += colsum(gy)
    gfirst = g2
    for j in range(ff // chunk):
        cols = slice(j * chunk, (j + 1) * chunk)
        gh = dot_rt(gffn, wd_ref[cols, :])
        gpre = (gh * dg_ref[:, cols].astype(F32)).astype(BF16)
        gpre_ref[:, cols] = gpre
        gub_ref[:, cols] += colsum(gpre.astype(F32))
        gfirst = gfirst + dot_rt(gpre, wu_ref[:, cols])
    g1 = norm_back(gfirst, xhat1, rs1, again)
    gattn = g1.astype(BF16)
    g1_ref[...] = g1
    gattn_ref[...] = gattn
    gsmall_ref[2:3, :] += colsum(gattn.astype(F32))
    gsmall_ref[3:4, :] += colsum(gfirst * xhat1)
    gsmall_ref[4:5, :] += colsum(gfirst)
    gmix_ref[...] = dot_rt(gattn, wo_ref[...]).astype(BF16)


def ffn_full_body(chunk, *refs):
    ffn_steps(chunk, *refs)


def ffn_both(mixed, x, gy, weights, small, ub, at=None, own=0, tile_rows=280, chunk=D):
    rows = x.shape[0]
    ff = ub.size
    tile = pl.BlockSpec((tile_rows, D), lambda c: (c, 0))
    wide = pl.BlockSpec((tile_rows, ff), lambda c: (c, 0))
    fixed = lambda a: pl.BlockSpec(a.shape, lambda c: (0,) * a.ndim, pipeline_mode=pl.Buffered(1))
    act = shaped((rows, D), BF16)
    big = shaped((rows, ff), BF16)
    scratch = [pltpu.VMEM((tile_rows, ff), F32)]
    body, place_of, specs = functools.partial(ffn_full_body, chunk), [], []
    if at is not None:
        body, place_of, specs = functools.partial(ffn_parts_body, chunk, own), [at], [pl.BlockSpec(memory_space=pltpu.SMEM)]
        scratch += [pltpu.VMEM((D, D), BF16), pltpu.VMEM((D, ff), BF16), pltpu.VMEM((ff, D), BF16)]
    return call(
        body, (rows // tile_rows,),
        specs + [tile, tile, tile] + [fixed(w) for w in weights] + [fixed(small), fixed(ub)],
        [tile, wide, tile, tile, wide, tile, tile, tile, pl.BlockSpec((8, D), lambda c: (0, 0)), pl.BlockSpec((1, ff), lambda c: (0, 0))],
        [act, big, act, act, big, act, shaped((rows, D), F32), act, shaped((8, D), F32), shaped((1, ff), F32)],
        scratch=scratch,
        flops=2 * rows * D * (2 * D + 4 * ff), moved=rows * (D * 20 + ff * 4) + D * (D + 2 * ff) * 2,
    )(*place_of, mixed, x, gy, *weights, small, ub)


def row_block(at_ref, far, own, dxy, dz):
    chip = ((at_ref[2] + dz) % far) * 4 + (at_ref[1] ^ dxy)
    return tuple(2 * chip + side for side in (at_ref[0], 1 - at_ref[0]))


def acc_rows(ref, m, d, own):
    at = pl.ds(pl.multiple_of(own * d, 8), own)
    return ref[at, :] if m is None else ref[m, at, :]


def keep_send(*shape):
    out = shaped((4,) + shape, BF16)
    spec = pl.BlockSpec(out.shape, lambda j: (0,) * len(out.shape))
    return [spec, spec], [out, out]


def wgrad_down_body(far, own, at_ref, hid_ref, gffn_ref, keep_ref, send_ref, acc_ref):
    acc_ref[...] = dot_lt(hid_ref[...], gffn_ref[...])
    for dxy in range(4):
        chip = at_ref[1] ^ dxy
        for out, side in zip((keep_ref, send_ref), (at_ref[0], 1 - at_ref[0])):
            out[dxy, 0] = acc_rows(acc_ref, None, 2 * chip + side, own).astype(BF16)


def wgrad_down(at, hidden, gffn, n):
    rows, ff = hidden.shape
    far = n // 8
    own = ff // n
    out = shaped((4, far, own, D), BF16)
    spec = pl.BlockSpec((4, 1, own, D), lambda j, at_ref: (0, (j + far - at_ref[2]) % far, 0, 0))
    return call(
        functools.partial(wgrad_down_body, far, own), (far,),
        [pl.BlockSpec((rows, ff // far), lambda j, at_ref: (0, j)), pl.BlockSpec((rows, D), lambda j, at_ref: (0, 0))],
        [spec, spec], [out, out], scratch=[pltpu.VMEM((ff // far, D), F32)], prefetch=1,
     vmem=60,)(at, hidden, gffn)


def wgrad_up_body(far, own, at_ref, low_ref, gpre_ref, mix_ref, gattn_ref, keep_ref, send_ref, acc_ref):
    j = pl.program_id(0)

    @pl.when(j < 4)
    def _():
        acc_ref[...] = dot_lt(low_ref[...], gpre_ref[...])

    @pl.when(j == 4)
    def _():
        acc_ref[...] = dot_lt(mix_ref[...], gattn_ref[...])

    for dxy in range(4):
        for dz in range(far):
            for out, d in zip((keep_ref, send_ref), row_block(at_ref, far, own, dxy, dz)):
                out[dxy, dz, 0] = acc_rows(acc_ref, None, d, own).astype(BF16)


def wgrad_up(at, low, gpre, mixed, gattn, own, n):
    rows = low.shape[0]
    far = n // 8
    act = pl.BlockSpec((rows, D), lambda j: (0, 0))
    out = shaped((4, far, 5, own, D), BF16)
    spec = pl.BlockSpec((4, far, 1, own, D), lambda j: (0, 0, j, 0, 0))
    got = call(
        functools.partial(wgrad_up_body, far, own), (5,),
        [pl.BlockSpec(memory_space=pltpu.SMEM), act, pl.BlockSpec((rows, D), lambda j: (0, jnp.minimum(j, 3))), act, act],
        [spec, spec], [out, out], scratch=[pltpu.VMEM((D, D), F32)],
     vmem=32,)(at, low, gpre, mixed, gattn)
    return [g.reshape(4, far, 5 * own, D) for g in got]


def wgrad_in_body(far, own, at_ref, x_ref, grad_ref, small_ref, ub_ref, keep_ref, send_ref, acc_ref):
    j = pl.program_id(0)
    acc_ref[j] = dot_lt(x_ref[...], grad_ref[...])

    @pl.when(j == 2)
    def _():
        lane = lax.broadcasted_iota(jnp.int32, (8, D), 1)
        row = lax.broadcasted_iota(jnp.int32, (8, D), 0)
        ff = ub_ref.shape[1]
        wide = ff // (8 * far)
        for dxy in range(4):
            for dz in range(far):
                for out, d in zip((keep_ref, send_ref), row_block(at_ref, far, own, dxy, dz)):
                    tail = pltpu.roll(small_ref[...], (D - own * d) % D, 1)
                    ub = pltpu.roll(ub_ref[...], (ff + 128 - wide * d) % ff, 1)[:, :D]
                    tail = jnp.where(lane < own, tail, 0.0)
                    tail = jnp.where((row == 0) & (lane >= 128) & (lane < 128 + wide), ub, tail)
                    parts = [acc_rows(acc_ref, m, d, own) for m in range(3)] + [tail]
                    out[dxy, dz] = jnp.concatenate(parts, axis=0).astype(BF16)


def wgrad_in(at, x, grads, small, ub, own, n):
    rows = x.shape[0]
    far = n // 8
    full = lambda a: pl.BlockSpec(a.shape, lambda i: (0,) * a.ndim)
    specs, outs = keep_send(far, 3 * own + 8, D)
    return call(
        functools.partial(wgrad_in_body, far, own), (3,),
        [pl.BlockSpec(memory_space=pltpu.SMEM), full(x), pl.BlockSpec((rows, D), lambda j: (0, j)), full(small), full(ub)],
        specs, outs, scratch=[pltpu.VMEM((3, D, D), F32)],
     vmem=36,)(at, x, grads, small, ub)


def pair_sum(keep, other, i):
    return keep[i].astype(F32) + other[i].astype(F32)


def near_parts(keep, other):
    return tuple(pair_sum(keep, other, i).astype(BF16) for i in (1, 2, 3))


def near_hops(parts, n):
    return tuple(hop(p, swap(n, 2 * i)) for i, p in enumerate(parts, 1))


def line_body(keep_ref, other_ref, x_ref, y_ref, d_ref, base_ref, *sent):
    total = keep_ref[...].astype(F32) + other_ref[...].astype(F32)
    for ref in (x_ref, y_ref, d_ref):
        total = total + ref[...].astype(F32)
    base_ref[...] = total[0, 0]
    for k, ref in enumerate(sent, 1):
        ref[...] = total[0, k].astype(BF16)


def line_sum(keep, other, near):
    far, rows = keep.shape[1:3]
    block = pl.BlockSpec((1, far, rows, D), lambda i: (0, 0, 0, 0))
    part = pl.BlockSpec((rows, D), lambda i: (0, 0))
    base, *sent = call(
        line_body, (1,), [block] * 5, [part] * far,
        [shaped((rows, D), F32)] + [shaped((rows, D), BF16)] * (far - 1), weight=WAIT,
     vmem=16,)(keep, other, *(p[None] for p in near))
    return base, sent


def far_hops(sent, n, which):
    return {k: hop(sent[k - 1], shift(n, k)) for k in which}


def last_sum(base, far):
    return base + sum(p.astype(F32) for p in far.values())


def input_grad_body(g1_ref, gq_ref, gk_ref, gv_ref, wq_ref, wk_ref, wv_ref, *rest):
    total = g1_ref[...] + dot_rt(gq_ref[...], wq_ref[...])
    total = total + dot_rt(gk_ref[...], wk_ref[...]) + dot_rt(gv_ref[...], wv_ref[...])
    rest[-1][...] = total.astype(BF16)


def input_grad(g1, grads, wq, wk, wv, start=0, stop=4, before=(), tiles=4):
    rows = g1.shape[0]
    tile = pl.BlockSpec((rows // tiles, D), lambda c: (c + start, 0))
    full = pl.BlockSpec((D, D), lambda c: (0, 0))
    return call(
        input_grad_body, (stop - start,),
        [tile] + [pl.BlockSpec((rows // tiles, D), lambda c, m=m: (c + start, m)) for m in range(3)] + [full, full, full] + [pl.BlockSpec(memory_space=pl.ANY)] * len(before),
        tile, shaped((rows, D), BF16), aliases={7: 0} if before else {},
        flops=6 * rows * D * D, moved=rows * D * 12 + 6 * D * D,
     vmem=24,)(g1, grads, grads, grads, wq, wk, wv, *before)


def residue_mask(cotangent, span_start, span_end):
    chains = span_start.shape[0]
    rows = cotangent.shape[0]
    positions = jnp.arange(rows // chains)
    inside = jnp.any(
        (positions[None, None, :] >= span_start[:, :, None]) & (positions[None, None, :] < span_end[:, :, None]),
        axis=1,
    )
    return jnp.where(inside.reshape(rows, 1), cotangent, jnp.zeros_like(cotangent))


def chunked(weight):
    own = weight.shape[0]
    return weight.reshape(own, -1, D).swapaxes(0, 1).reshape(-1, D)


def fast_shards(
    n, tokens, cotangent, lengths, span_start, span_end,
    query_weight, query_bias, key_weight, value_weight, value_bias, out_weight, out_bias,
    attn_gain, attn_shift, up_weight, up_bias, down_weight, down_bias, ffn_gain, ffn_shift,
):
    own = query_weight.shape[0]
    wide = up_bias.shape[0]
    vectors = (query_bias, value_bias, out_bias, attn_gain, attn_shift, down_bias, ffn_gain, ffn_shift)
    at = jnp.stack(place()).astype(jnp.int32)
    block = jnp.concatenate([query_weight, key_weight, value_weight, pack_small(vectors, up_bias)], axis=0)
    second = jnp.concatenate([down_weight, chunked(up_weight), out_weight], axis=0)
    chains = lengths.shape[0]
    ahead = chains * 3 // 7

    def attend(w, start, stop, before=()):
        return w, attn_fwd(tokens, *w[:4], lengths, start, stop, before)

    gy, ((wq, wk, wv, table, ub), (q, k, v, mixed, lse)), mine, other = gather_all(
        block, second, n,
        (lambda given: residue_mask(*given), (cotangent, span_start, span_end)),
        (
            lambda mine, other: assemble(at, mine, other, own, n),
            lambda w: attend(w, 0, ahead),
            lambda held: attend(held[0], ahead, chains, held[1]),
        ),
    )
    layer_out, hidden, gffn, low, gpre, gattn, g1, gmixed, gtable, gub = ffn_both(
        mixed, tokens, gy, mine + other, table, ub, at, own
    )
    cuts = (0, 1, 4, chains)
    keep_d, send_d = wgrad_down(at, hidden, gffn, n)
    gmixed, keep_d, send_d = tie(gmixed, keep_d, send_d)
    other_d = hop(send_d, swap(n, 1))
    begun = attn_bwd(q, k, v, gmixed, lse, lengths, cuts[0], cuts[1], weight=WAIT)
    begun, other_d = tie(begun, other_d)
    low, begun, parts_d = tie(low, begun, near_parts(keep_d, other_d))
    near_d = near_hops(parts_d, n)
    keep_u, send_u = wgrad_up(at, low, gpre, mixed, gattn, own, n)
    begun, keep_u, send_u = tie(begun, keep_u, send_u)
    other_u = hop(send_u, swap(n, 1))
    begun = attn_bwd(q, k, v, gmixed, lse, lengths, cuts[1], cuts[2], begun)
    begun, near_d = tie(begun, near_d)
    base_d, sent_d = line_sum(keep_d, other_d, near_d)
    base_d, sent_d, other_u = tie(base_d, sent_d, other_u)
    far_d = far_hops(sent_d, n, (1, 3))
    begun, parts_u = tie(begun, near_parts(keep_u, other_u))
    near_u = near_hops(parts_u, n)
    grads, gqb, gvb = attn_bwd(q, k, v, gmixed, lse, lengths, cuts[2], cuts[3], begun)
    grads, far_d, sent_d = tie(grads, far_d, sent_d)
    far_d.update(far_hops(sent_d, n, (2,)))
    gtable = jnp.concatenate([gqb, gvb, gtable[2:]], axis=0)
    keep_i, send_i = wgrad_in(at, tokens, grads, gtable, gub, own, n)
    g1, keep_i, send_i = tie(g1, keep_i, send_i)
    other_i = hop(send_i, swap(n, 1))
    in_grad = input_grad(g1, grads, wq, wk, wv, 0, 2)
    in_grad, near_u, far_d = tie(in_grad, near_u, far_d)
    base_u, sent_u = line_sum(keep_u, other_u, near_u)
    base_u, sent_u, other_i = tie(base_u, sent_u, other_i)
    far_u = far_hops(sent_u, n, (1, 2))
    in_grad, parts_i = tie(in_grad, near_parts(keep_i, other_i))
    near_i = near_hops(parts_i, n)
    in_grad = input_grad(g1, grads, wq, wk, wv, 2, 4, (in_grad,))
    in_grad, near_i, far_u = tie(in_grad, near_i, far_u)
    base_i, sent_i = line_sum(keep_i, other_i, near_i)
    far_i = far_hops(sent_i, n, (1, 2, 3))
    far_u.update(far_hops(sent_u, n, (3,)))
    down_own, up_own, in_own = last_sum(base_d, far_d), last_sum(base_u, far_u), last_sum(base_i, far_i)

    gq_w, gk_w, gv_w = (in_own[own * i : own * (i + 1)] for i in range(3))
    gqb, gvb, gob, gag, gas, gdb, gfg, gfs = (in_own[3 * own + i, :own] for i in range(8))
    gub = in_own[3 * own, 128 : 128 + wide]
    gup = jnp.concatenate([up_own[own * i : own * (i + 1)] for i in range(wide // own)], axis=1)
    go_w = up_own[wide : wide + own]
    return (
        layer_out, in_grad, gq_w, gqb, gk_w, gv_w, gvb, go_w, gob, gag, gas, gup, gub, down_own, gdb, gfg, gfs,
    )


def plain_shards(
    tokens, cotangent, lengths, span_start, span_end,
    query_weight, query_bias, key_weight, value_weight, value_bias, out_weight, out_bias,
    attn_gain, attn_shift, up_weight, up_bias, down_weight, down_bias, ffn_gain, ffn_shift,
):
    own = query_weight.shape[0]
    parts = D // own
    ff = up_weight.shape[1]
    wide = own * ff // D
    vectors = (query_bias, value_bias, out_bias, attn_gain, attn_shift, down_bias, ffn_gain, ffn_shift, up_bias)
    packed = jnp.concatenate(vectors)
    packed = jnp.pad(packed, (0, D - packed.shape[0])).reshape(1, D)
    sent = jnp.concatenate(
        [query_weight, key_weight, value_weight, out_weight, chunked(up_weight), down_weight, packed], axis=0
    )
    held = lax.all_gather(sent, "fsdp", axis=0, tiled=False)
    wq, wk, wv, wo = (held[:, own * i : own * (i + 1)].reshape(D, D) for i in range(4))
    wu = jnp.concatenate(
        [held[:, own * (4 + i) : own * (5 + i)].reshape(D, D) for i in range(ff // D)], axis=1
    )
    wd = held[:, 4 * own + wide : 4 * own + 2 * wide].reshape(ff, D)
    small = held[:, -1].astype(F32)
    table = jnp.concatenate([small[:, own * i : own * (i + 1)].reshape(1, D) for i in range(8)], axis=0)
    ub = small[:, 8 * own : 8 * own + wide].reshape(ff // D, D)
    gy = residue_mask(cotangent, span_start, span_end)

    q, k, v, mixed, lse = attn_fwd(tokens, wq, wk, wv, table, lengths)
    layer_out, hidden, gffn, low, gpre, gattn, g1, gmixed, gtable, gub = ffn_both(
        mixed, tokens, gy, (wo, wu, wd), table, ub
    )
    down_grad = wgrad(hidden, gffn)
    up_grad = wgrad(low, gpre)
    ffn_parts = jnp.concatenate([up_grad.reshape(parts, wide, D), down_grad.reshape(parts, wide, D)], axis=1)
    ffn_own = lax.psum_scatter(ffn_parts, "fsdp", scatter_dimension=0, tiled=False).astype(F32)
    out_grad = wgrad(mixed, gattn)
    grads, gqb, gvb = attn_bwd(q, k, v, gmixed, lse, lengths)
    query_grad, key_grad, value_grad = (wgrad(tokens, grads)[:, D * i : D * (i + 1)] for i in range(3))
    vec = [gqb, gvb] + [gtable[i : i + 1] for i in range(2, 8)]
    vec = jnp.concatenate([p.reshape(parts, own) for p in vec] + [gub.reshape(parts, wide)], axis=1)
    vec = jnp.pad(vec.astype(BF16), ((0, 0), (0, D - vec.shape[1]))).reshape(parts, 1, D)
    attn_parts = jnp.concatenate(
        [g.reshape(parts, own, D) for g in (query_grad, key_grad, value_grad, out_grad)] + [vec], axis=1
    )
    attn_own = lax.psum_scatter(attn_parts, "fsdp", scatter_dimension=0, tiled=False).astype(F32)
    in_grad = input_grad(g1, grads, wq, wk, wv)

    gq_w, gk_w, gv_w, go_w = (attn_own[own * i : own * (i + 1)] for i in range(4))
    vec = attn_own[-1]
    gqb, gvb, gob, gag, gas, gdb, gfg, gfs = (vec[own * i : own * (i + 1)] for i in range(8))
    gub = vec[8 * own : 8 * own + wide]
    gup = ffn_own[:wide].reshape(own, ff)
    gdown = ffn_own[wide:]
    return (
        layer_out, in_grad, gq_w, gqb, gk_w, gv_w, gvb, go_w, gob, gag, gas, gup, gub, gdown, gdb, gfg, gfs,
    )


def solution(mesh):
    two, one = P("fsdp", None), P("fsdp")
    n = mesh.shape["fsdp"]
    whole_tiles = n % 8 == 0 and n // 8 == 4 and (D // n) % 8 == 0
    return jax.shard_map(
        functools.partial(fast_shards, n) if whole_tiles else plain_shards,
        mesh=mesh,
        in_specs=(two, two, one, two, two, two, one, two, two, one, two, one, one, one, two, one, two, one, one, one),
        out_specs=(two, two, two, one, two, two, one, two, one, one, one, two, one, two, one, one, one),
        check_vma=False,
    )
```

```python
import functools
import jax
import jax.numpy as jnp
from jax import lax
from jax.sharding import PartitionSpec as P
from jax.experimental import pallas as pl
from jax.experimental.pallas import tpu as pltpu

D = 768
HEADS = 12
HEAD = 64
epsilon = 1e-05
masked_score = -1000000000.0
F32 = jnp.float32
BF16 = jnp.bfloat16
WAIT = 1 << 40


def dot(left, right):
    return lax.dot_general(left, right, (((1,), (0,)), ((), ())), preferred_element_type=F32)


def dot_rt(left, right):
    return lax.dot_general(left, right, (((1,), (1,)), ((), ())), preferred_element_type=F32)


def dot_lt(left, right):
    return lax.dot_general(left, right, (((0,), (0,)), ((), ())), preferred_element_type=F32)


def call(body, grid, in_specs, out_specs, out_shape, scratch=(), flops=0, moved=0, vmem=60, aliases={}, weight=0, prefetch=0):
    return pl.pallas_call(
        body,
        grid_spec=pltpu.PrefetchScalarGridSpec(
            num_scalar_prefetch=prefetch, grid=grid, in_specs=in_specs, out_specs=out_specs, scratch_shapes=scratch
        ),
        out_shape=out_shape,
        input_output_aliases=aliases,
        compiler_params=pltpu.CompilerParams(vmem_limit_bytes=vmem * 1024 * 1024),
        cost_estimate=pl.CostEstimate(flops=weight, bytes_accessed=weight // 64, transcendentals=0),
    )


def shaped(shape, dtype):
    return jax.ShapeDtypeStruct(shape, dtype)


GROUP = 4


def by_head(values, scale=1.0):
    lane = lax.broadcasted_iota(jnp.int32, (1, GROUP * HEAD), 1) // HEAD
    return jnp.concatenate([values * jnp.where(lane == t, scale, 0.0).astype(BF16) for t in range(GROUP)], axis=0)


def own_columns(stacked):
    rows = stacked.shape[0] // GROUP
    lane = lax.broadcasted_iota(jnp.int32, (1, GROUP * HEAD), 1) // HEAD
    out = stacked[:rows]
    for t in range(1, GROUP):
        out = jnp.where(lane == t, stacked[rows * t : rows * (t + 1)], out)
    return out


def attn_fwd_body(start, len_ref, x_ref, wq_ref, wk_ref, wv_ref, table_ref, *rest):
    q_ref, k_ref, v_ref, mix_ref, lse_ref = rest[-5:]
    x = x_ref[...]
    length = x.shape[0]
    q_ref[...] = (dot(x, wq_ref[...]) + table_ref[0:1, :]).astype(BF16)
    k_ref[...] = dot(x, wk_ref[...]).astype(BF16)
    v_ref[...] = (dot(x, wv_ref[...]) + table_ref[1:2, :]).astype(BF16)
    valid = lax.broadcasted_iota(jnp.int32, (length, length), 0) < len_ref[pl.program_id(0) + start]
    for g in range(HEADS // GROUP):
        cols = slice(GROUP * HEAD * g, GROUP * HEAD * (g + 1))
        scores = dot_rt(by_head(k_ref[:, cols], 0.125), q_ref[:, cols])
        probs = []
        for t in range(GROUP):
            s = jnp.where(valid, scores[length * t : length * (t + 1)], masked_score)
            m = jnp.max(s, axis=0, keepdims=True)
            e = jnp.exp(s - m)
            total = jnp.sum(e, axis=0, keepdims=True)
            probs.append((e * (1.0 / total)).astype(BF16))
            lse_ref[0, GROUP * g + t : GROUP * g + t + 1, :] = m + jnp.log(total)
        mix_ref[:, cols] = dot_lt(jnp.concatenate(probs, axis=0), by_head(v_ref[:, cols])).astype(BF16)


def attn_fwd(x, wq, wk, wv, table, lengths, start=0, stop=None, before=()):
    rows = x.shape[0]
    n = lengths.shape[0]
    stop = n if stop is None else stop
    length = rows // n
    tile = pl.BlockSpec((length, D), lambda c: (c + start, 0))
    full = pl.BlockSpec((D, D), lambda c: (0, 0))
    eight = pl.BlockSpec((8, D), lambda c: (0, 0))
    act = shaped((rows, D), BF16)
    return call(
        functools.partial(attn_fwd_body, start), (stop - start,),
        [pl.BlockSpec(memory_space=pltpu.SMEM), tile, full, full, full, eight] + [pl.BlockSpec(memory_space=pl.ANY)] * len(before),
        [tile, tile, tile, tile, pl.BlockSpec((1, HEADS, length), lambda c: (c + start, 0, 0))],
        [act, act, act, act, shaped((n, HEADS, length), F32)],
        flops=2 * rows * D * D * 3 + 4 * rows * length * D * 4, moved=rows * D * 10 + 6 * D * D,
        aliases={6 + i: i for i in range(5)} if before else {},
     vmem=24,)(lengths, x, wq, wk, wv, table, *before)


def attn_bwd_body(start, len_ref, q_ref, k_ref, v_ref, gm_ref, lse_ref, *rest):
    grads_ref, gbq_ref, gbv_ref = rest[-3:]
    c = pl.program_id(0)
    length = q_ref.shape[0]
    valid = lax.broadcasted_iota(jnp.int32, (length, length), 0) < len_ref[c + start]

    @pl.when(c == 0)
    def _():
        gbq_ref[...] = rest[1][...] if start else jnp.zeros_like(gbq_ref)
        gbv_ref[...] = rest[2][...] if start else jnp.zeros_like(gbv_ref)

    for g in range(HEADS // GROUP):
        cols = slice(GROUP * HEAD * g, GROUP * HEAD * (g + 1))
        q, gm = q_ref[:, cols], gm_ref[:, cols]
        keys = by_head(k_ref[:, cols], 0.125)
        scores = dot_rt(keys, q)
        gprobs = dot_rt(by_head(v_ref[:, cols]), gm)
        probs, gscores = [], []
        for t in range(GROUP):
            rows = slice(length * t, length * (t + 1))
            h = GROUP * g + t
            pf = jnp.exp(jnp.where(valid, scores[rows], masked_score) - lse_ref[0, h : h + 1, :])
            gp = gprobs[rows]
            gs = pf * (gp - jnp.sum(pf * gp, axis=0, keepdims=True))
            probs.append(pf.astype(BF16))
            gscores.append(gs.astype(BF16))
        gscores = jnp.concatenate(gscores, axis=0)
        gv = own_columns(dot(jnp.concatenate(probs, axis=0), gm)).astype(BF16)
        gk = (own_columns(dot(gscores, q)) * 0.125).astype(BF16)
        gq = dot_lt(gscores, keys).astype(BF16)
        for m, value in enumerate((gq, gk, gv)):
            grads_ref[:, m * D + cols.start : m * D + cols.stop] = value
        gbq_ref[:, cols] += jnp.sum(gq.astype(F32), axis=0, keepdims=True)
        gbv_ref[:, cols] += jnp.sum(gv.astype(F32), axis=0, keepdims=True)


def attn_bwd(q, k, v, gm, lse, lengths, start=0, stop=None, before=(), weight=0):
    rows = q.shape[0]
    n = lengths.shape[0]
    stop = n if stop is None else stop
    length = rows // n
    tile = pl.BlockSpec((length, D), lambda c: (c + start, 0))
    one = pl.BlockSpec((1, D), lambda c: (0, 0))
    whole = pl.BlockSpec(memory_space=pl.ANY)
    return call(
        functools.partial(attn_bwd_body, start), (stop - start,),
        [pl.BlockSpec(memory_space=pltpu.SMEM), tile, tile, tile, tile, pl.BlockSpec((1, HEADS, length), lambda c: (c + start, 0, 0))]
        + ([whole, one, one] if before else []),
        [pl.BlockSpec((length, 3 * D), lambda c: (c + start, 0)), one, one],
        [shaped((rows, 3 * D), BF16), shaped((1, D), F32), shaped((1, D), F32)],
        flops=2 * (stop - start) * length * length * D * 5 * 4, moved=(stop - start) * length * D * 14,
        aliases={6: 0} if before else {}, weight=weight,
     vmem=20,)(lengths, q, k, v, gm, lse, *before)


def mean(v):
    return jnp.sum(v, axis=-1, keepdims=True) * (1.0 / D)


def normalize(values):
    center = values - mean(values)
    scale = lax.rsqrt(mean(center * center) + epsilon)
    return center * scale, scale


def norm_back(incoming, normed, scale, gain):
    weighted = incoming * gain
    return scale * (weighted - mean(weighted) - normed * mean(weighted * normed))


def colsum(v):
    return jnp.sum(v, axis=0, keepdims=True)


def gelu_parts(pre):
    cdf = 0.5 + 0.5 * lax.erf(pre * 0.7071067811865476)
    pdf = 0.3989422804014327 * jnp.exp(-0.5 * pre * pre)
    return pre * cdf, cdf + pre * pdf


def wgrad_body(l_ref, r_ref, o_ref):
    o_ref[...] = dot_lt(l_ref[...], r_ref[...]).astype(o_ref.dtype)


def wgrad(left, right, tile_m=768, dtype=BF16):
    rows, m = left.shape
    n = right.shape[1]
    tn = min(n, 768)
    return call(
        wgrad_body, (n // tn, m // tile_m),
        [pl.BlockSpec((rows, tile_m), lambda j, i: (0, i)), pl.BlockSpec((rows, tn), lambda j, i: (0, j))],
        pl.BlockSpec((tile_m, tn), lambda j, i: (i, j)),
        shaped((m, n), dtype),
        flops=2 * rows * m * n, moved=2 * (rows * (m + n) + m * n),
    )(left, right)

def tie(*values):
    return lax.optimization_barrier(values)


def place():
    idx = lax.axis_index("fsdp")
    return idx % 2, (idx // 2) % 4, idx // 8

def swap(n, bits):
    return [(i, i ^ bits) for i in range(n)]

def shift(n, k):
    return [(i, (i + 8 * k) % n) for i in range(n)]

def hop(value, pairs):
    return lax.ppermute(value, "fsdp", pairs)


def join_body(*refs):
    at = 0
    for ref in refs[:-1]:
        refs[-1][at : at + ref.shape[0]] = ref[...]
        at += ref.shape[0]


def join(*parts):
    parts = [p if p.ndim == 3 else p[None] for p in parts]
    full = lambda a: pl.BlockSpec(a.shape, lambda i: (0, 0, 0))
    out = shaped((sum(p.shape[0] for p in parts),) + parts[0].shape[1:], BF16)
    return call(join_body, (1,), [full(p) for p in parts], full(out), out, vmem=16)(*parts)


def gather_all(first, second, n, spare, steps):
    work, given = spare
    across = lambda part: hop(part, swap(n, 1))
    f1, f2, f3 = (hop(first, shift(n, k)) for k in (1, 2, 3))
    x0, y0, d0 = (hop(second, swap(n, b)) for b in (2, 4, 6))
    line = jnp.stack([first, f1, f2, f3])
    line, second = tie(line, second)
    near = [hop(line, swap(n, b)) for b in (2, 4, 6)]
    z1, z3 = (hop(second, shift(n, k)) for k in (1, 3))
    near, second, z1, z3, given, x0, y0, d0 = tie(near, second, z1, z3, given, x0, y0, d0)
    mine = jnp.concatenate([line, *near])
    other = across(mine)
    pair = jnp.stack([z1, z3])
    z2 = hop(second, shift(n, 2))
    x13, y13 = (hop(pair, swap(n, b)) for b in (2, 4))
    other, begun = tie(other, join(second, x0, y0, z1, z3))
    begun_other = across(begun)
    held = steps[1](steps[0](mine, other))
    held, d0, z2, x13, y13, begun_other, done = tie(held, d0, z2, x13, y13, begun_other, work(given))
    middle = jnp.concatenate([d0[None], z2[None], x13, y13])
    middle_other = across(middle)
    last = [hop(z2, swap(n, b)) for b in (2, 4, 6)] + [hop(d0, shift(n, k)) for k in (1, 3)]
    held, middle_other = tie(held, middle_other)
    held, last = tie(steps[2](held), last)
    last = [p[None] for p in last]
    return done, held, [begun, middle, *last], [begun_other, middle_other, *(across(p) for p in last)]


def first_sources():
    return [(d, k) for d in range(4) for k in range(4)]


def second_sources():
    begun = [(0, 0), (1, 0), (2, 0), (0, 1), (0, 3)]
    middle = [(3, 0), (0, 2), (1, 1), (1, 3), (2, 1), (2, 3)]
    last = [[(1, 2)], [(2, 2)], [(3, 2)], [(3, 1)], [(3, 3)]]
    return [(p, i, *at) for p, part in enumerate([begun, middle] + last) for i, at in enumerate(part)]


def assemble_body(own, at_ref, mine_ref, other_ref, wq_ref, wk_ref, wv_ref, table_ref, ub_ref):
    core, fast, slow = at_ref[0], at_ref[1], at_ref[2]
    table = jnp.zeros((8, D), F32)
    ub = jnp.zeros((8, D), F32)
    for i, (dxy, dz) in enumerate(first_sources()):
        chip = ((slow - dz) % 4) * 4 + (fast ^ dxy)
        a, b = mine_ref[i], other_ref[i]
        low, high = jnp.where(core == 0, a, b), jnp.where(core == 0, b, a)
        for m, ref in enumerate((wq_ref, wk_ref, wv_ref)):
            rows = slice(own * m, own * m + own)
            ref[chip] = jnp.concatenate([low[rows], high[rows]], axis=0)
        for side, got in ((0, low), (1, high)):
            tail = got[3 * own :].astype(F32)
            spot = chip * 2 + side
            lane = lax.broadcasted_iota(jnp.int32, (8, D), 1)
            row = lax.broadcasted_iota(jnp.int32, (8, D), 0)
            table = table + pltpu.roll(jnp.where(lane < own, tail, 0.0), spot * own, 1)
            wide = jnp.where((lane >= 128) & (lane < 128 + 4 * own) & (row == spot // 8), tail[0:1], 0.0)
            ub = ub + pltpu.roll(wide, (D - 128 + spot % 8 * 4 * own) % D, 1)
    table_ref[...] = table
    ub_ref[...] = ub[:4]


def assemble(at, mine, other, own, n):
    full = lambda a: pl.BlockSpec(a.shape, lambda i: (0,) * a.ndim)
    arrays = [mine, other]
    w = shaped((n // 2, 2 * own, D), BF16)
    outs = [w, w, w, shaped((8, D), F32), shaped((4, D), F32)]
    wq, wk, wv, table, ub = call(
        functools.partial(assemble_body, own), (1,),
        [pl.BlockSpec(memory_space=pltpu.SMEM)] + [full(a) for a in arrays],
        [full(a) for a in outs], outs, moved=7 * D * D * 2,
     vmem=28,)(at, *arrays)
    return wq.reshape(D, D), wk.reshape(D, D), wv.reshape(D, D), table, ub


def pack_small(vectors, wide):
    total = jnp.pad(wide[None, :], ((0, 7), (128, D - 128 - wide.shape[0])))
    for i, v in enumerate(vectors):
        total = total + jnp.pad(v[None, :], ((i, 7 - i), (0, D - v.shape[0])))
    return total


def ffn_parts_body(chunk, own, at_ref, mix_ref, x_ref, gy_ref, *rest):
    mine, other, (small_ref, ub_ref) = rest[:7], rest[7:14], rest[14:16]
    outs, (dg_ref, wo_ref, wu_ref, wd_ref) = rest[16:-4], rest[-4:]
    wide = 4 * own

    @pl.when(pl.program_id(0) == 0)
    def _():
        core, fast, slow = at_ref[0], at_ref[1], at_ref[2]
        for part, i, dxy, dz in second_sources():
            chip = ((slow - dz) % 4) * 4 + (fast ^ dxy)
            a, b = mine[part][i], other[part][i]
            low, high = jnp.where(core == 0, a, b), jnp.where(core == 0, b, a)
            at = pl.ds(pl.multiple_of(2 * wide * chip, 16), wide)
            wd_ref[at, :] = low[:wide]
            at = pl.ds(pl.multiple_of(2 * wide * chip + wide, 16), wide)
            wd_ref[at, :] = high[:wide]
            at = pl.ds(pl.multiple_of(2 * own * chip, 16), 2 * own)
            for j in range(5):
                rows = slice(wide + own * j, wide + own * j + own)
                both = jnp.concatenate([low[rows], high[rows]], axis=0)
                if j < 4:
                    wu_ref[at, D * j : D * j + D] = both
                else:
                    wo_ref[at, :] = both

    ffn_steps(chunk, mix_ref, x_ref, gy_ref, wo_ref, wu_ref, wd_ref, small_ref, ub_ref, *outs, dg_ref)


def ffn_steps(chunk, mix_ref, x_ref, gy_ref, wo_ref, wu_ref, wd_ref, small_ref, ub_ref,
              out_ref, hid_ref, gffn_ref, low_ref, gpre_ref, gattn_ref, g1_ref, gmix_ref, gsmall_ref, gub_ref, dg_ref):
    bo, again, ashift, bd, fgain, fshift = (small_ref[j : j + 1, :] for j in range(2, 8))
    ff = wu_ref.shape[1]
    size = x_ref.shape[0]
    middle = (size // 2 + 15) // 16 * 16
    halves = (slice(0, middle), slice(middle, size))

    @pl.when(pl.program_id(0) == 0)
    def _():
        gsmall_ref[...] = jnp.zeros_like(gsmall_ref)
        gub_ref[...] = jnp.zeros_like(gub_ref)

    def total(index, values):
        gsmall_ref[index : index + 1, :] += sum(colsum(v) for v in values)

    def norm_first(rows, attn):
        xhat, rs = normalize(x_ref[rows].astype(F32) + attn + bo)
        first = xhat * again + ashift
        low = first.astype(BF16)
        low_ref[rows] = low
        return xhat, rs, first, low

    def up(j, rows, low):
        cols = slice(j * chunk, (j + 1) * chunk)
        hid, dg = gelu_parts(dot(low, wu_ref[:, cols]) + ub_ref[j : j + 1, :])
        hid = hid.astype(BF16)
        hid_ref[rows, cols] = hid
        dg_ref[rows, cols] = dg.astype(dg_ref.dtype)
        return hid

    def norm_second(rows, first, ffn):
        xhat, rs = normalize(first + ffn + bd)
        out_ref[rows] = (xhat * fgain + fshift).astype(BF16)
        gy = gy_ref[rows].astype(F32)
        g2 = norm_back(gy, xhat, rs, fgain)
        gffn = g2.astype(BF16)
        gffn_ref[rows] = gffn
        return g2, gffn, gy, gy * xhat

    def back(j, rows, gffn):
        cols = slice(j * chunk, (j + 1) * chunk)
        gpre = (dot_rt(gffn, wd_ref[cols, :]) * dg_ref[rows, cols].astype(F32)).astype(BF16)
        gpre_ref[rows, cols] = gpre
        return gpre

    count = ff // chunk
    attn = [dot(mix_ref[rows], wo_ref[...]) for rows in halves]
    state, hid, ffn = [None, None], [None, None], [0.0, 0.0]
    for i, rows in enumerate(halves):
        state[i] = norm_first(rows, attn[i])
        hid[i] = up(0, rows, state[i][3])
    for j in range(count):
        for i, rows in enumerate(halves):
            ffn[i] = ffn[i] + dot(hid[i], wd_ref[j * chunk : (j + 1) * chunk, :])
            if j + 1 < count:
                hid[i] = up(j + 1, rows, state[i][3])
    grads, gpre, gfirst = [None, None], [None, None], [None, None]
    for i, rows in enumerate(halves):
        grads[i] = norm_second(rows, state[i][2], ffn[i])
        gfirst[i] = grads[i][0]
        gpre[i] = back(0, rows, grads[i][1])
    total(5, [g[1].astype(F32) for g in grads])
    total(6, [g[3] for g in grads])
    total(7, [g[2] for g in grads])
    for j in range(count):
        cols = slice(j * chunk, (j + 1) * chunk)
        gub_ref[:, cols] += sum(colsum(g.astype(F32)) for g in gpre)
        for i, rows in enumerate(halves):
            gfirst[i] = gfirst[i] + dot_rt(gpre[i], wu_ref[:, cols])
            if j + 1 < count:
                gpre[i] = back(j + 1, rows, grads[i][1])
    gattn = [None, None]
    for i, rows in enumerate(halves):
        xhat, rs = state[i][:2]
        g1 = norm_back(gfirst[i], xhat, rs, again)
        gattn[i] = g1.astype(BF16)
        g1_ref[rows] = g1
        gattn_ref[rows] = gattn[i]
        gmix_ref[rows] = dot_rt(gattn[i], wo_ref[...]).astype(BF16)
    total(2, [g.astype(F32) for g in gattn])
    total(3, [gfirst[i] * state[i][0] for i in range(2)])
    total(4, gfirst)


def ffn_full_body(chunk, *refs):
    ffn_steps(chunk, *refs)


def ffn_both(mixed, x, gy, weights, small, ub, at=None, own=0, tile_rows=560, chunk=D):
    rows = x.shape[0]
    ff = ub.size
    tile = pl.BlockSpec((tile_rows, D), lambda c: (c, 0))
    wide = pl.BlockSpec((tile_rows, ff), lambda c: (c, 0))
    fixed = lambda a: pl.BlockSpec(a.shape, lambda c: (0,) * a.ndim, pipeline_mode=pl.Buffered(1))
    act = shaped((rows, D), BF16)
    big = shaped((rows, ff), BF16)
    scratch = [pltpu.VMEM((tile_rows, ff), BF16)]
    body, place_of, specs = functools.partial(ffn_full_body, chunk), [], []
    if at is not None:
        body, place_of, specs = functools.partial(ffn_parts_body, chunk, own), [at], [pl.BlockSpec(memory_space=pltpu.SMEM)]
        scratch += [pltpu.VMEM((D, D), BF16), pltpu.VMEM((D, ff), BF16), pltpu.VMEM((ff, D), BF16)]
    return call(
        body, (rows // tile_rows,),
        specs + [tile, tile, tile] + [fixed(w) for w in weights] + [fixed(small), fixed(ub)],
        [tile, wide, tile, tile, wide, tile, tile, tile, pl.BlockSpec((8, D), lambda c: (0, 0)), pl.BlockSpec((1, ff), lambda c: (0, 0))],
        [act, big, act, act, big, act, shaped((rows, D), F32), act, shaped((8, D), F32), shaped((1, ff), F32)],
        scratch=scratch, vmem=61,
        flops=2 * rows * D * (2 * D + 4 * ff), moved=rows * (D * 20 + ff * 4) + D * (D + 2 * ff) * 2,
    )(*place_of, mixed, x, gy, *weights, small, ub)


def row_block(at_ref, far, own, dxy, dz):
    chip = ((at_ref[2] + dz) % far) * 4 + (at_ref[1] ^ dxy)
    return tuple(2 * chip + side for side in (at_ref[0], 1 - at_ref[0]))


def acc_rows(ref, m, d, own):
    at = pl.ds(pl.multiple_of(own * d, 8), own)
    return ref[at, :] if m is None else ref[m, at, :]


def keep_send(*shape):
    out = shaped((4,) + shape, BF16)
    spec = pl.BlockSpec(out.shape, lambda j: (0,) * len(out.shape))
    return [spec, spec], [out, out]


def wgrad_down_body(far, own, at_ref, hid_ref, gffn_ref, keep_ref, send_ref, acc_ref):
    acc_ref[...] = dot_lt(hid_ref[...], gffn_ref[...])
    for dxy in range(4):
        chip = at_ref[1] ^ dxy
        for out, side in zip((keep_ref, send_ref), (at_ref[0], 1 - at_ref[0])):
            out[dxy, 0] = acc_rows(acc_ref, None, 2 * chip + side, own).astype(BF16)


def wgrad_down(at, hidden, gffn, n):
    rows, ff = hidden.shape
    far = n // 8
    own = ff // n
    out = shaped((4, far, own, D), BF16)
    spec = pl.BlockSpec((4, 1, own, D), lambda j, at_ref: (0, (j + far - at_ref[2]) % far, 0, 0))
    return call(
        functools.partial(wgrad_down_body, far, own), (far,),
        [pl.BlockSpec((rows, ff // far), lambda j, at_ref: (0, j)), pl.BlockSpec((rows, D), lambda j, at_ref: (0, 0))],
        [spec, spec], [out, out], scratch=[pltpu.VMEM((ff // far, D), F32)], prefetch=1,
     vmem=60,)(at, hidden, gffn)


def wgrad_up_body(far, own, at_ref, low_ref, gpre_ref, mix_ref, gattn_ref, keep_ref, send_ref, acc_ref):
    j = pl.program_id(0)

    @pl.when(j < 4)
    def _():
        acc_ref[...] = dot_lt(low_ref[...], gpre_ref[...])

    @pl.when(j == 4)
    def _():
        acc_ref[...] = dot_lt(mix_ref[...], gattn_ref[...])

    for dxy in range(4):
        for dz in range(far):
            for out, d in zip((keep_ref, send_ref), row_block(at_ref, far, own, dxy, dz)):
                out[dxy, dz, 0] = acc_rows(acc_ref, None, d, own).astype(BF16)


def wgrad_up(at, low, gpre, mixed, gattn, own, n):
    rows = low.shape[0]
    far = n // 8
    act = pl.BlockSpec((rows, D), lambda j: (0, 0))
    out = shaped((4, far, 5, own, D), BF16)
    spec = pl.BlockSpec((4, far, 1, own, D), lambda j: (0, 0, j, 0, 0))
    got = call(
        functools.partial(wgrad_up_body, far, own), (5,),
        [pl.BlockSpec(memory_space=pltpu.SMEM), act, pl.BlockSpec((rows, D), lambda j: (0, jnp.minimum(j, 3))), act, act],
        [spec, spec], [out, out], scratch=[pltpu.VMEM((D, D), F32)],
     vmem=32,)(at, low, gpre, mixed, gattn)
    return [g.reshape(4, far, 5 * own, D) for g in got]


def wgrad_in_body(far, own, at_ref, x_ref, grad_ref, small_ref, ub_ref, keep_ref, send_ref, acc_ref):
    j = pl.program_id(0)
    acc_ref[j] = dot_lt(x_ref[...], grad_ref[...])

    @pl.when(j == 2)
    def _():
        lane = lax.broadcasted_iota(jnp.int32, (8, D), 1)
        row = lax.broadcasted_iota(jnp.int32, (8, D), 0)
        ff = ub_ref.shape[1]
        wide = ff // (8 * far)
        for dxy in range(4):
            for dz in range(far):
                for out, d in zip((keep_ref, send_ref), row_block(at_ref, far, own, dxy, dz)):
                    tail = pltpu.roll(small_ref[...], (D - own * d) % D, 1)
                    ub = pltpu.roll(ub_ref[...], (ff + 128 - wide * d) % ff, 1)[:, :D]
                    tail = jnp.where(lane < own, tail, 0.0)
                    tail = jnp.where((row == 0) & (lane >= 128) & (lane < 128 + wide), ub, tail)
                    parts = [acc_rows(acc_ref, m, d, own) for m in range(3)] + [tail]
                    out[dxy, dz] = jnp.concatenate(parts, axis=0).astype(BF16)


def wgrad_in(at, x, grads, small, ub, own, n):
    rows = x.shape[0]
    far = n // 8
    full = lambda a: pl.BlockSpec(a.shape, lambda i: (0,) * a.ndim)
    specs, outs = keep_send(far, 3 * own + 8, D)
    return call(
        functools.partial(wgrad_in_body, far, own), (3,),
        [pl.BlockSpec(memory_space=pltpu.SMEM), full(x), pl.BlockSpec((rows, D), lambda j: (0, j)), full(small), full(ub)],
        specs, outs, scratch=[pltpu.VMEM((3, D, D), F32)],
     vmem=36,)(at, x, grads, small, ub)


def pair_sum(keep, other, i):
    return keep[i].astype(F32) + other[i].astype(F32)


def near_parts(keep, other):
    return tuple(pair_sum(keep, other, i).astype(BF16) for i in (1, 2, 3))


def near_hops(parts, n):
    return tuple(hop(p, swap(n, 2 * i)) for i, p in enumerate(parts, 1))


def line_body(keep_ref, other_ref, x_ref, y_ref, d_ref, base_ref, *sent):
    total = keep_ref[...].astype(F32) + other_ref[...].astype(F32)
    for ref in (x_ref, y_ref, d_ref):
        total = total + ref[...].astype(F32)
    base_ref[...] = total[0, 0]
    for k, ref in enumerate(sent, 1):
        ref[...] = total[0, k].astype(BF16)


def line_sum(keep, other, near):
    far, rows = keep.shape[1:3]
    block = pl.BlockSpec((1, far, rows, D), lambda i: (0, 0, 0, 0))
    part = pl.BlockSpec((rows, D), lambda i: (0, 0))
    base, *sent = call(
        line_body, (1,), [block] * 5, [part] * far,
        [shaped((rows, D), F32)] + [shaped((rows, D), BF16)] * (far - 1),
     vmem=16,)(keep, other, *(p[None] for p in near))
    return base, sent


def pass_body(in_ref, out_ref):
    out_ref[...] = in_ref[...]


def passed(value):
    full = pl.BlockSpec(value.shape, lambda i: (0, 0))
    return call(pass_body, (1,), [full], full, shaped(value.shape, value.dtype), weight=WAIT, vmem=8)(value)


def far_hops(sent, n, which):
    return {k: hop(sent[k - 1], shift(n, k)) for k in which}


def last_sum(base, far):
    return base + sum(p.astype(F32) for p in far.values())


def input_grad_body(g1_ref, gq_ref, gk_ref, gv_ref, wq_ref, wk_ref, wv_ref, *rest):
    total = g1_ref[...] + dot_rt(gq_ref[...], wq_ref[...])
    total = total + dot_rt(gk_ref[...], wk_ref[...]) + dot_rt(gv_ref[...], wv_ref[...])
    rest[-1][...] = total.astype(BF16)


def input_grad(g1, grads, wq, wk, wv, start=0, stop=4, before=(), tiles=4):
    rows = g1.shape[0]
    tile = pl.BlockSpec((rows // tiles, D), lambda c: (c + start, 0))
    full = pl.BlockSpec((D, D), lambda c: (0, 0))
    return call(
        input_grad_body, (stop - start,),
        [tile] + [pl.BlockSpec((rows // tiles, D), lambda c, m=m: (c + start, m)) for m in range(3)] + [full, full, full] + [pl.BlockSpec(memory_space=pl.ANY)] * len(before),
        tile, shaped((rows, D), BF16), aliases={7: 0} if before else {},
        flops=6 * rows * D * D, moved=rows * D * 12 + 6 * D * D,
     vmem=24,)(g1, grads, grads, grads, wq, wk, wv, *before)


def residue_mask(cotangent, span_start, span_end):
    chains = span_start.shape[0]
    rows = cotangent.shape[0]
    positions = jnp.arange(rows // chains)
    inside = jnp.any(
        (positions[None, None, :] >= span_start[:, :, None]) & (positions[None, None, :] < span_end[:, :, None]),
        axis=1,
    )
    return jnp.where(inside.reshape(rows, 1), cotangent, jnp.zeros_like(cotangent))


def chunked(weight):
    own = weight.shape[0]
    return weight.reshape(own, -1, D).swapaxes(0, 1).reshape(-1, D)


def fast_shards(
    n, tokens, cotangent, lengths, span_start, span_end,
    query_weight, query_bias, key_weight, value_weight, value_bias, out_weight, out_bias,
    attn_gain, attn_shift, up_weight, up_bias, down_weight, down_bias, ffn_gain, ffn_shift,
):
    own = query_weight.shape[0]
    wide = up_bias.shape[0]
    vectors = (query_bias, value_bias, out_bias, attn_gain, attn_shift, down_bias, ffn_gain, ffn_shift)
    at = jnp.stack(place()).astype(jnp.int32)
    block = jnp.concatenate([query_weight, key_weight, value_weight, pack_small(vectors, up_bias)], axis=0)
    second = jnp.concatenate([down_weight, chunked(up_weight), out_weight], axis=0)
    chains = lengths.shape[0]
    ahead = chains * 3 // 7

    def attend(w, start, stop, before=()):
        return w, attn_fwd(tokens, *w[:4], lengths, start, stop, before)

    gy, ((wq, wk, wv, table, ub), (q, k, v, mixed, lse)), mine, other = gather_all(
        block, second, n,
        (lambda given: residue_mask(*given), (cotangent, span_start, span_end)),
        (
            lambda mine, other: assemble(at, mine, other, own, n),
            lambda w: attend(w, 0, ahead),
            lambda held: attend(held[0], ahead, chains, held[1]),
        ),
    )
    layer_out, hidden, gffn, low, gpre, gattn, g1, gmixed, gtable, gub = ffn_both(
        mixed, tokens, gy, mine + other, table, ub, at, own
    )
    cuts = (0, 1, 4, chains)
    keep_d, send_d = wgrad_down(at, hidden, gffn, n)
    gmixed, keep_d, send_d = tie(gmixed, keep_d, send_d)
    other_d = hop(send_d, swap(n, 1))
    begun = attn_bwd(q, k, v, gmixed, lse, lengths, cuts[0], cuts[1], weight=WAIT)
    begun, other_d = tie(begun, other_d)
    low, begun, parts_d = tie(low, begun, near_parts(keep_d, other_d))
    near_d = near_hops(parts_d, n)
    keep_u, send_u = wgrad_up(at, low, gpre, mixed, gattn, own, n)
    begun, keep_u, send_u = tie(begun, keep_u, send_u)
    other_u = hop(send_u, swap(n, 1))
    begun = attn_bwd(q, k, v, gmixed, lse, lengths, cuts[1], cuts[2], begun)
    begun, near_d = tie(begun, near_d)
    begun = [begun[0], passed(begun[1]), begun[2]]
    begun, other_u = tie(begun, other_u)
    begun, parts_u = tie(begun, near_parts(keep_u, other_u))
    near_u = near_hops(parts_u, n)
    base_d, sent_d = line_sum(keep_d, other_d, near_d)
    begun, base_d, sent_d = tie(begun, base_d, sent_d)
    far_d = far_hops(sent_d, n, (1, 3))
    grads, gqb, gvb = attn_bwd(q, k, v, gmixed, lse, lengths, cuts[2], cuts[3], begun)
    grads, far_d, sent_d = tie(grads, far_d, sent_d)
    far_d.update(far_hops(sent_d, n, (2,)))
    gtable = jnp.concatenate([gqb, gvb, gtable[2:]], axis=0)
    keep_i, send_i = wgrad_in(at, tokens, grads, gtable, gub, own, n)
    g1, keep_i, send_i = tie(g1, keep_i, send_i)
    other_i = hop(send_i, swap(n, 1))
    in_grad = input_grad(g1, grads, wq, wk, wv, 0, 2)
    in_grad, near_u, far_d, base_d = tie(in_grad, near_u, far_d, base_d)
    base_d = passed(base_d)
    base_d, other_i = tie(base_d, other_i)
    in_grad, parts_i, base_d = tie(in_grad, near_parts(keep_i, other_i), base_d)
    near_i = near_hops(parts_i, n)
    base_u, sent_u = line_sum(keep_u, other_u, near_u)
    in_grad, base_u, sent_u = tie(in_grad, base_u, sent_u)
    far_u = far_hops(sent_u, n, (1, 2))
    in_grad = input_grad(g1, grads, wq, wk, wv, 2, 4, (in_grad,))
    in_grad, near_i, far_u = tie(in_grad, near_i, far_u)
    base_i, sent_i = line_sum(keep_i, other_i, near_i)
    far_i = far_hops(sent_i, n, (1, 2, 3))
    far_u.update(far_hops(sent_u, n, (3,)))
    down_own, up_own, in_own = last_sum(base_d, far_d), last_sum(base_u, far_u), last_sum(base_i, far_i)

    gq_w, gk_w, gv_w = (in_own[own * i : own * (i + 1)] for i in range(3))
    gqb, gvb, gob, gag, gas, gdb, gfg, gfs = (in_own[3 * own + i, :own] for i in range(8))
    gub = in_own[3 * own, 128 : 128 + wide]
    gup = jnp.concatenate([up_own[own * i : own * (i + 1)] for i in range(wide // own)], axis=1)
    go_w = up_own[wide : wide + own]
    return (
        layer_out, in_grad, gq_w, gqb, gk_w, gv_w, gvb, go_w, gob, gag, gas, gup, gub, down_own, gdb, gfg, gfs,
    )


def plain_shards(
    tokens, cotangent, lengths, span_start, span_end,
    query_weight, query_bias, key_weight, value_weight, value_bias, out_weight, out_bias,
    attn_gain, attn_shift, up_weight, up_bias, down_weight, down_bias, ffn_gain, ffn_shift,
):
    own = query_weight.shape[0]
    parts = D // own
    ff = up_weight.shape[1]
    wide = own * ff // D
    vectors = (query_bias, value_bias, out_bias, attn_gain, attn_shift, down_bias, ffn_gain, ffn_shift, up_bias)
    packed = jnp.concatenate(vectors)
    packed = jnp.pad(packed, (0, D - packed.shape[0])).reshape(1, D)
    sent = jnp.concatenate(
        [query_weight, key_weight, value_weight, out_weight, chunked(up_weight), down_weight, packed], axis=0
    )
    held = lax.all_gather(sent, "fsdp", axis=0, tiled=False)
    wq, wk, wv, wo = (held[:, own * i : own * (i + 1)].reshape(D, D) for i in range(4))
    wu = jnp.concatenate(
        [held[:, own * (4 + i) : own * (5 + i)].reshape(D, D) for i in range(ff // D)], axis=1
    )
    wd = held[:, 4 * own + wide : 4 * own + 2 * wide].reshape(ff, D)
    small = held[:, -1].astype(F32)
    table = jnp.concatenate([small[:, own * i : own * (i + 1)].reshape(1, D) for i in range(8)], axis=0)
    ub = small[:, 8 * own : 8 * own + wide].reshape(ff // D, D)
    gy = residue_mask(cotangent, span_start, span_end)

    q, k, v, mixed, lse = attn_fwd(tokens, wq, wk, wv, table, lengths)
    layer_out, hidden, gffn, low, gpre, gattn, g1, gmixed, gtable, gub = ffn_both(
        mixed, tokens, gy, (wo, wu, wd), table, ub
    )
    down_grad = wgrad(hidden, gffn)
    up_grad = wgrad(low, gpre)
    ffn_parts = jnp.concatenate([up_grad.reshape(parts, wide, D), down_grad.reshape(parts, wide, D)], axis=1)
    ffn_own = lax.psum_scatter(ffn_parts, "fsdp", scatter_dimension=0, tiled=False).astype(F32)
    out_grad = wgrad(mixed, gattn)
    grads, gqb, gvb = attn_bwd(q, k, v, gmixed, lse, lengths)
    query_grad, key_grad, value_grad = (wgrad(tokens, grads)[:, D * i : D * (i + 1)] for i in range(3))
    vec = [gqb, gvb] + [gtable[i : i + 1] for i in range(2, 8)]
    vec = jnp.concatenate([p.reshape(parts, own) for p in vec] + [gub.reshape(parts, wide)], axis=1)
    vec = jnp.pad(vec.astype(BF16), ((0, 0), (0, D - vec.shape[1]))).reshape(parts, 1, D)
    attn_parts = jnp.concatenate(
        [g.reshape(parts, own, D) for g in (query_grad, key_grad, value_grad, out_grad)] + [vec], axis=1
    )
    attn_own = lax.psum_scatter(attn_parts, "fsdp", scatter_dimension=0, tiled=False).astype(F32)
    in_grad = input_grad(g1, grads, wq, wk, wv)

    gq_w, gk_w, gv_w, go_w = (attn_own[own * i : own * (i + 1)] for i in range(4))
    vec = attn_own[-1]
    gqb, gvb, gob, gag, gas, gdb, gfg, gfs = (vec[own * i : own * (i + 1)] for i in range(8))
    gub = vec[8 * own : 8 * own + wide]
    gup = ffn_own[:wide].reshape(own, ff)
    gdown = ffn_own[wide:]
    return (
        layer_out, in_grad, gq_w, gqb, gk_w, gv_w, gvb, go_w, gob, gag, gas, gup, gub, gdown, gdb, gfg, gfs,
    )


def solution(mesh):
    two, one = P("fsdp", None), P("fsdp")
    n = mesh.shape["fsdp"]
    whole_tiles = n % 8 == 0 and n // 8 == 4 and (D // n) % 8 == 0
    return jax.shard_map(
        functools.partial(fast_shards, n) if whole_tiles else plain_shards,
        mesh=mesh,
        in_specs=(two, two, one, two, two, two, one, two, two, one, two, one, one, one, two, one, two, one, one, one),
        out_specs=(two, two, two, one, two, two, one, two, one, one, one, two, one, two, one, one, one),
        check_vma=False,
    )
```

```python
import functools
import jax
import jax.numpy as jnp
from jax import lax
from jax.sharding import PartitionSpec as P
from jax.experimental import pallas as pl
from jax.experimental.pallas import tpu as pltpu

D = 768
HEADS = 12
HEAD = 64
epsilon = 1e-05
masked_score = -1000000000.0
F32 = jnp.float32
BF16 = jnp.bfloat16
WAIT = 1 << 40


def dot(left, right):
    return lax.dot_general(left, right, (((1,), (0,)), ((), ())), preferred_element_type=F32)


def dot_rt(left, right):
    return lax.dot_general(left, right, (((1,), (1,)), ((), ())), preferred_element_type=F32)


def dot_lt(left, right):
    return lax.dot_general(left, right, (((0,), (0,)), ((), ())), preferred_element_type=F32)


def call(body, grid, in_specs, out_specs, out_shape, scratch=(), flops=0, moved=0, vmem=60, aliases={}, weight=0, prefetch=0):
    return pl.pallas_call(
        body,
        grid_spec=pltpu.PrefetchScalarGridSpec(
            num_scalar_prefetch=prefetch, grid=grid, in_specs=in_specs, out_specs=out_specs, scratch_shapes=scratch
        ),
        out_shape=out_shape,
        input_output_aliases=aliases,
        compiler_params=pltpu.CompilerParams(vmem_limit_bytes=vmem * 1024 * 1024),
        cost_estimate=pl.CostEstimate(flops=weight, bytes_accessed=weight // 64, transcendentals=0),
    )


def shaped(shape, dtype):
    return jax.ShapeDtypeStruct(shape, dtype)


GROUP = 4


def by_head(values, scale=1.0):
    lane = lax.broadcasted_iota(jnp.int32, (1, GROUP * HEAD), 1) // HEAD
    return jnp.concatenate([values * jnp.where(lane == t, scale, 0.0).astype(BF16) for t in range(GROUP)], axis=0)


def own_columns(stacked):
    rows = stacked.shape[0] // GROUP
    lane = lax.broadcasted_iota(jnp.int32, (1, GROUP * HEAD), 1) // HEAD
    out = stacked[:rows]
    for t in range(1, GROUP):
        out = jnp.where(lane == t, stacked[rows * t : rows * (t + 1)], out)
    return out


def attn_fwd_body(start, len_ref, x_ref, wq_ref, wk_ref, wv_ref, table_ref, *rest):
    q_ref, k_ref, v_ref, mix_ref, lse_ref = rest[-5:]
    x = x_ref[...]
    length = x.shape[0]
    q_ref[...] = (dot(x, wq_ref[...]) + table_ref[0:1, :]).astype(BF16)
    k_ref[...] = dot(x, wk_ref[...]).astype(BF16)
    v_ref[...] = (dot(x, wv_ref[...]) + table_ref[1:2, :]).astype(BF16)
    valid = lax.broadcasted_iota(jnp.int32, (length, length), 0) < len_ref[pl.program_id(0) + start]
    for g in range(HEADS // GROUP):
        cols = slice(GROUP * HEAD * g, GROUP * HEAD * (g + 1))
        scores = dot_rt(by_head(k_ref[:, cols], 0.125), q_ref[:, cols])
        probs = []
        for t in range(GROUP):
            s = jnp.where(valid, scores[length * t : length * (t + 1)], masked_score)
            m = jnp.max(s, axis=0, keepdims=True)
            e = jnp.exp(s - m)
            total = jnp.sum(e, axis=0, keepdims=True)
            probs.append((e * (1.0 / total)).astype(BF16))
            lse_ref[0, GROUP * g + t : GROUP * g + t + 1, :] = m + jnp.log(total)
        mix_ref[:, cols] = dot_lt(jnp.concatenate(probs, axis=0), by_head(v_ref[:, cols])).astype(BF16)


def attn_fwd(x, wq, wk, wv, table, lengths, start=0, stop=None, before=()):
    rows = x.shape[0]
    n = lengths.shape[0]
    stop = n if stop is None else stop
    length = rows // n
    tile = pl.BlockSpec((length, D), lambda c: (c + start, 0))
    full = pl.BlockSpec((D, D), lambda c: (0, 0))
    eight = pl.BlockSpec((8, D), lambda c: (0, 0))
    act = shaped((rows, D), BF16)
    return call(
        functools.partial(attn_fwd_body, start), (stop - start,),
        [pl.BlockSpec(memory_space=pltpu.SMEM), tile, full, full, full, eight] + [pl.BlockSpec(memory_space=pl.ANY)] * len(before),
        [tile, tile, tile, tile, pl.BlockSpec((1, HEADS, length), lambda c: (c + start, 0, 0))],
        [act, act, act, act, shaped((n, HEADS, length), F32)],
        flops=2 * rows * D * D * 3 + 4 * rows * length * D * 4, moved=rows * D * 10 + 6 * D * D,
        aliases={6 + i: i for i in range(5)} if before else {},
     vmem=24,)(lengths, x, wq, wk, wv, table, *before)


def attn_bwd_body(start, len_ref, q_ref, k_ref, v_ref, gm_ref, lse_ref, *rest):
    grads_ref, gbq_ref, gbv_ref = rest[-3:]
    c = pl.program_id(0)
    length = q_ref.shape[0]
    valid = lax.broadcasted_iota(jnp.int32, (length, length), 0) < len_ref[c + start]

    @pl.when(c == 0)
    def _():
        gbq_ref[...] = rest[1][...] if start else jnp.zeros_like(gbq_ref)
        gbv_ref[...] = rest[2][...] if start else jnp.zeros_like(gbv_ref)

    for g in range(HEADS // GROUP):
        cols = slice(GROUP * HEAD * g, GROUP * HEAD * (g + 1))
        q, gm = q_ref[:, cols], gm_ref[:, cols]
        keys = by_head(k_ref[:, cols], 0.125)
        scores = dot_rt(keys, q)
        gprobs = dot_rt(by_head(v_ref[:, cols]), gm)
        probs, gscores = [], []
        for t in range(GROUP):
            rows = slice(length * t, length * (t + 1))
            h = GROUP * g + t
            pf = jnp.exp(jnp.where(valid, scores[rows], masked_score) - lse_ref[0, h : h + 1, :])
            gp = gprobs[rows]
            gs = pf * (gp - jnp.sum(pf * gp, axis=0, keepdims=True))
            probs.append(pf.astype(BF16))
            gscores.append(gs.astype(BF16))
        gscores = jnp.concatenate(gscores, axis=0)
        gv = own_columns(dot(jnp.concatenate(probs, axis=0), gm)).astype(BF16)
        gk = (own_columns(dot(gscores, q)) * 0.125).astype(BF16)
        gq = dot_lt(gscores, keys).astype(BF16)
        for m, value in enumerate((gq, gk, gv)):
            grads_ref[:, m * D + cols.start : m * D + cols.stop] = value
        gbq_ref[:, cols] += jnp.sum(gq.astype(F32), axis=0, keepdims=True)
        gbv_ref[:, cols] += jnp.sum(gv.astype(F32), axis=0, keepdims=True)


def attn_bwd(q, k, v, gm, lse, lengths, start=0, stop=None, before=(), weight=0):
    rows = q.shape[0]
    n = lengths.shape[0]
    stop = n if stop is None else stop
    length = rows // n
    tile = pl.BlockSpec((length, D), lambda c: (c + start, 0))
    one = pl.BlockSpec((1, D), lambda c: (0, 0))
    whole = pl.BlockSpec(memory_space=pl.ANY)
    return call(
        functools.partial(attn_bwd_body, start), (stop - start,),
        [pl.BlockSpec(memory_space=pltpu.SMEM), tile, tile, tile, tile, pl.BlockSpec((1, HEADS, length), lambda c: (c + start, 0, 0))]
        + ([whole, one, one] if before else []),
        [pl.BlockSpec((length, 3 * D), lambda c: (c + start, 0)), one, one],
        [shaped((rows, 3 * D), BF16), shaped((1, D), F32), shaped((1, D), F32)],
        flops=2 * (stop - start) * length * length * D * 5 * 4, moved=(stop - start) * length * D * 14,
        aliases={6: 0} if before else {}, weight=weight,
     vmem=20,)(lengths, q, k, v, gm, lse, *before)


def mean(v):
    return jnp.sum(v, axis=-1, keepdims=True) * (1.0 / D)


def normalize(values):
    center = values - mean(values)
    scale = lax.rsqrt(mean(center * center) + epsilon)
    return center * scale, scale


def norm_back(incoming, normed, scale, gain):
    weighted = incoming * gain
    return scale * (weighted - mean(weighted) - normed * mean(weighted * normed))


def colsum(v):
    return jnp.sum(v, axis=0, keepdims=True)


def gelu_parts(pre):
    cdf = 0.5 + 0.5 * lax.erf(pre * 0.7071067811865476)
    pdf = 0.3989422804014327 * jnp.exp(-0.5 * pre * pre)
    return pre * cdf, cdf + pre * pdf


def wgrad_body(l_ref, r_ref, o_ref):
    o_ref[...] = dot_lt(l_ref[...], r_ref[...]).astype(o_ref.dtype)


def wgrad(left, right, tile_m=768, dtype=BF16):
    rows, m = left.shape
    n = right.shape[1]
    tn = min(n, 768)
    return call(
        wgrad_body, (n // tn, m // tile_m),
        [pl.BlockSpec((rows, tile_m), lambda j, i: (0, i)), pl.BlockSpec((rows, tn), lambda j, i: (0, j))],
        pl.BlockSpec((tile_m, tn), lambda j, i: (i, j)),
        shaped((m, n), dtype),
        flops=2 * rows * m * n, moved=2 * (rows * (m + n) + m * n),
    )(left, right)

def tie(*values):
    return lax.optimization_barrier(values)


def place():
    idx = lax.axis_index("fsdp")
    return idx % 2, (idx // 2) % 4, idx // 8

def swap(n, bits):
    return [(i, i ^ bits) for i in range(n)]

def shift(n, k):
    return [(i, (i + 8 * k) % n) for i in range(n)]

def hop(value, pairs):
    return lax.ppermute(value, "fsdp", pairs)


def join_body(*refs):
    at = 0
    for ref in refs[:-1]:
        refs[-1][at : at + ref.shape[0]] = ref[...]
        at += ref.shape[0]


def join(*parts):
    parts = [p if p.ndim == 3 else p[None] for p in parts]
    full = lambda a: pl.BlockSpec(a.shape, lambda i: (0, 0, 0))
    out = shaped((sum(p.shape[0] for p in parts),) + parts[0].shape[1:], BF16)
    return call(join_body, (1,), [full(p) for p in parts], full(out), out, vmem=16)(*parts)


def gather_all(first, second, n, spare, steps):
    work, given = spare
    across = lambda part: hop(part, swap(n, 1))
    f1, f2, f3 = (hop(first, shift(n, k)) for k in (1, 2, 3))
    x0, y0, d0 = (hop(second, swap(n, b)) for b in (2, 4, 6))
    line = jnp.stack([first, f1, f2, f3])
    line, second = tie(line, second)
    near = [hop(line, swap(n, b)) for b in (2, 4, 6)]
    z1, z3 = (hop(second, shift(n, k)) for k in (1, 3))
    near, second, z1, z3, given, x0, y0, d0 = tie(near, second, z1, z3, given, x0, y0, d0)
    mine = jnp.concatenate([line, *near])
    other = across(mine)
    pair = jnp.stack([z1, z3])
    z2 = hop(second, shift(n, 2))
    x13, y13 = (hop(pair, swap(n, b)) for b in (2, 4))
    other, begun = tie(other, join(second, x0, y0, z1, z3))
    begun_other = across(begun)
    held = steps[1](steps[0](mine, other))
    held, d0, z2, x13, y13, begun_other, done = tie(held, d0, z2, x13, y13, begun_other, work(given))
    middle = jnp.concatenate([d0[None], z2[None], x13, y13])
    middle_other = across(middle)
    last = [hop(z2, swap(n, b)) for b in (2, 4, 6)] + [hop(d0, shift(n, k)) for k in (1, 3)]
    held, middle_other = tie(held, middle_other)
    held, last = tie(steps[2](held), last)
    last = [p[None] for p in last]
    return done, held, [begun, middle, *last], [begun_other, middle_other, *(across(p) for p in last)]


def first_sources():
    return [(d, k) for d in range(4) for k in range(4)]


def second_sources():
    begun = [(0, 0), (1, 0), (2, 0), (0, 1), (0, 3)]
    middle = [(3, 0), (0, 2), (1, 1), (1, 3), (2, 1), (2, 3)]
    last = [[(1, 2)], [(2, 2)], [(3, 2)], [(3, 1)], [(3, 3)]]
    return [(p, i, *at) for p, part in enumerate([begun, middle] + last) for i, at in enumerate(part)]


def assemble_body(own, at_ref, mine_ref, other_ref, wq_ref, wk_ref, wv_ref, table_ref, ub_ref):
    core, fast, slow = at_ref[0], at_ref[1], at_ref[2]
    table = jnp.zeros((8, D), F32)
    ub = jnp.zeros((8, D), F32)
    def add(i, sums):
        table, ub = sums
        dxy, dz = i // 4, i % 4
        chip = ((slow - dz) % 4) * 4 + (fast ^ dxy)
        a, b = mine_ref[i], other_ref[i]
        low, high = jnp.where(core == 0, a, b), jnp.where(core == 0, b, a)
        for m, ref in enumerate((wq_ref, wk_ref, wv_ref)):
            rows = slice(own * m, own * m + own)
            ref[chip] = jnp.concatenate([low[rows], high[rows]], axis=0)
        for side, got in ((0, low), (1, high)):
            tail = got[3 * own :].astype(F32)
            spot = chip * 2 + side
            lane = lax.broadcasted_iota(jnp.int32, (8, D), 1)
            row = lax.broadcasted_iota(jnp.int32, (8, D), 0)
            table = table + pltpu.roll(jnp.where(lane < own, tail, 0.0), spot * own, 1)
            wide = jnp.where((lane >= 128) & (lane < 128 + 4 * own) & (row == spot // 8), tail[0:1], 0.0)
            ub = ub + pltpu.roll(wide, (D - 128 + spot % 8 * 4 * own) % D, 1)
        return table, ub

    table, ub = lax.fori_loop(0, 16, add, (table, ub))
    table_ref[...] = table
    ub_ref[...] = ub[:4]


def assemble(at, mine, other, own, n):
    full = lambda a: pl.BlockSpec(a.shape, lambda i: (0,) * a.ndim)
    arrays = [mine, other]
    w = shaped((n // 2, 2 * own, D), BF16)
    outs = [w, w, w, shaped((8, D), F32), shaped((4, D), F32)]
    wq, wk, wv, table, ub = call(
        functools.partial(assemble_body, own), (1,),
        [pl.BlockSpec(memory_space=pltpu.SMEM)] + [full(a) for a in arrays],
        [full(a) for a in outs], outs, moved=7 * D * D * 2,
     vmem=28,)(at, *arrays)
    return wq.reshape(D, D), wk.reshape(D, D), wv.reshape(D, D), table, ub


def pack_small(vectors, wide):
    total = jnp.pad(wide[None, :], ((0, 7), (128, D - 128 - wide.shape[0])))
    for i, v in enumerate(vectors):
        total = total + jnp.pad(v[None, :], ((i, 7 - i), (0, D - v.shape[0])))
    return total


def ffn_parts_body(chunk, own, at_ref, mix_ref, x_ref, gy_ref, *rest):
    mine, other, (small_ref, ub_ref) = rest[:7], rest[7:14], rest[14:16]
    outs, (dg_ref, wo_ref, wu_ref, wd_ref) = rest[16:-4], rest[-4:]
    wide = 4 * own

    @pl.when(pl.program_id(0) == 0)
    def _():
        core, fast, slow = at_ref[0], at_ref[1], at_ref[2]
        for part, i, dxy, dz in second_sources():
            chip = ((slow - dz) % 4) * 4 + (fast ^ dxy)
            a, b = mine[part][i], other[part][i]
            low, high = jnp.where(core == 0, a, b), jnp.where(core == 0, b, a)
            at = pl.ds(pl.multiple_of(2 * wide * chip, 16), wide)
            wd_ref[at, :] = low[:wide]
            at = pl.ds(pl.multiple_of(2 * wide * chip + wide, 16), wide)
            wd_ref[at, :] = high[:wide]
            at = pl.ds(pl.multiple_of(2 * own * chip, 16), 2 * own)
            for j in range(5):
                rows = slice(wide + own * j, wide + own * j + own)
                both = jnp.concatenate([low[rows], high[rows]], axis=0)
                if j < 4:
                    wu_ref[at, D * j : D * j + D] = both
                else:
                    wo_ref[at, :] = both

    ffn_steps(chunk, mix_ref, x_ref, gy_ref, wo_ref, wu_ref, wd_ref, small_ref, ub_ref, *outs, dg_ref)


def ffn_steps(chunk, mix_ref, x_ref, gy_ref, wo_ref, wu_ref, wd_ref, small_ref, ub_ref,
              out_ref, hid_ref, gffn_ref, low_ref, gpre_ref, gattn_ref, g1_ref, gmix_ref, gsmall_ref, gub_ref, dg_ref):
    i = pl.program_id(0)
    bo, again, ashift, bd, fgain, fshift = (small_ref[j : j + 1, :] for j in range(2, 8))
    ff = wu_ref.shape[1]

    @pl.when(i == 0)
    def _():
        gsmall_ref[...] = jnp.zeros_like(gsmall_ref)
        gub_ref[...] = jnp.zeros_like(gub_ref)

    attn = dot(mix_ref[...], wo_ref[...]) + bo
    xhat1, rs1 = normalize(x_ref[...].astype(F32) + attn)
    first = xhat1 * again + ashift
    low = first.astype(BF16)
    low_ref[...] = low
    ffn = 0.0
    for j in range(ff // chunk):
        cols = slice(j * chunk, (j + 1) * chunk)
        pre = dot(low, wu_ref[:, cols]) + ub_ref[j : j + 1, :]
        hid, dg = gelu_parts(pre)
        hid = hid.astype(BF16)
        hid_ref[:, cols] = hid
        dg_ref[:, cols] = dg.astype(dg_ref.dtype)
        ffn = ffn + dot(hid, wd_ref[cols, :])
    xhat2, rs2 = normalize(first + ffn + bd)
    out_ref[...] = (xhat2 * fgain + fshift).astype(BF16)
    gy = gy_ref[...].astype(F32)
    g2 = norm_back(gy, xhat2, rs2, fgain)
    gffn = g2.astype(BF16)
    gffn_ref[...] = gffn
    gsmall_ref[5:6, :] += colsum(gffn.astype(F32))
    gsmall_ref[6:7, :] += colsum(gy * xhat2)
    gsmall_ref[7:8, :] += colsum(gy)
    gfirst = g2
    for j in range(ff // chunk):
        cols = slice(j * chunk, (j + 1) * chunk)
        gh = dot_rt(gffn, wd_ref[cols, :])
        gpre = (gh * dg_ref[:, cols].astype(F32)).astype(BF16)
        gpre_ref[:, cols] = gpre
        gub_ref[j : j + 1, :] += colsum(gpre.astype(F32))
        gfirst = gfirst + dot_rt(gpre, wu_ref[:, cols])
    g1 = norm_back(gfirst, xhat1, rs1, again)
    gattn = g1.astype(BF16)
    g1_ref[...] = g1
    gattn_ref[...] = gattn
    gsmall_ref[2:3, :] += colsum(gattn.astype(F32))
    gsmall_ref[3:4, :] += colsum(gfirst * xhat1)
    gsmall_ref[4:5, :] += colsum(gfirst)
    gmix_ref[...] = dot_rt(gattn, wo_ref[...]).astype(BF16)


def ffn_full_body(chunk, *refs):
    ffn_steps(chunk, *refs)


def ffn_both(mixed, x, gy, weights, small, ub, at=None, own=0, tile_rows=280, chunk=D):
    rows = x.shape[0]
    ff = ub.size
    tile = pl.BlockSpec((tile_rows, D), lambda c: (c, 0))
    wide = pl.BlockSpec((tile_rows, ff), lambda c: (c, 0))
    fixed = lambda a: pl.BlockSpec(a.shape, lambda c: (0,) * a.ndim, pipeline_mode=pl.Buffered(1))
    act = shaped((rows, D), BF16)
    big = shaped((rows, ff), BF16)
    scratch = [pltpu.VMEM((tile_rows, ff), F32)]
    body, place_of, specs = functools.partial(ffn_full_body, chunk), [], []
    if at is not None:
        body, place_of, specs = functools.partial(ffn_parts_body, chunk, own), [at], [pl.BlockSpec(memory_space=pltpu.SMEM)]
        scratch += [pltpu.VMEM((D, D), BF16), pltpu.VMEM((D, ff), BF16), pltpu.VMEM((ff, D), BF16)]
    return call(
        body, (rows // tile_rows,),
        specs + [tile, tile, tile] + [fixed(w) for w in weights] + [fixed(small), fixed(ub)],
        [tile, wide, tile, tile, wide, tile, tile, tile, pl.BlockSpec((8, D), lambda c: (0, 0)), pl.BlockSpec((ff // D, D), lambda c: (0, 0))],
        [act, big, act, act, big, act, shaped((rows, D), F32), act, shaped((8, D), F32), shaped((ff // D, D), F32)],
        scratch=scratch, vmem=46,
        flops=2 * rows * D * (2 * D + 4 * ff), moved=rows * (D * 20 + ff * 4) + D * (D + 2 * ff) * 2,
    )(*place_of, mixed, x, gy, *weights, small, ub)


def row_block(at_ref, far, own, dxy, dz):
    chip = ((at_ref[2] + dz) % far) * 4 + (at_ref[1] ^ dxy)
    return tuple(2 * chip + side for side in (at_ref[0], 1 - at_ref[0]))


def acc_rows(ref, m, d, own):
    at = pl.ds(pl.multiple_of(own * d, 8), own)
    return ref[at, :] if m is None else ref[m, at, :]


def keep_send(*shape):
    out = shaped((4,) + shape, BF16)
    spec = pl.BlockSpec(out.shape, lambda j: (0,) * len(out.shape))
    return [spec, spec], [out, out]


def wgrad_down_body(far, own, at_ref, hid_ref, gffn_ref, keep_ref, send_ref, acc_ref):
    acc_ref[...] = dot_lt(hid_ref[...], gffn_ref[...])
    for dxy in range(4):
        chip = at_ref[1] ^ dxy
        for out, side in zip((keep_ref, send_ref), (at_ref[0], 1 - at_ref[0])):
            out[dxy, 0] = acc_rows(acc_ref, None, 2 * chip + side, own).astype(BF16)


def wgrad_down(at, hidden, gffn, n):
    rows, ff = hidden.shape
    far = n // 8
    own = ff // n
    out = shaped((4, far, own, D), BF16)
    spec = pl.BlockSpec((4, 1, own, D), lambda j, at_ref: (0, (j + far - at_ref[2]) % far, 0, 0))
    return call(
        functools.partial(wgrad_down_body, far, own), (far,),
        [pl.BlockSpec((rows, ff // far), lambda j, at_ref: (0, j)), pl.BlockSpec((rows, D), lambda j, at_ref: (0, 0))],
        [spec, spec], [out, out], scratch=[pltpu.VMEM((ff // far, D), F32)], prefetch=1,
     vmem=60,)(at, hidden, gffn)


def wgrad_up_body(far, own, at_ref, low_ref, gpre_ref, mix_ref, gattn_ref, keep_ref, send_ref, acc_ref):
    j = pl.program_id(0)

    @pl.when(j < 4)
    def _():
        acc_ref[...] = dot_lt(low_ref[...], gpre_ref[...])

    @pl.when(j == 4)
    def _():
        acc_ref[...] = dot_lt(mix_ref[...], gattn_ref[...])

    def along(dz, _):
        for dxy in range(4):
            for out, d in zip((keep_ref, send_ref), row_block(at_ref, far, own, dxy, dz)):
                out[dxy, dz, 0] = acc_rows(acc_ref, None, d, own).astype(BF16)
        return 0

    lax.fori_loop(0, far, along, 0)


def wgrad_up(at, low, gpre, mixed, gattn, own, n):
    rows = low.shape[0]
    far = n // 8
    act = pl.BlockSpec((rows, D), lambda j: (0, 0))
    out = shaped((4, far, 5, own, D), BF16)
    spec = pl.BlockSpec((4, far, 1, own, D), lambda j: (0, 0, j, 0, 0))
    got = call(
        functools.partial(wgrad_up_body, far, own), (5,),
        [pl.BlockSpec(memory_space=pltpu.SMEM), act, pl.BlockSpec((rows, D), lambda j: (0, jnp.minimum(j, 3))), act, act],
        [spec, spec], [out, out], scratch=[pltpu.VMEM((D, D), F32)],
     vmem=32,)(at, low, gpre, mixed, gattn)
    return [g.reshape(4, far, 5 * own, D) for g in got]


def wgrad_in_body(far, own, at_ref, x_ref, grad_ref, small_ref, ub_ref, keep_ref, send_ref, acc_ref):
    j = pl.program_id(0)
    acc_ref[j] = dot_lt(x_ref[...], grad_ref[...])

    @pl.when(j == 2)
    def _():
        lane = lax.broadcasted_iota(jnp.int32, (8, D), 1)
        row = lax.broadcasted_iota(jnp.int32, (8, D), 0)
        wide = ub_ref.size // (8 * far)
        per = D // wide
        def along(dz, _):
            for dxy in range(4):
                for out, d in zip((keep_ref, send_ref), row_block(at_ref, far, own, dxy, dz)):
                    tail = pltpu.roll(small_ref[...], (D - own * d) % D, 1)
                    ub = pltpu.roll(ub_ref[pl.ds(d // per, 1), :], (D + 128 - wide * (d % per)) % D, 1)
                    tail = jnp.where(lane < own, tail, 0.0)
                    tail = jnp.where((row == 0) & (lane >= 128) & (lane < 128 + wide), ub, tail)
                    parts = [acc_rows(acc_ref, m, d, own) for m in range(3)] + [tail]
                    out[dxy, dz] = jnp.concatenate(parts, axis=0).astype(BF16)
            return 0

        lax.fori_loop(0, far, along, 0)


def wgrad_in(at, x, grads, small, ub, own, n):
    rows = x.shape[0]
    far = n // 8
    full = lambda a: pl.BlockSpec(a.shape, lambda i: (0,) * a.ndim)
    specs, outs = keep_send(far, 3 * own + 8, D)
    return call(
        functools.partial(wgrad_in_body, far, own), (3,),
        [pl.BlockSpec(memory_space=pltpu.SMEM), full(x), pl.BlockSpec((rows, D), lambda j: (0, j)), full(small), full(ub)],
        specs, outs, scratch=[pltpu.VMEM((3, D, D), F32)],
     vmem=36,)(at, x, grads, small, ub)


def pair_sum(keep, other, i):
    return keep[i].astype(F32) + other[i].astype(F32)


def near_parts(keep, other):
    return tuple(pair_sum(keep, other, i).astype(BF16) for i in (1, 2, 3))


def near_hops(parts, n):
    return tuple(hop(p, swap(n, 2 * i)) for i, p in enumerate(parts, 1))


def line_body(keep_ref, other_ref, x_ref, y_ref, d_ref, base_ref, *sent):
    total = keep_ref[...].astype(F32) + other_ref[...].astype(F32)
    for ref in (x_ref, y_ref, d_ref):
        total = total + ref[...].astype(F32)
    base_ref[...] = total[0, 0]
    for k, ref in enumerate(sent, 1):
        ref[...] = total[0, k].astype(BF16)


def line_sum(keep, other, near):
    far, rows = keep.shape[1:3]
    block = pl.BlockSpec((1, far, rows, D), lambda i: (0, 0, 0, 0))
    part = pl.BlockSpec((rows, D), lambda i: (0, 0))
    base, *sent = call(
        line_body, (1,), [block] * 5, [part] * far,
        [shaped((rows, D), F32)] + [shaped((rows, D), BF16)] * (far - 1),
     vmem=16,)(keep, other, *(p[None] for p in near))
    return base, sent


def pass_body(in_ref, out_ref):
    out_ref[...] = in_ref[...]


def passed(value):
    full = pl.BlockSpec(value.shape, lambda i: (0, 0))
    return call(pass_body, (1,), [full], full, shaped(value.shape, value.dtype), weight=WAIT, vmem=8)(value)


def far_hops(sent, n, which):
    return {k: hop(sent[k - 1], shift(n, k)) for k in which}


def last_sum(base, far):
    return base + sum(p.astype(F32) for p in far.values())


def input_grad_body(g1_ref, gq_ref, gk_ref, gv_ref, wq_ref, wk_ref, wv_ref, *rest):
    total = g1_ref[...] + dot_rt(gq_ref[...], wq_ref[...])
    total = total + dot_rt(gk_ref[...], wk_ref[...]) + dot_rt(gv_ref[...], wv_ref[...])
    rest[-1][...] = total.astype(BF16)


def input_grad(g1, grads, wq, wk, wv, start=0, stop=4, before=(), tiles=4):
    rows = g1.shape[0]
    tile = pl.BlockSpec((rows // tiles, D), lambda c: (c + start, 0))
    full = pl.BlockSpec((D, D), lambda c: (0, 0))
    return call(
        input_grad_body, (stop - start,),
        [tile] + [pl.BlockSpec((rows // tiles, D), lambda c, m=m: (c + start, m)) for m in range(3)] + [full, full, full] + [pl.BlockSpec(memory_space=pl.ANY)] * len(before),
        tile, shaped((rows, D), BF16), aliases={7: 0} if before else {},
        flops=6 * rows * D * D, moved=rows * D * 12 + 6 * D * D,
     vmem=24,)(g1, grads, grads, grads, wq, wk, wv, *before)


def residue_mask(cotangent, span_start, span_end):
    chains = span_start.shape[0]
    rows = cotangent.shape[0]
    positions = jnp.arange(rows // chains)
    inside = jnp.any(
        (positions[None, None, :] >= span_start[:, :, None]) & (positions[None, None, :] < span_end[:, :, None]),
        axis=1,
    )
    return jnp.where(inside.reshape(rows, 1), cotangent, jnp.zeros_like(cotangent))


def chunked(weight):
    own = weight.shape[0]
    return weight.reshape(own, -1, D).swapaxes(0, 1).reshape(-1, D)


def fast_shards(
    n, tokens, cotangent, lengths, span_start, span_end,
    query_weight, query_bias, key_weight, value_weight, value_bias, out_weight, out_bias,
    attn_gain, attn_shift, up_weight, up_bias, down_weight, down_bias, ffn_gain, ffn_shift,
):
    own = query_weight.shape[0]
    wide = up_bias.shape[0]
    vectors = (query_bias, value_bias, out_bias, attn_gain, attn_shift, down_bias, ffn_gain, ffn_shift)
    at = jnp.stack(place()).astype(jnp.int32)
    block = jnp.concatenate([query_weight, key_weight, value_weight, pack_small(vectors, up_bias)], axis=0)
    second = jnp.concatenate([down_weight, chunked(up_weight), out_weight], axis=0)
    chains = lengths.shape[0]
    ahead = chains * 3 // 7

    def attend(w, start, stop, before=()):
        return w, attn_fwd(tokens, *w[:4], lengths, start, stop, before)

    gy, ((wq, wk, wv, table, ub), (q, k, v, mixed, lse)), mine, other = gather_all(
        block, second, n,
        (lambda given: residue_mask(*given), (cotangent, span_start, span_end)),
        (
            lambda mine, other: assemble(at, mine, other, own, n),
            lambda w: attend(w, 0, ahead),
            lambda held: attend(held[0], ahead, chains, held[1]),
        ),
    )
    layer_out, hidden, gffn, low, gpre, gattn, g1, gmixed, gtable, gub = ffn_both(
        mixed, tokens, gy, mine + other, table, ub, at, own
    )
    cuts = (0, 1, 4, chains)
    keep_d, send_d = wgrad_down(at, hidden, gffn, n)
    gmixed, keep_d, send_d = tie(gmixed, keep_d, send_d)
    other_d = hop(send_d, swap(n, 1))
    begun = attn_bwd(q, k, v, gmixed, lse, lengths, cuts[0], cuts[1], weight=WAIT)
    begun, other_d = tie(begun, other_d)
    low, begun, parts_d = tie(low, begun, near_parts(keep_d, other_d))
    near_d = near_hops(parts_d, n)
    keep_u, send_u = wgrad_up(at, low, gpre, mixed, gattn, own, n)
    begun, keep_u, send_u = tie(begun, keep_u, send_u)
    other_u = hop(send_u, swap(n, 1))
    begun = attn_bwd(q, k, v, gmixed, lse, lengths, cuts[1], cuts[2], begun)
    begun, near_d = tie(begun, near_d)
    begun = [begun[0], passed(begun[1]), begun[2]]
    begun, other_u = tie(begun, other_u)
    begun, parts_u = tie(begun, near_parts(keep_u, other_u))
    near_u = near_hops(parts_u, n)
    base_d, sent_d = line_sum(keep_d, other_d, near_d)
    begun, base_d, sent_d = tie(begun, base_d, sent_d)
    far_d = far_hops(sent_d, n, (1, 3))
    grads, gqb, gvb = attn_bwd(q, k, v, gmixed, lse, lengths, cuts[2], cuts[3], begun)
    grads, far_d, sent_d = tie(grads, far_d, sent_d)
    far_d.update(far_hops(sent_d, n, (2,)))
    gtable = jnp.concatenate([gqb, gvb, gtable[2:]], axis=0)
    keep_i, send_i = wgrad_in(at, tokens, grads, gtable, gub, own, n)
    g1, keep_i, send_i = tie(g1, keep_i, send_i)
    other_i = hop(send_i, swap(n, 1))
    in_grad = input_grad(g1, grads, wq, wk, wv, 0, 2)
    in_grad, near_u, far_d, base_d = tie(in_grad, near_u, far_d, base_d)
    base_d = passed(base_d)
    base_d, other_i = tie(base_d, other_i)
    in_grad, parts_i, base_d = tie(in_grad, near_parts(keep_i, other_i), base_d)
    near_i = near_hops(parts_i, n)
    base_u, sent_u = line_sum(keep_u, other_u, near_u)
    in_grad, base_u, sent_u = tie(in_grad, base_u, sent_u)
    far_u = far_hops(sent_u, n, (1, 2))
    in_grad = input_grad(g1, grads, wq, wk, wv, 2, 4, (in_grad,))
    in_grad, near_i, far_u = tie(in_grad, near_i, far_u)
    base_i, sent_i = line_sum(keep_i, other_i, near_i)
    far_i = far_hops(sent_i, n, (1, 2, 3))
    far_u.update(far_hops(sent_u, n, (3,)))
    down_own, up_own, in_own = last_sum(base_d, far_d), last_sum(base_u, far_u), last_sum(base_i, far_i)

    gq_w, gk_w, gv_w = (in_own[own * i : own * (i + 1)] for i in range(3))
    gqb, gvb, gob, gag, gas, gdb, gfg, gfs = (in_own[3 * own + i, :own] for i in range(8))
    gub = in_own[3 * own, 128 : 128 + wide]
    gup = jnp.concatenate([up_own[own * i : own * (i + 1)] for i in range(wide // own)], axis=1)
    go_w = up_own[wide : wide + own]
    return (
        layer_out, in_grad, gq_w, gqb, gk_w, gv_w, gvb, go_w, gob, gag, gas, gup, gub, down_own, gdb, gfg, gfs,
    )


def plain_shards(
    tokens, cotangent, lengths, span_start, span_end,
    query_weight, query_bias, key_weight, value_weight, value_bias, out_weight, out_bias,
    attn_gain, attn_shift, up_weight, up_bias, down_weight, down_bias, ffn_gain, ffn_shift,
):
    own = query_weight.shape[0]
    parts = D // own
    ff = up_weight.shape[1]
    wide = own * ff // D
    vectors = (query_bias, value_bias, out_bias, attn_gain, attn_shift, down_bias, ffn_gain, ffn_shift, up_bias)
    packed = jnp.concatenate(vectors)
    packed = jnp.pad(packed, (0, D - packed.shape[0])).reshape(1, D)
    sent = jnp.concatenate(
        [query_weight, key_weight, value_weight, out_weight, chunked(up_weight), down_weight, packed], axis=0
    )
    held = lax.all_gather(sent, "fsdp", axis=0, tiled=False)
    wq, wk, wv, wo = (held[:, own * i : own * (i + 1)].reshape(D, D) for i in range(4))
    wu = jnp.concatenate(
        [held[:, own * (4 + i) : own * (5 + i)].reshape(D, D) for i in range(ff // D)], axis=1
    )
    wd = held[:, 4 * own + wide : 4 * own + 2 * wide].reshape(ff, D)
    small = held[:, -1].astype(F32)
    table = jnp.concatenate([small[:, own * i : own * (i + 1)].reshape(1, D) for i in range(8)], axis=0)
    ub = small[:, 8 * own : 8 * own + wide].reshape(ff // D, D)
    gy = residue_mask(cotangent, span_start, span_end)

    q, k, v, mixed, lse = attn_fwd(tokens, wq, wk, wv, table, lengths)
    layer_out, hidden, gffn, low, gpre, gattn, g1, gmixed, gtable, gub = ffn_both(
        mixed, tokens, gy, (wo, wu, wd), table, ub
    )
    down_grad = wgrad(hidden, gffn)
    up_grad = wgrad(low, gpre)
    ffn_parts = jnp.concatenate([up_grad.reshape(parts, wide, D), down_grad.reshape(parts, wide, D)], axis=1)
    ffn_own = lax.psum_scatter(ffn_parts, "fsdp", scatter_dimension=0, tiled=False).astype(F32)
    out_grad = wgrad(mixed, gattn)
    grads, gqb, gvb = attn_bwd(q, k, v, gmixed, lse, lengths)
    query_grad, key_grad, value_grad = (wgrad(tokens, grads)[:, D * i : D * (i + 1)] for i in range(3))
    vec = [gqb, gvb] + [gtable[i : i + 1] for i in range(2, 8)]
    vec = jnp.concatenate([p.reshape(parts, own) for p in vec] + [gub.reshape(parts, wide)], axis=1)
    vec = jnp.pad(vec.astype(BF16), ((0, 0), (0, D - vec.shape[1]))).reshape(parts, 1, D)
    attn_parts = jnp.concatenate(
        [g.reshape(parts, own, D) for g in (query_grad, key_grad, value_grad, out_grad)] + [vec], axis=1
    )
    attn_own = lax.psum_scatter(attn_parts, "fsdp", scatter_dimension=0, tiled=False).astype(F32)
    in_grad = input_grad(g1, grads, wq, wk, wv)

    gq_w, gk_w, gv_w, go_w = (attn_own[own * i : own * (i + 1)] for i in range(4))
    vec = attn_own[-1]
    gqb, gvb, gob, gag, gas, gdb, gfg, gfs = (vec[own * i : own * (i + 1)] for i in range(8))
    gub = vec[8 * own : 8 * own + wide]
    gup = ffn_own[:wide].reshape(own, ff)
    gdown = ffn_own[wide:]
    return (
        layer_out, in_grad, gq_w, gqb, gk_w, gv_w, gvb, go_w, gob, gag, gas, gup, gub, gdown, gdb, gfg, gfs,
    )


def solution(mesh):
    two, one = P("fsdp", None), P("fsdp")
    n = mesh.shape["fsdp"]
    whole_tiles = n % 8 == 0 and n // 8 == 4 and (D // n) % 8 == 0
    return jax.shard_map(
        functools.partial(fast_shards, n) if whole_tiles else plain_shards,
        mesh=mesh,
        in_specs=(two, two, one, two, two, two, one, two, two, one, two, one, one, one, two, one, two, one, one, one),
        out_specs=(two, two, two, one, two, two, one, two, one, one, one, two, one, two, one, one, one),
        check_vma=False,
    )
```

```python
import functools
import jax
import jax.numpy as jnp
from jax import lax
from jax.sharding import PartitionSpec as P
from jax.experimental import pallas as pl
from jax.experimental.pallas import tpu as pltpu

D = 768
HEADS = 12
HEAD = 64
epsilon = 1e-05
masked_score = -1000000000.0
F32 = jnp.float32
BF16 = jnp.bfloat16
WAIT = 1 << 40


def dot(left, right):
    return lax.dot_general(left, right, (((1,), (0,)), ((), ())), preferred_element_type=F32)


def dot_rt(left, right):
    return lax.dot_general(left, right, (((1,), (1,)), ((), ())), preferred_element_type=F32)


def dot_lt(left, right):
    return lax.dot_general(left, right, (((0,), (0,)), ((), ())), preferred_element_type=F32)


def call(body, grid, in_specs, out_specs, out_shape, scratch=(), flops=0, moved=0, vmem=60, aliases={}, weight=0, prefetch=0):
    return pl.pallas_call(
        body,
        grid_spec=pltpu.PrefetchScalarGridSpec(
            num_scalar_prefetch=prefetch, grid=grid, in_specs=in_specs, out_specs=out_specs, scratch_shapes=scratch
        ),
        out_shape=out_shape,
        input_output_aliases=aliases,
        compiler_params=pltpu.CompilerParams(vmem_limit_bytes=vmem * 1024 * 1024),
        cost_estimate=pl.CostEstimate(flops=weight, bytes_accessed=weight // 64, transcendentals=0),
    )


def shaped(shape, dtype):
    return jax.ShapeDtypeStruct(shape, dtype)


GROUP = 4


def by_head(values, scale=1.0):
    lane = lax.broadcasted_iota(jnp.int32, (1, GROUP * HEAD), 1) // HEAD
    return jnp.concatenate([values * jnp.where(lane == t, scale, 0.0).astype(BF16) for t in range(GROUP)], axis=0)


def own_columns(stacked):
    rows = stacked.shape[0] // GROUP
    lane = lax.broadcasted_iota(jnp.int32, (1, GROUP * HEAD), 1) // HEAD
    out = stacked[:rows]
    for t in range(1, GROUP):
        out = jnp.where(lane == t, stacked[rows * t : rows * (t + 1)], out)
    return out


def attn_fwd_body(start, len_ref, x_ref, wq_ref, wk_ref, wv_ref, table_ref, *rest):
    q_ref, k_ref, v_ref, mix_ref, lse_ref = rest[-5:]
    x = x_ref[...]
    length = x.shape[0]
    q_ref[...] = (dot(x, wq_ref[...]) + table_ref[0:1, :]).astype(BF16)
    k_ref[...] = dot(x, wk_ref[...]).astype(BF16)
    v_ref[...] = (dot(x, wv_ref[...]) + table_ref[1:2, :]).astype(BF16)
    valid = lax.broadcasted_iota(jnp.int32, (length, length), 0) < len_ref[pl.program_id(0) + start]
    for g in range(HEADS // GROUP):
        cols = slice(GROUP * HEAD * g, GROUP * HEAD * (g + 1))
        scores = dot_rt(by_head(k_ref[:, cols], 0.125), q_ref[:, cols])
        probs = []
        for t in range(GROUP):
            s = jnp.where(valid, scores[length * t : length * (t + 1)], masked_score)
            m = jnp.max(s, axis=0, keepdims=True)
            e = jnp.exp(s - m)
            total = jnp.sum(e, axis=0, keepdims=True)
            probs.append((e * (1.0 / total)).astype(BF16))
            lse_ref[0, GROUP * g + t : GROUP * g + t + 1, :] = m + jnp.log(total)
        mix_ref[:, cols] = dot_lt(jnp.concatenate(probs, axis=0), by_head(v_ref[:, cols])).astype(BF16)


def attn_fwd(x, wq, wk, wv, table, lengths, start=0, stop=None, before=()):
    rows = x.shape[0]
    n = lengths.shape[0]
    stop = n if stop is None else stop
    length = rows // n
    tile = pl.BlockSpec((length, D), lambda c: (c + start, 0))
    full = pl.BlockSpec((D, D), lambda c: (0, 0))
    eight = pl.BlockSpec((8, D), lambda c: (0, 0))
    act = shaped((rows, D), BF16)
    return call(
        functools.partial(attn_fwd_body, start), (stop - start,),
        [pl.BlockSpec(memory_space=pltpu.SMEM), tile, full, full, full, eight] + [pl.BlockSpec(memory_space=pl.ANY)] * len(before),
        [tile, tile, tile, tile, pl.BlockSpec((1, HEADS, length), lambda c: (c + start, 0, 0))],
        [act, act, act, act, shaped((n, HEADS, length), F32)],
        flops=2 * rows * D * D * 3 + 4 * rows * length * D * 4, moved=rows * D * 10 + 6 * D * D,
        aliases={6 + i: i for i in range(5)} if before else {},
     vmem=24,)(lengths, x, wq, wk, wv, table, *before)


def attn_bwd_body(start, len_ref, q_ref, k_ref, v_ref, gm_ref, lse_ref, *rest):
    grads_ref, gbq_ref, gbv_ref = rest[-3:]
    c = pl.program_id(0)
    length = q_ref.shape[0]
    valid = lax.broadcasted_iota(jnp.int32, (length, length), 0) < len_ref[c + start]

    @pl.when(c == 0)
    def _():
        gbq_ref[...] = rest[1][...] if start else jnp.zeros_like(gbq_ref)
        gbv_ref[...] = rest[2][...] if start else jnp.zeros_like(gbv_ref)

    for g in range(HEADS // GROUP):
        cols = slice(GROUP * HEAD * g, GROUP * HEAD * (g + 1))
        q, gm = q_ref[:, cols], gm_ref[:, cols]
        keys = by_head(k_ref[:, cols], 0.125)
        scores = dot_rt(keys, q)
        gprobs = dot_rt(by_head(v_ref[:, cols]), gm)
        probs, gscores = [], []
        for t in range(GROUP):
            rows = slice(length * t, length * (t + 1))
            h = GROUP * g + t
            pf = jnp.exp(jnp.where(valid, scores[rows], masked_score) - lse_ref[0, h : h + 1, :])
            gp = gprobs[rows]
            gs = pf * (gp - jnp.sum(pf * gp, axis=0, keepdims=True))
            probs.append(pf.astype(BF16))
            gscores.append(gs.astype(BF16))
        gscores = jnp.concatenate(gscores, axis=0)
        gv = own_columns(dot(jnp.concatenate(probs, axis=0), gm)).astype(BF16)
        gk = (own_columns(dot(gscores, q)) * 0.125).astype(BF16)
        gq = dot_lt(gscores, keys).astype(BF16)
        for m, value in enumerate((gq, gk, gv)):
            grads_ref[:, m * D + cols.start : m * D + cols.stop] = value
        gbq_ref[:, cols] += jnp.sum(gq.astype(F32), axis=0, keepdims=True)
        gbv_ref[:, cols] += jnp.sum(gv.astype(F32), axis=0, keepdims=True)


def attn_bwd(q, k, v, gm, lse, lengths, start=0, stop=None, before=(), weight=0):
    rows = q.shape[0]
    n = lengths.shape[0]
    stop = n if stop is None else stop
    length = rows // n
    tile = pl.BlockSpec((length, D), lambda c: (c + start, 0))
    one = pl.BlockSpec((1, D), lambda c: (0, 0))
    whole = pl.BlockSpec(memory_space=pl.ANY)
    return call(
        functools.partial(attn_bwd_body, start), (stop - start,),
        [pl.BlockSpec(memory_space=pltpu.SMEM), tile, tile, tile, tile, pl.BlockSpec((1, HEADS, length), lambda c: (c + start, 0, 0))]
        + ([whole, one, one] if before else []),
        [pl.BlockSpec((length, 3 * D), lambda c: (c + start, 0)), one, one],
        [shaped((rows, 3 * D), BF16), shaped((1, D), F32), shaped((1, D), F32)],
        flops=2 * (stop - start) * length * length * D * 5 * 4, moved=(stop - start) * length * D * 14,
        aliases={6: 0} if before else {}, weight=weight,
     vmem=20,)(lengths, q, k, v, gm, lse, *before)


def mean(v):
    return jnp.sum(v, axis=-1, keepdims=True) * (1.0 / D)


def normalize(values):
    center = values - mean(values)
    scale = lax.rsqrt(mean(center * center) + epsilon)
    return center * scale, scale


def norm_back(incoming, normed, scale, gain):
    weighted = incoming * gain
    return scale * (weighted - mean(weighted) - normed * mean(weighted * normed))


def colsum(v):
    return jnp.sum(v, axis=0, keepdims=True)


def gelu_parts(pre):
    cdf = 0.5 + 0.5 * lax.erf(pre * 0.7071067811865476)
    pdf = 0.3989422804014327 * jnp.exp(-0.5 * pre * pre)
    return pre * cdf, cdf + pre * pdf


def wgrad_body(l_ref, r_ref, o_ref):
    o_ref[...] = dot_lt(l_ref[...], r_ref[...]).astype(o_ref.dtype)


def wgrad(left, right, tile_m=768, dtype=BF16):
    rows, m = left.shape
    n = right.shape[1]
    tn = min(n, 768)
    return call(
        wgrad_body, (n // tn, m // tile_m),
        [pl.BlockSpec((rows, tile_m), lambda j, i: (0, i)), pl.BlockSpec((rows, tn), lambda j, i: (0, j))],
        pl.BlockSpec((tile_m, tn), lambda j, i: (i, j)),
        shaped((m, n), dtype),
        flops=2 * rows * m * n, moved=2 * (rows * (m + n) + m * n),
    )(left, right)

def tie(*values):
    return lax.optimization_barrier(values)


def place():
    idx = lax.axis_index("fsdp")
    return idx % 2, (idx // 2) % 4, idx // 8

def swap(n, bits):
    return [(i, i ^ bits) for i in range(n)]

def shift(n, k):
    return [(i, (i + 8 * k) % n) for i in range(n)]

def hop(value, pairs):
    return lax.ppermute(value, "fsdp", pairs)


def join_body(*refs):
    at = 0
    for ref in refs[:-1]:
        refs[-1][at : at + ref.shape[0]] = ref[...]
        at += ref.shape[0]


def join(*parts):
    parts = [p if p.ndim == 3 else p[None] for p in parts]
    full = lambda a: pl.BlockSpec(a.shape, lambda i: (0, 0, 0))
    out = shaped((sum(p.shape[0] for p in parts),) + parts[0].shape[1:], BF16)
    return call(join_body, (1,), [full(p) for p in parts], full(out), out, vmem=16)(*parts)


def gather_all(first, second, n, spare, steps):
    work, given = spare
    across = lambda part: hop(part, swap(n, 1))
    f1, f2, f3 = (hop(first, shift(n, k)) for k in (1, 2, 3))
    x0, y0, d0 = (hop(second, swap(n, b)) for b in (2, 4, 6))
    line = jnp.stack([first, f1, f2, f3])
    line, second = tie(line, second)
    near = [hop(line, swap(n, b)) for b in (2, 4, 6)]
    z1, z3 = (hop(second, shift(n, k)) for k in (1, 3))
    near, second, z1, z3, given, x0, y0, d0 = tie(near, second, z1, z3, given, x0, y0, d0)
    mine = jnp.concatenate([line, *near])
    other = across(mine)
    pair = jnp.stack([z1, z3])
    z2 = hop(second, shift(n, 2))
    x13, y13 = (hop(pair, swap(n, b)) for b in (2, 4))
    other, begun = tie(other, join(second, x0, y0, z1, z3))
    begun_other = across(begun)
    held = steps[1](steps[0](mine, other))
    held, d0, z2, x13, y13, begun_other, done = tie(held, d0, z2, x13, y13, begun_other, work(given))
    middle = jnp.concatenate([d0[None], z2[None], x13, y13])
    middle_other = across(middle)
    last = [hop(z2, swap(n, b)) for b in (2, 4, 6)] + [hop(d0, shift(n, k)) for k in (1, 3)]
    held, middle_other = tie(held, middle_other)
    held, last = tie(steps[2](held), last)
    last = [p[None] for p in last]
    return done, held, [begun, middle, *last], [begun_other, middle_other, *(across(p) for p in last)]


def first_sources():
    return [(d, k) for d in range(4) for k in range(4)]


def second_sources():
    begun = [(0, 0), (1, 0), (2, 0), (0, 1), (0, 3)]
    middle = [(3, 0), (0, 2), (1, 1), (1, 3), (2, 1), (2, 3)]
    last = [[(1, 2)], [(2, 2)], [(3, 2)], [(3, 1)], [(3, 3)]]
    return [(p, i, *at) for p, part in enumerate([begun, middle] + last) for i, at in enumerate(part)]


def assemble_body(own, at_ref, mine_ref, other_ref, wq_ref, wk_ref, wv_ref, table_ref, ub_ref):
    core, fast, slow = at_ref[0], at_ref[1], at_ref[2]
    table = jnp.zeros((8, D), F32)
    ub = jnp.zeros((8, D), F32)
    def add(i, sums):
        table, ub = sums
        dxy, dz = i // 4, i % 4
        chip = ((slow - dz) % 4) * 4 + (fast ^ dxy)
        a, b = mine_ref[i], other_ref[i]
        low, high = jnp.where(core == 0, a, b), jnp.where(core == 0, b, a)
        for m, ref in enumerate((wq_ref, wk_ref, wv_ref)):
            rows = slice(own * m, own * m + own)
            ref[chip] = jnp.concatenate([low[rows], high[rows]], axis=0)
        for side, got in ((0, low), (1, high)):
            tail = got[3 * own :].astype(F32)
            spot = chip * 2 + side
            lane = lax.broadcasted_iota(jnp.int32, (8, D), 1)
            row = lax.broadcasted_iota(jnp.int32, (8, D), 0)
            table = table + pltpu.roll(jnp.where(lane < own, tail, 0.0), spot * own, 1)
            wide = jnp.where((lane >= 128) & (lane < 128 + 4 * own) & (row == spot // 8), tail[0:1], 0.0)
            ub = ub + pltpu.roll(wide, (D - 128 + spot % 8 * 4 * own) % D, 1)
        return table, ub

    table, ub = lax.fori_loop(0, 16, add, (table, ub))
    table_ref[...] = table
    ub_ref[...] = ub[:4]


def assemble(at, mine, other, own, n):
    full = lambda a: pl.BlockSpec(a.shape, lambda i: (0,) * a.ndim)
    arrays = [mine, other]
    w = shaped((n // 2, 2 * own, D), BF16)
    outs = [w, w, w, shaped((8, D), F32), shaped((4, D), F32)]
    wq, wk, wv, table, ub = call(
        functools.partial(assemble_body, own), (1,),
        [pl.BlockSpec(memory_space=pltpu.SMEM)] + [full(a) for a in arrays],
        [full(a) for a in outs], outs, moved=7 * D * D * 2,
     vmem=28,)(at, *arrays)
    return wq.reshape(D, D), wk.reshape(D, D), wv.reshape(D, D), table, ub


def pack_small(vectors, wide):
    total = jnp.pad(wide[None, :], ((0, 7), (128, D - 128 - wide.shape[0])))
    for i, v in enumerate(vectors):
        total = total + jnp.pad(v[None, :], ((i, 7 - i), (0, D - v.shape[0])))
    return total


def ffn_parts_body(chunk, own, at_ref, mix_ref, x_ref, gy_ref, *rest):
    mine, other, (small_ref, ub_ref) = rest[:7], rest[7:14], rest[14:16]
    outs, (dg_ref, wo_ref, wu_ref, wd_ref) = rest[16:-4], rest[-4:]
    wide = 4 * own

    @pl.when(pl.program_id(0) == 0)
    def _():
        core, fast, slow = at_ref[0], at_ref[1], at_ref[2]
        for part, i, dxy, dz in second_sources():
            chip = ((slow - dz) % 4) * 4 + (fast ^ dxy)
            a, b = mine[part][i], other[part][i]
            low, high = jnp.where(core == 0, a, b), jnp.where(core == 0, b, a)
            at = pl.ds(pl.multiple_of(2 * wide * chip, 16), wide)
            wd_ref[at, :] = low[:wide]
            at = pl.ds(pl.multiple_of(2 * wide * chip + wide, 16), wide)
            wd_ref[at, :] = high[:wide]
            at = pl.ds(pl.multiple_of(2 * own * chip, 16), 2 * own)
            for j in range(5):
                rows = slice(wide + own * j, wide + own * j + own)
                both = jnp.concatenate([low[rows], high[rows]], axis=0)
                if j < 4:
                    wu_ref[at, D * j : D * j + D] = both
                else:
                    wo_ref[at, :] = both

    ffn_steps(chunk, mix_ref, x_ref, gy_ref, wo_ref, wu_ref, wd_ref, small_ref, ub_ref, *outs, dg_ref)


def ffn_steps(chunk, mix_ref, x_ref, gy_ref, wo_ref, wu_ref, wd_ref, small_ref, ub_ref,
              out_ref, hid_ref, gffn_ref, low_ref, gpre_ref, gattn_ref, g1_ref, gmix_ref, gsmall_ref, gub_ref, dg_ref):
    i = pl.program_id(0)
    bo, again, ashift, bd, fgain, fshift = (small_ref[j : j + 1, :] for j in range(2, 8))
    ff = wu_ref.shape[1]

    @pl.when(i == 0)
    def _():
        gsmall_ref[...] = jnp.zeros_like(gsmall_ref)
        gub_ref[...] = jnp.zeros_like(gub_ref)

    attn = dot(mix_ref[...], wo_ref[...]) + bo
    xhat1, rs1 = normalize(x_ref[...].astype(F32) + attn)
    first = xhat1 * again + ashift
    low = first.astype(BF16)
    low_ref[...] = low
    ffn = 0.0
    for j in range(ff // chunk):
        cols = slice(j * chunk, (j + 1) * chunk)
        pre = dot(low, wu_ref[:, cols]) + ub_ref[j : j + 1, :]
        hid, dg = gelu_parts(pre)
        hid = hid.astype(BF16)
        hid_ref[:, cols] = hid
        dg_ref[:, cols] = dg.astype(dg_ref.dtype)
        ffn = ffn + dot(hid, wd_ref[cols, :])
    xhat2, rs2 = normalize(first + ffn + bd)
    out_ref[...] = (xhat2 * fgain + fshift).astype(BF16)
    gy = gy_ref[...].astype(F32)
    g2 = norm_back(gy, xhat2, rs2, fgain)
    gffn = g2.astype(BF16)
    gffn_ref[...] = gffn
    gsmall_ref[5:6, :] += colsum(gffn.astype(F32))
    gsmall_ref[6:7, :] += colsum(gy * xhat2)
    gsmall_ref[7:8, :] += colsum(gy)
    gfirst = g2
    for j in range(ff // chunk):
        cols = slice(j * chunk, (j + 1) * chunk)
        gh = dot_rt(gffn, wd_ref[cols, :])
        gpre = (gh * dg_ref[:, cols].astype(F32)).astype(BF16)
        gpre_ref[:, cols] = gpre
        gub_ref[j : j + 1, :] += colsum(gpre.astype(F32))
        gfirst = gfirst + dot_rt(gpre, wu_ref[:, cols])
    g1 = norm_back(gfirst, xhat1, rs1, again)
    gattn = g1.astype(BF16)
    g1_ref[...] = g1
    gattn_ref[...] = gattn
    gsmall_ref[2:3, :] += colsum(gattn.astype(F32))
    gsmall_ref[3:4, :] += colsum(gfirst * xhat1)
    gsmall_ref[4:5, :] += colsum(gfirst)
    gmix_ref[...] = dot_rt(gattn, wo_ref[...]).astype(BF16)


def ffn_full_body(chunk, *refs):
    ffn_steps(chunk, *refs)


def ffn_both(mixed, x, gy, weights, small, ub, at=None, own=0, tile_rows=280, chunk=D):
    rows = x.shape[0]
    ff = ub.size
    tile = pl.BlockSpec((tile_rows, D), lambda c: (c, 0))
    wide = pl.BlockSpec((tile_rows, ff), lambda c: (c, 0))
    fixed = lambda a: pl.BlockSpec(a.shape, lambda c: (0,) * a.ndim, pipeline_mode=pl.Buffered(1))
    act = shaped((rows, D), BF16)
    big = shaped((rows, ff), BF16)
    scratch = [pltpu.VMEM((tile_rows, ff), F32)]
    body, place_of, specs = functools.partial(ffn_full_body, chunk), [], []
    if at is not None:
        body, place_of, specs = functools.partial(ffn_parts_body, chunk, own), [at], [pl.BlockSpec(memory_space=pltpu.SMEM)]
        scratch += [pltpu.VMEM((D, D), BF16), pltpu.VMEM((D, ff), BF16), pltpu.VMEM((ff, D), BF16)]
    return call(
        body, (rows // tile_rows,),
        specs + [tile, tile, tile] + [fixed(w) for w in weights] + [fixed(small), fixed(ub)],
        [tile, wide, tile, tile, wide, tile, tile, tile, pl.BlockSpec((8, D), lambda c: (0, 0)), pl.BlockSpec((ff // D, D), lambda c: (0, 0))],
        [act, big, act, act, big, act, shaped((rows, D), F32), act, shaped((8, D), F32), shaped((ff // D, D), F32)],
        scratch=scratch, vmem=48,
        flops=2 * rows * D * (2 * D + 4 * ff), moved=rows * (D * 20 + ff * 4) + D * (D + 2 * ff) * 2,
    )(*place_of, mixed, x, gy, *weights, small, ub)


def row_block(at_ref, far, own, dxy, dz):
    chip = ((at_ref[2] + dz) % far) * 4 + (at_ref[1] ^ dxy)
    return tuple(2 * chip + side for side in (at_ref[0], 1 - at_ref[0]))


def acc_rows(ref, m, d, own):
    at = pl.ds(pl.multiple_of(own * d, 8), own)
    return ref[at, :] if m is None else ref[m, at, :]


def keep_send(*shape):
    out = shaped((4,) + shape, BF16)
    spec = pl.BlockSpec(out.shape, lambda j: (0,) * len(out.shape))
    return [spec, spec], [out, out]


def wgrad_down_body(far, own, at_ref, hid_ref, gffn_ref, keep_ref, send_ref, acc_ref):
    acc_ref[...] = dot_lt(hid_ref[...], gffn_ref[...])
    for dxy in range(4):
        chip = at_ref[1] ^ dxy
        for out, side in zip((keep_ref, send_ref), (at_ref[0], 1 - at_ref[0])):
            out[dxy, 0] = acc_rows(acc_ref, None, 2 * chip + side, own).astype(BF16)


def wgrad_down(at, hidden, gffn, n):
    rows, ff = hidden.shape
    far = n // 8
    own = ff // n
    out = shaped((4, far, own, D), BF16)
    spec = pl.BlockSpec((4, 1, own, D), lambda j, at_ref: (0, (j + far - at_ref[2]) % far, 0, 0))
    return call(
        functools.partial(wgrad_down_body, far, own), (far,),
        [pl.BlockSpec((rows, ff // far), lambda j, at_ref: (0, j)), pl.BlockSpec((rows, D), lambda j, at_ref: (0, 0))],
        [spec, spec], [out, out], scratch=[pltpu.VMEM((ff // far, D), F32)], prefetch=1,
     vmem=60,)(at, hidden, gffn)


def wgrad_up_body(far, own, at_ref, low_ref, gpre_ref, mix_ref, gattn_ref, keep_ref, send_ref, acc_ref):
    j = pl.program_id(0)

    @pl.when(j < 4)
    def _():
        acc_ref[...] = dot_lt(low_ref[...], gpre_ref[...])

    @pl.when(j == 4)
    def _():
        acc_ref[...] = dot_lt(mix_ref[...], gattn_ref[...])

    def along(dz, _):
        for dxy in range(4):
            for out, d in zip((keep_ref, send_ref), row_block(at_ref, far, own, dxy, dz)):
                out[dxy, dz, 0] = acc_rows(acc_ref, None, d, own).astype(BF16)
        return 0

    lax.fori_loop(0, far, along, 0)


def wgrad_up(at, low, gpre, mixed, gattn, own, n):
    rows = low.shape[0]
    far = n // 8
    act = pl.BlockSpec((rows, D), lambda j: (0, 0))
    out = shaped((4, far, 5, own, D), BF16)
    spec = pl.BlockSpec((4, far, 1, own, D), lambda j: (0, 0, j, 0, 0))
    got = call(
        functools.partial(wgrad_up_body, far, own), (5,),
        [pl.BlockSpec(memory_space=pltpu.SMEM), act, pl.BlockSpec((rows, D), lambda j: (0, jnp.minimum(j, 3))), act, act],
        [spec, spec], [out, out], scratch=[pltpu.VMEM((D, D), F32)],
     vmem=32,)(at, low, gpre, mixed, gattn)
    return [g.reshape(4, far, 5 * own, D) for g in got]


def wgrad_in_body(far, own, at_ref, x_ref, grad_ref, small_ref, ub_ref, keep_ref, send_ref, acc_ref):
    j = pl.program_id(0)
    acc_ref[j] = dot_lt(x_ref[...], grad_ref[...])

    @pl.when(j == 2)
    def _():
        lane = lax.broadcasted_iota(jnp.int32, (8, D), 1)
        row = lax.broadcasted_iota(jnp.int32, (8, D), 0)
        wide = ub_ref.size // (8 * far)
        per = D // wide
        def along(dz, _):
            for dxy in range(4):
                for out, d in zip((keep_ref, send_ref), row_block(at_ref, far, own, dxy, dz)):
                    tail = pltpu.roll(small_ref[...], (D - own * d) % D, 1)
                    ub = pltpu.roll(ub_ref[pl.ds(d // per, 1), :], (D + 128 - wide * (d % per)) % D, 1)
                    tail = jnp.where(lane < own, tail, 0.0)
                    tail = jnp.where((row == 0) & (lane >= 128) & (lane < 128 + wide), ub, tail)
                    parts = [acc_rows(acc_ref, m, d, own) for m in range(3)] + [tail]
                    out[dxy, dz] = jnp.concatenate(parts, axis=0).astype(BF16)
            return 0

        lax.fori_loop(0, far, along, 0)


def wgrad_in(at, x, grads, small, ub, own, n):
    rows = x.shape[0]
    far = n // 8
    full = lambda a: pl.BlockSpec(a.shape, lambda i: (0,) * a.ndim)
    specs, outs = keep_send(far, 3 * own + 8, D)
    return call(
        functools.partial(wgrad_in_body, far, own), (3,),
        [pl.BlockSpec(memory_space=pltpu.SMEM), full(x), pl.BlockSpec((rows, D), lambda j: (0, j)), full(small), full(ub)],
        specs, outs, scratch=[pltpu.VMEM((3, D, D), F32)],
     vmem=28,)(at, x, grads, small, ub)


def pair_sum(keep, other, i):
    return keep[i].astype(F32) + other[i].astype(F32)


def near_parts(keep, other):
    return tuple(pair_sum(keep, other, i).astype(BF16) for i in (1, 2, 3))


def near_hops(parts, n):
    return tuple(hop(p, swap(n, 2 * i)) for i, p in enumerate(parts, 1))


def line_body(keep_ref, other_ref, x_ref, y_ref, d_ref, base_ref, *sent):
    total = keep_ref[...].astype(F32) + other_ref[...].astype(F32)
    for ref in (x_ref, y_ref, d_ref):
        total = total + ref[...].astype(F32)
    base_ref[...] = total[0, 0]
    for k, ref in enumerate(sent, 1):
        ref[...] = total[0, k].astype(BF16)


def line_sum(keep, other, near):
    far, rows = keep.shape[1:3]
    block = pl.BlockSpec((1, far, rows, D), lambda i: (0, 0, 0, 0))
    part = pl.BlockSpec((rows, D), lambda i: (0, 0))
    base, *sent = call(
        line_body, (1,), [block] * 5, [part] * far,
        [shaped((rows, D), F32)] + [shaped((rows, D), BF16)] * (far - 1),
     vmem=10,)(keep, other, *(p[None] for p in near))
    return base, sent


def pass_body(in_ref, out_ref):
    out_ref[...] = in_ref[...]


def passed(value):
    full = pl.BlockSpec(value.shape, lambda i: (0, 0))
    return call(pass_body, (1,), [full], full, shaped(value.shape, value.dtype), weight=WAIT, vmem=8)(value)


def far_hops(sent, n, which):
    return {k: hop(sent[k - 1], shift(n, k)) for k in which}


def last_sum(base, far):
    return base + sum(p.astype(F32) for p in far.values())


def input_grad_body(g1_ref, gq_ref, gk_ref, gv_ref, wq_ref, wk_ref, wv_ref, *rest):
    total = g1_ref[...] + dot_rt(gq_ref[...], wq_ref[...])
    total = total + dot_rt(gk_ref[...], wk_ref[...]) + dot_rt(gv_ref[...], wv_ref[...])
    rest[-1][...] = total.astype(BF16)


def input_grad(g1, grads, wq, wk, wv, start=0, stop=4, before=(), tiles=4):
    rows = g1.shape[0]
    tile = pl.BlockSpec((rows // tiles, D), lambda c: (c + start, 0))
    full = pl.BlockSpec((D, D), lambda c: (0, 0))
    return call(
        input_grad_body, (stop - start,),
        [tile] + [pl.BlockSpec((rows // tiles, D), lambda c, m=m: (c + start, m)) for m in range(3)] + [full, full, full] + [pl.BlockSpec(memory_space=pl.ANY)] * len(before),
        tile, shaped((rows, D), BF16), aliases={7: 0} if before else {},
        flops=6 * rows * D * D, moved=rows * D * 12 + 6 * D * D,
     vmem=24,)(g1, grads, grads, grads, wq, wk, wv, *before)


def residue_mask(cotangent, span_start, span_end):
    chains = span_start.shape[0]
    rows = cotangent.shape[0]
    positions = jnp.arange(rows // chains)
    inside = jnp.any(
        (positions[None, None, :] >= span_start[:, :, None]) & (positions[None, None, :] < span_end[:, :, None]),
        axis=1,
    )
    return jnp.where(inside.reshape(rows, 1), cotangent, jnp.zeros_like(cotangent))


def chunked(weight):
    own = weight.shape[0]
    return weight.reshape(own, -1, D).swapaxes(0, 1).reshape(-1, D)


def fast_shards(
    n, tokens, cotangent, lengths, span_start, span_end,
    query_weight, query_bias, key_weight, value_weight, value_bias, out_weight, out_bias,
    attn_gain, attn_shift, up_weight, up_bias, down_weight, down_bias, ffn_gain, ffn_shift,
):
    own = query_weight.shape[0]
    wide = up_bias.shape[0]
    vectors = (query_bias, value_bias, out_bias, attn_gain, attn_shift, down_bias, ffn_gain, ffn_shift)
    at = jnp.stack(place()).astype(jnp.int32)
    block = jnp.concatenate([query_weight, key_weight, value_weight, pack_small(vectors, up_bias)], axis=0)
    second = jnp.concatenate([down_weight, chunked(up_weight), out_weight], axis=0)
    chains = lengths.shape[0]
    ahead = chains * 3 // 7

    def attend(w, start, stop, before=()):
        return w, attn_fwd(tokens, *w[:4], lengths, start, stop, before)

    gy, ((wq, wk, wv, table, ub), (q, k, v, mixed, lse)), mine, other = gather_all(
        block, second, n,
        (lambda given: residue_mask(*given), (cotangent, span_start, span_end)),
        (
            lambda mine, other: assemble(at, mine, other, own, n),
            lambda w: attend(w, 0, ahead),
            lambda held: attend(held[0], ahead, chains, held[1]),
        ),
    )
    layer_out, hidden, gffn, low, gpre, gattn, g1, gmixed, gtable, gub = ffn_both(
        mixed, tokens, gy, mine + other, table, ub, at, own
    )
    cuts = (0, 1, 6, chains)
    keep_d, send_d = wgrad_down(at, hidden, gffn, n)
    gmixed, keep_d, send_d = tie(gmixed, keep_d, send_d)
    other_d = hop(send_d, swap(n, 1))
    begun = attn_bwd(q, k, v, gmixed, lse, lengths, cuts[0], cuts[1], weight=WAIT)
    begun, other_d = tie(begun, other_d)
    low, begun, parts_d = tie(low, begun, near_parts(keep_d, other_d))
    near_d = near_hops(parts_d, n)
    keep_u, send_u = wgrad_up(at, low, gpre, mixed, gattn, own, n)
    begun, keep_u, send_u = tie(begun, keep_u, send_u)
    other_u = hop(send_u, swap(n, 1))
    begun = attn_bwd(q, k, v, gmixed, lse, lengths, cuts[1], cuts[2], begun)
    begun, near_d = tie(begun, near_d)
    begun = [begun[0], passed(begun[1]), begun[2]]
    begun, other_u = tie(begun, other_u)
    begun, parts_u = tie(begun, near_parts(keep_u, other_u))
    near_u = near_hops(parts_u, n)
    base_d, sent_d = line_sum(keep_d, other_d, near_d)
    begun, base_d, sent_d = tie(begun, base_d, sent_d)
    far_d = far_hops(sent_d, n, (1, 3))
    grads, gqb, gvb = attn_bwd(q, k, v, gmixed, lse, lengths, cuts[2], cuts[3], begun)
    grads, far_d, sent_d = tie(grads, far_d, sent_d)
    far_d.update(far_hops(sent_d, n, (2,)))
    gtable = jnp.concatenate([gqb, gvb, gtable[2:]], axis=0)
    keep_i, send_i = wgrad_in(at, tokens, grads, gtable, gub, own, n)
    g1, keep_i, send_i = tie(g1, keep_i, send_i)
    other_i = hop(send_i, swap(n, 1))
    in_grad = input_grad(g1, grads, wq, wk, wv, 0, 2)
    in_grad, near_u, far_d, base_d = tie(in_grad, near_u, far_d, base_d)
    base_d = passed(base_d)
    base_d, other_i = tie(base_d, other_i)
    in_grad, parts_i, base_d = tie(in_grad, near_parts(keep_i, other_i), base_d)
    near_i = near_hops(parts_i, n)
    base_u, sent_u = line_sum(keep_u, other_u, near_u)
    in_grad, base_u, sent_u = tie(in_grad, base_u, sent_u)
    far_u = far_hops(sent_u, n, (1, 2))
    in_grad = input_grad(g1, grads, wq, wk, wv, 2, 4, (in_grad,))
    in_grad, near_i, far_u = tie(in_grad, near_i, far_u)
    base_i, sent_i = line_sum(keep_i, other_i, near_i)
    sent_i, far_u = tie(sent_i, far_u)
    far_i = far_hops(sent_i, n, (1, 2, 3))
    far_u.update(far_hops(sent_u, n, (3,)))
    down_own, up_own = last_sum(base_d, far_d), last_sum(base_u, far_u)
    piece = lambda *at: base_i[at] + sum(p[at].astype(F32) for p in far_i.values())

    gq_w, gk_w, gv_w = (piece(slice(own * i, own * (i + 1))) for i in range(3))
    gqb, gvb, gob, gag, gas, gdb, gfg, gfs = (piece(3 * own + i, slice(0, own)) for i in range(8))
    gub = piece(3 * own, slice(128, 128 + wide))
    gup = jnp.concatenate([up_own[own * i : own * (i + 1)] for i in range(wide // own)], axis=1)
    go_w = up_own[wide : wide + own]
    return (
        layer_out, in_grad, gq_w, gqb, gk_w, gv_w, gvb, go_w, gob, gag, gas, gup, gub, down_own, gdb, gfg, gfs,
    )


def plain_shards(
    tokens, cotangent, lengths, span_start, span_end,
    query_weight, query_bias, key_weight, value_weight, value_bias, out_weight, out_bias,
    attn_gain, attn_shift, up_weight, up_bias, down_weight, down_bias, ffn_gain, ffn_shift,
):
    own = query_weight.shape[0]
    parts = D // own
    ff = up_weight.shape[1]
    wide = own * ff // D
    vectors = (query_bias, value_bias, out_bias, attn_gain, attn_shift, down_bias, ffn_gain, ffn_shift, up_bias)
    packed = jnp.concatenate(vectors)
    packed = jnp.pad(packed, (0, D - packed.shape[0])).reshape(1, D)
    sent = jnp.concatenate(
        [query_weight, key_weight, value_weight, out_weight, chunked(up_weight), down_weight, packed], axis=0
    )
    held = lax.all_gather(sent, "fsdp", axis=0, tiled=False)
    wq, wk, wv, wo = (held[:, own * i : own * (i + 1)].reshape(D, D) for i in range(4))
    wu = jnp.concatenate(
        [held[:, own * (4 + i) : own * (5 + i)].reshape(D, D) for i in range(ff // D)], axis=1
    )
    wd = held[:, 4 * own + wide : 4 * own + 2 * wide].reshape(ff, D)
    small = held[:, -1].astype(F32)
    table = jnp.concatenate([small[:, own * i : own * (i + 1)].reshape(1, D) for i in range(8)], axis=0)
    ub = small[:, 8 * own : 8 * own + wide].reshape(ff // D, D)
    gy = residue_mask(cotangent, span_start, span_end)

    q, k, v, mixed, lse = attn_fwd(tokens, wq, wk, wv, table, lengths)
    layer_out, hidden, gffn, low, gpre, gattn, g1, gmixed, gtable, gub = ffn_both(
        mixed, tokens, gy, (wo, wu, wd), table, ub
    )
    down_grad = wgrad(hidden, gffn)
    up_grad = wgrad(low, gpre)
    ffn_parts = jnp.concatenate([up_grad.reshape(parts, wide, D), down_grad.reshape(parts, wide, D)], axis=1)
    ffn_own = lax.psum_scatter(ffn_parts, "fsdp", scatter_dimension=0, tiled=False).astype(F32)
    out_grad = wgrad(mixed, gattn)
    grads, gqb, gvb = attn_bwd(q, k, v, gmixed, lse, lengths)
    query_grad, key_grad, value_grad = (wgrad(tokens, grads)[:, D * i : D * (i + 1)] for i in range(3))
    vec = [gqb, gvb] + [gtable[i : i + 1] for i in range(2, 8)]
    vec = jnp.concatenate([p.reshape(parts, own) for p in vec] + [gub.reshape(parts, wide)], axis=1)
    vec = jnp.pad(vec.astype(BF16), ((0, 0), (0, D - vec.shape[1]))).reshape(parts, 1, D)
    attn_parts = jnp.concatenate(
        [g.reshape(parts, own, D) for g in (query_grad, key_grad, value_grad, out_grad)] + [vec], axis=1
    )
    attn_own = lax.psum_scatter(attn_parts, "fsdp", scatter_dimension=0, tiled=False).astype(F32)
    in_grad = input_grad(g1, grads, wq, wk, wv)

    gq_w, gk_w, gv_w, go_w = (attn_own[own * i : own * (i + 1)] for i in range(4))
    vec = attn_own[-1]
    gqb, gvb, gob, gag, gas, gdb, gfg, gfs = (vec[own * i : own * (i + 1)] for i in range(8))
    gub = vec[8 * own : 8 * own + wide]
    gup = ffn_own[:wide].reshape(own, ff)
    gdown = ffn_own[wide:]
    return (
        layer_out, in_grad, gq_w, gqb, gk_w, gv_w, gvb, go_w, gob, gag, gas, gup, gub, gdown, gdb, gfg, gfs,
    )


def solution(mesh):
    two, one = P("fsdp", None), P("fsdp")
    n = mesh.shape["fsdp"]
    whole_tiles = n % 8 == 0 and n // 8 == 4 and (D // n) % 8 == 0
    return jax.shard_map(
        functools.partial(fast_shards, n) if whole_tiles else plain_shards,
        mesh=mesh,
        in_specs=(two, two, one, two, two, two, one, two, two, one, two, one, one, one, two, one, two, one, one, one),
        out_specs=(two, two, two, one, two, two, one, two, one, one, one, two, one, two, one, one, one),
        check_vma=False,
    )
```
